32 devices in a mesh: groups: 2 (over y), lib: 4 (over x, core), qry: 4 (over z).
Axes of the slice: x: 2, y: 2, z: 4, core: 2. Of those that a mesh axis runs over, the one named last changes fastest.
Arguments:
- queries: bfloat16 [4096, 1024], P(('groups', 'lib', 'qry')), parts along dimension 0, may hold values from -24 to 24
- library_keys: bfloat16 [4096, 1024], P(('groups', 'lib', 'qry')), parts along dimension 0, may hold values from -6 to 6
- library_values: bfloat16 [4096, 512], P(('groups', 'lib', 'qry')), parts along dimension 0, may hold values from -6 to 6
- key_scale: bfloat16 [4096], P(('groups', 'lib', 'qry')), parts along dimension 0, may hold values from 0.29 to 3.1
- block_list: int32 [32, 4], P('groups'), parts along dimension 0, may hold values from 0 to 15, as said below
- block_count: int32 [32], P('groups'), parts along dimension 0, may hold values from 1 to 4, as said below
Outputs:
- retrieved: bfloat16 [4096, 512], P(('groups', 'lib', 'qry')), parts along dimension 0
The draws below stay inside these ranges and needn't reach their ends.
There are 2 independent parts, one for each index of `groups`. The reference program is written for one: setup_inputs(seed, part) draws one part's arguments, and reference() takes and returns one part's arrays. A program takes and returns all parts, laid end to end along the dimension named above; each array names one. Nothing has to cross between parts.
Inputs may be any that keep to these rules, and one draw needn't show every extreme that they name: Row p holds block_list[p, 0] + k modulo 16 at position k (a run of consecutive blocks, all distinct); only the first block_count[p] are active. `block_count`: at least one panel has exactly 4.
All inputs are finite; a program needn't handle non-finite values.
Results may differ from the reference program's by a relative error of at most 0.004.
Values may be sent and summed in bfloat16 or wider, within the bound.
No kernel may reach another device: no remote copies, remote signals or barrier semaphores. Data moves between devices by JAX's collectives and lax.ppermute only.
A program may use at most 64 MiB of HBM per device.

```python
import math
import jax
import jax.numpy as jnp
from jax import lax

E = 1024
DV = 512
TILE = 128
NQ = 2048
NL = 2048
NPANEL = 16
NBLOCK = 16
MAXB = 4


def mass_windows(key):
    key = jax.random.fold_in(key, 11)
    key_first, key_one, key_two, key_peak = jax.random.split(key, 4)
    first = jax.random.randint(key_first, (NPANEL,), 0, NBLOCK)
    counts = jnp.minimum(jax.random.randint(key_one, (NPANEL,), 1, MAXB + 1), jax.random.randint(key_two, (NPANEL,), 1, MAXB + 1))
    peak = jax.random.randint(key_peak, (), 0, NPANEL)
    counts = jnp.where(jnp.arange(NPANEL) == peak, MAXB, counts)
    return (first.astype(jnp.int32), counts.astype(jnp.int32))


def base_library(key):
    key = jax.random.fold_in(key, 12)
    key_rows, key_scale = jax.random.split(key, 2)
    library = jnp.clip(jax.random.normal(key_rows, (NL, E), jnp.float32), -6.0, 6.0)
    scales = jnp.exp(jax.random.uniform(key_scale, (NL,), jnp.float32, math.log(0.3), math.log(3.0)))
    return (library, scales)


def draw_library_keys(key, part):
    library, scales = base_library(key)
    return library.astype(jnp.bfloat16)


def draw_key_scale(key, part):
    library, scales = base_library(key)
    return scales.astype(jnp.bfloat16)


def draw_queries(key, part):
    key = jax.random.fold_in(key, 3)
    drawn = jnp.clip(jax.random.normal(key, (NQ, E), jnp.float32), -6.0, 6.0)
    return drawn.astype(jnp.bfloat16)


def draw_block_list(key, part):
    first, counts = mass_windows(key)
    offsets = jnp.arange(MAXB, dtype=jnp.int32)
    return ((first[:, None] + offsets[None, :]) % NBLOCK).astype(jnp.int32)


def draw_block_count(key, part):
    first, counts = mass_windows(key)
    return counts


def block_scale(stream_key, dims, cuts, least, high):
    factor_of = 1.0
    for axis_at, blocks in cuts:
        steps = jax.random.uniform(jax.random.fold_in(jax.random.fold_in(stream_key, 6), axis_at), (blocks,), jnp.float32, least / len(cuts), high / len(cuts))
        factor_of = factor_of * jnp.repeat(jnp.exp(steps), dims[axis_at] // blocks).reshape((-1,) + (1,) * (len(dims) - 1 - axis_at))
    return factor_of


def bell_draw(own_key, shape, width, most, cuts=(), kind=jnp.bfloat16):
    factor_of = block_scale(own_key, shape, cuts, -0.22, 0.18) if cuts else 1.0
    values = jax.random.normal(own_key, shape, jnp.float32) * width * factor_of
    return jnp.minimum(jnp.maximum(values, -most), most).astype(kind)


def setup_inputs(seed: int = 0, part: int = 0) -> dict:
    seeds = jax.random.split(jax.random.key(seed), 7)
    own_keys = jax.random.split(jax.random.fold_in(seeds[6], part), 7)
    queries = draw_queries(jax.random.fold_in(jax.random.fold_in(seeds[6], part), 71), part)
    library_keys = draw_library_keys(jax.random.fold_in(jax.random.fold_in(seeds[6], part), 71), part)
    library_values = bell_draw(own_keys[2], (NL, DV), 1.0, 6.0, ((0, 16),))
    key_scale = draw_key_scale(jax.random.fold_in(jax.random.fold_in(seeds[6], part), 71), part)
    block_list = draw_block_list(jax.random.fold_in(jax.random.fold_in(seeds[6], part), 71), part)
    block_count = draw_block_count(jax.random.fold_in(jax.random.fold_in(seeds[6], part), 71), part)
    return {"queries": queries, "library_keys": library_keys, "library_values": library_values, "key_scale": key_scale, "block_list": block_list, "block_count": block_count}


MASKED_SCORE = -1e+30

def reference(queries, library_keys, library_values, key_scale, block_list, block_count):
    inverse_root = 1.0 / math.sqrt(E)
    scaled = key_scale.astype(jnp.float32) * inverse_root
    key_blocks = library_keys.reshape(NBLOCK, TILE, E)
    value_blocks = library_values.reshape(NBLOCK, TILE, DV)
    scale_blocks = scaled.reshape(NBLOCK, TILE)

    def one_panel(inputs):
        panel_rows, window_list, window_count = inputs
        picked_keys = key_blocks[window_list].reshape(MAXB * TILE, E)
        picked_values = value_blocks[window_list].reshape(MAXB * TILE, DV)
        picked_scale = scale_blocks[window_list].reshape(MAXB * TILE)
        in_window = jnp.repeat(jnp.arange(MAXB, dtype=jnp.int32) < window_count, TILE)
        scores = lax.dot_general(panel_rows, picked_keys, (((1,), (1,)), ((), ())), preferred_element_type=jnp.float32)
        scores = scores * picked_scale[None, :]
        scores = jnp.where(in_window[None, :], scores, MASKED_SCORE)
        row_max = lax.optimization_barrier(jnp.max(scores, axis=1))
        weights = jnp.where(in_window[None, :], jnp.exp(scores - row_max[:, None]), 0.0)
        weight_sum = lax.optimization_barrier(jnp.sum(weights, axis=1))
        weight_high = weights.astype(jnp.bfloat16)
        weight_low = (weights - weight_high.astype(jnp.float32)).astype(jnp.bfloat16)
        mixed = jnp.dot(weight_high, picked_values, preferred_element_type=jnp.float32)
        mixed = mixed + jnp.dot(weight_low, picked_values, preferred_element_type=jnp.float32)
        return (mixed / weight_sum[:, None]).astype(jnp.bfloat16)
    result = lax.map(one_panel, (queries.reshape(NPANEL, TILE, E), block_list, block_count))
    return result.reshape(NQ, DV)
```

```python
import functools
import math

import jax
import jax.numpy as jnp
from jax import lax
from jax.experimental import pallas as pl
from jax.experimental.pallas import tpu as pltpu
from jax.sharding import PartitionSpec as P

TILE = 128
LANES = 128
MASKED_SCORE = -1e30
VMEM_LIMIT = 48 * 1024 * 1024


def swap(value, axis, mask):
    length = lax.axis_size(axis)
    return lax.ppermute(value, axis, [(i, i ^ mask) for i in range(length)])


def split_three(value):
    high = value.astype(jnp.bfloat16)
    rest = value - high.astype(jnp.float32)
    middle = rest.astype(jnp.bfloat16)
    low = (rest - middle.astype(jnp.float32)).astype(jnp.bfloat16)
    return high, middle, low


def attend(masks, panel_mask, lists_ref, counts_ref, query_ref, key_refs, value_refs, score_ref, total_ref, mass_ref):
    lib_index = lax.axis_index("lib")
    qry_index = lax.axis_index("qry")
    qry_count = lax.axis_size("qry")
    block_total = lax.axis_size("lib") * qry_count
    panel = lib_index * qry_count + lax.bitwise_xor(qry_index, panel_mask)
    first = lists_ref[panel, 0]
    count = counts_ref[panel]
    width = query_ref.shape[1]
    value_width = total_ref.shape[1]
    inverse_root = 1.0 / math.sqrt(width)

    def active(lib_mask, qry_mask):
        block = lax.bitwise_xor(lib_index, lib_mask) * qry_count + lax.bitwise_xor(qry_index, qry_mask)
        return lax.rem(block - first + block_total, block_total) < count

    flags = [active(*mask) for mask in masks]
    score_ref[...] = jnp.full(score_ref.shape, MASKED_SCORE, jnp.float32)
    total_ref[...] = jnp.zeros(total_ref.shape, jnp.float32)
    mass_ref[...] = jnp.zeros(mass_ref.shape, jnp.float32)
    for at, flag in enumerate(flags):

        @pl.when(flag)
        def _(at=at):
            scale = value_refs[at][0:16, value_width : value_width + TILE].astype(jnp.float32)[0:1] * inverse_root
            product = lax.dot_general(
                query_ref[...], key_refs[at][...], (((1,), (1,)), ((), ())), preferred_element_type=jnp.float32
            )
            score_ref[at] = product * scale

    largest = score_ref[0]
    for at in range(1, len(flags)):
        largest = jnp.maximum(largest, score_ref[at])
    row_max = jnp.max(largest, axis=1, keepdims=True)
    for at, flag in enumerate(flags):

        @pl.when(flag)
        def _(at=at):
            weights = jnp.exp(score_ref[at] - row_max)
            mass_ref[...] += weights
            weight_high = weights.astype(jnp.bfloat16)
            weight_low = (weights - weight_high.astype(jnp.float32)).astype(jnp.bfloat16)
            values = value_refs[at][:, 0:value_width]
            added = jnp.dot(weight_high, values, preferred_element_type=jnp.float32)
            added = added + jnp.dot(weight_low, values, preferred_element_type=jnp.float32)
            total_ref[...] += added

    return row_max


def visit_kernel(masks, panel_mask, *refs):
    count = len(masks)
    lists_ref, counts_ref, query_ref = refs[:3]
    key_refs = refs[3 : 3 + count]
    value_refs = refs[3 + count : 3 + 2 * count]
    packed_ref, score_ref, total_ref, mass_ref = refs[3 + 2 * count :]
    row_max = attend(
        masks, panel_mask, lists_ref, counts_ref, query_ref, key_refs, value_refs, score_ref, total_ref, mass_ref
    )
    row_sum = jnp.sum(mass_ref[...], axis=1, keepdims=True)
    value_width = total_ref.shape[1]
    divisor = jnp.where(row_sum > 0.0, row_sum, 1.0)
    packed_ref[:, 0:value_width] = (total_ref[...] / divisor).astype(jnp.bfloat16)
    lane = lax.broadcasted_iota(jnp.int32, (TILE, LANES), 1)
    packed = jnp.zeros((TILE, LANES), jnp.float32)
    for at, part in enumerate(split_three(row_max) + split_three(row_sum)):
        packed = jnp.where(lane == at, part.astype(jnp.float32), packed)
    packed_ref[:, value_width:] = packed.astype(jnp.bfloat16)


def home_kernel(masks, *refs):
    count = len(masks)
    lists_ref, counts_ref, query_ref = refs[:3]
    key_refs = refs[3 : 3 + count]
    value_refs = refs[3 + count : 3 + 2 * count]
    total_ref, stats_ref, score_ref, mass_ref = refs[3 + 2 * count :]
    row_max = attend(masks, 0, lists_ref, counts_ref, query_ref, key_refs, value_refs, score_ref, total_ref, mass_ref)
    row_sum = jnp.sum(mass_ref[...], axis=1, keepdims=True)
    stats_ref[0] = jnp.broadcast_to(row_max, (TILE, LANES))
    stats_ref[1] = jnp.broadcast_to(row_sum, (TILE, LANES))


def merge_kernel(total_ref, stats_ref, *refs):
    packed_refs, out_ref = refs[:-1], refs[-1]
    value_width = total_ref.shape[1]
    lane = lax.broadcasted_iota(jnp.int32, (TILE, LANES), 1)
    maxima = [stats_ref[0]]
    sums = [stats_ref[1]]
    for packed_ref in packed_refs:
        packed = packed_ref[:, value_width:].astype(jnp.float32)

        def lanes_sum(low, packed=packed):
            picked = jnp.where((lane >= low) & (lane < low + 3), packed, 0.0)
            return jnp.broadcast_to(jnp.sum(picked, axis=1, keepdims=True), (TILE, LANES))

        maxima.append(lanes_sum(0))
        sums.append(lanes_sum(3))
    top = functools.reduce(jnp.maximum, maxima)
    factors = [jnp.exp(row_max - top) for row_max in maxima]
    masses = [factor * row_sum for factor, row_sum in zip(factors, sums)]
    inverse = 1.0 / functools.reduce(jnp.add, masses)
    scales = [factors[0] * inverse] + [mass * inverse for mass in masses[1:]]
    for at in range(0, value_width, LANES):
        merged = total_ref[:, at : at + LANES] * scales[0]
        for packed_ref, scale in zip(packed_refs, scales[1:]):
            merged = merged + packed_ref[:, at : at + LANES].astype(jnp.float32) * scale
        out_ref[:, at : at + LANES] = merged.astype(jnp.bfloat16)


def params():
    return pltpu.CompilerParams(vmem_limit_bytes=VMEM_LIMIT)


def pack_kernel(values_ref, scale_ref, packed_ref):
    value_width = values_ref.shape[1]
    packed_ref[:, 0:value_width] = values_ref[...]
    row = scale_ref[...].astype(jnp.float32)
    packed_ref[:, value_width:] = jnp.broadcast_to(row, (TILE, TILE)).astype(jnp.bfloat16)


def body(queries, library_keys, library_values, key_scale, block_list, block_count):
    qry_count = lax.axis_size("qry")
    lib_count = lax.axis_size("lib")
    value_width = library_values.shape[1]
    smem = pl.BlockSpec(memory_space=pltpu.SMEM)
    vmem = pl.BlockSpec(memory_space=pltpu.VMEM)

    values_packed = pl.pallas_call(
        pack_kernel,
        out_shape=jax.ShapeDtypeStruct((TILE, value_width + TILE), jnp.bfloat16),
        in_specs=[vmem, vmem],
        out_specs=vmem,
        compiler_params=params(),
    )(library_values, key_scale.reshape(1, TILE))

    steps = [("qry", 1)]
    mask = lib_count // 2
    while mask:
        steps.append(("lib", mask))
        mask //= 2
    pieces = [((0, 0), library_keys, values_packed)]
    for axis, mask in steps:
        arrived = []
        for (lib_mask, qry_mask), keys, values in pieces:
            place = (lib_mask, mask) if axis == "qry" else (lib_mask | mask, qry_mask)
            arrived.append((place, swap(keys, axis, mask), swap(values, axis, mask)))
        pieces = pieces + arrived
    masks = [piece[0] for piece in pieces]
    keys = [piece[1] for piece in pieces]
    values = [piece[2] for piece in pieces]
    count = len(pieces)

    cost = pl.CostEstimate(flops=2 * TILE * 4 * TILE * (1024 + 1024), bytes_accessed=count * 400 * 1024, transcendentals=0)
    scratch = [
        pltpu.VMEM((count, TILE, TILE), jnp.float32),
        pltpu.VMEM((TILE, value_width), jnp.float32),
        pltpu.VMEM((TILE, TILE), jnp.float32),
    ]
    returned = []
    visit_masks = [2 * at + 1 for at in range(1, qry_count // 2)]
    for visit_mask in visit_masks:
        visitor = swap(queries, "qry", visit_mask)
        packed = pl.pallas_call(
            functools.partial(visit_kernel, masks, visit_mask),
            out_shape=jax.ShapeDtypeStruct((TILE, value_width + LANES), jnp.bfloat16),
            in_specs=[smem, smem] + [vmem] * (1 + 2 * count),
            out_specs=vmem,
            scratch_shapes=scratch,
            compiler_params=params(),
            cost_estimate=cost,
        )(block_list, block_count, visitor, *keys, *values)
        returned.append(swap(packed, "qry", visit_mask))

    total, stats = pl.pallas_call(
        functools.partial(home_kernel, masks),
        out_shape=(
            jax.ShapeDtypeStruct((TILE, value_width), jnp.float32),
            jax.ShapeDtypeStruct((2, TILE, LANES), jnp.float32),
        ),
        in_specs=[smem, smem] + [vmem] * (1 + 2 * count),
        out_specs=(vmem, vmem),
        scratch_shapes=[scratch[0], scratch[2]],
        compiler_params=params(),
        cost_estimate=cost,
    )(block_list, block_count, queries, *keys, *values)

    return pl.pallas_call(
        merge_kernel,
        out_shape=jax.ShapeDtypeStruct((TILE, value_width), jnp.bfloat16),
        in_specs=[vmem] * (2 + len(returned)),
        out_specs=vmem,
        compiler_params=params(),
    )(total, stats, *returned)


def solution(mesh):
    in_specs = (
        P(("groups", "lib", "qry"), None),
        P(("groups", "lib", "qry"), None),
        P(("groups", "lib", "qry"), None),
        P(("groups", "lib", "qry")),
        P("groups", None),
        P("groups"),
    )
    out_specs = P(("groups", "lib", "qry"), None)
    return jax.shard_map(body, mesh=mesh, in_specs=in_specs, out_specs=out_specs, check_vma=False)
```

```python
import functools
import math

import jax
import jax.numpy as jnp
from jax import lax
from jax.experimental import pallas as pl
from jax.experimental.pallas import tpu as pltpu
from jax.sharding import PartitionSpec as P

TILE = 128
LANES = 128
EXTRA = 16
MASKED_SCORE = -1e30
SMEM = pl.BlockSpec(memory_space=pltpu.SMEM)
VMEM = pl.BlockSpec(memory_space=pltpu.VMEM)


def params(operand_bytes=0):
    return pltpu.CompilerParams(vmem_limit_bytes=operand_bytes * 3 // 2 + 6 * 1024 * 1024)


def swap(value, axis, mask):
    length = lax.axis_size(axis)
    return lax.ppermute(value, axis, [(i, i ^ mask) for i in range(length)])


def tie(*values):
    return lax.optimization_barrier(values)


def split_three(value):
    high = value.astype(jnp.bfloat16)
    rest = value - high.astype(jnp.float32)
    middle = rest.astype(jnp.bfloat16)
    low = (rest - middle.astype(jnp.float32)).astype(jnp.bfloat16)
    return high, middle, low


def pack_kernel(values_ref, scale_ref, packed_ref):
    value_width = values_ref.shape[1]
    packed_ref[0:TILE, :] = values_ref[...]
    row = scale_ref[...].astype(jnp.float32)
    packed_ref[TILE:, 0:TILE] = jnp.broadcast_to(row, (EXTRA, TILE)).astype(jnp.bfloat16)
    packed_ref[TILE:, TILE:] = jnp.zeros((EXTRA, value_width - TILE), jnp.bfloat16)


def bundle_kernel(*refs):
    bundle_ref, at = refs[-1], 0
    width = bundle_ref.shape[1]
    for ref in refs[:-1]:
        rows = ref.shape[0]
        for column in range(0, ref.shape[1], width):
            bundle_ref[at : at + rows, :] = ref[:, column : column + width]
            at += rows


class Piece:
    def __init__(self, place, keys_ref=None, values_ref=None, bundle_ref=None, first_row=0):
        self.place = place
        self.refs = (keys_ref, values_ref, bundle_ref)
        self.first_row = first_row

    def scores(self, query_ref, inverse_root):
        keys_ref, values_ref, bundle_ref = self.refs
        width = query_ref.shape[1]
        dims = (((1,), (1,)), ((), ()))
        if bundle_ref is None:
            product = lax.dot_general(query_ref[...], keys_ref[...], dims, preferred_element_type=jnp.float32)
            scale = values_ref[TILE : TILE + EXTRA, 0:TILE]
        else:
            group = bundle_ref.shape[1]
            product = 0.0
            for at in range(width // group):
                rows = pl.ds(self.first_row + at * TILE, TILE)
                product = product + lax.dot_general(
                    query_ref[:, at * group : (at + 1) * group],
                    bundle_ref[rows, :],
                    dims,
                    preferred_element_type=jnp.float32,
                )
            scale = bundle_ref[pl.ds(self.first_row + width // group * TILE + TILE, EXTRA), 0:TILE]
        return product * (scale.astype(jnp.float32)[0:1] * inverse_root)

    def values(self, width):
        keys_ref, values_ref, bundle_ref = self.refs
        if bundle_ref is None:
            return values_ref[0:TILE, :]
        return bundle_ref[pl.ds(self.first_row + width // bundle_ref.shape[1] * TILE, TILE), :]


def read_pieces(layout, width, refs):
    pieces = []
    for entry in layout:
        if entry[0] == "pair":
            pieces.append(Piece(entry[1], refs[0], refs[1]))
            refs = refs[2:]
        else:
            for at, place in enumerate(entry[1]):
                group = refs[0].shape[1]
                rows = (width // group + 1) * TILE + EXTRA
                pieces.append(Piece(place, bundle_ref=refs[0], first_row=at * rows))
            refs = refs[1:]
    return pieces, refs


def attend(pieces, panel_mask, lists_ref, counts_ref, query_ref, score_ref, total_ref, mass_ref):
    lib_index = lax.axis_index("lib")
    qry_index = lax.axis_index("qry")
    qry_count = lax.axis_size("qry")
    block_total = lax.axis_size("lib") * qry_count
    panel = lib_index * qry_count + lax.bitwise_xor(qry_index, panel_mask)
    first = lists_ref[panel, 0]
    count = counts_ref[panel]
    width = query_ref.shape[1]
    inverse_root = 1.0 / math.sqrt(width)

    def active(lib_mask, qry_mask):
        block = lax.bitwise_xor(lib_index, lib_mask) * qry_count + lax.bitwise_xor(qry_index, qry_mask)
        return lax.rem(block - first + block_total, block_total) < count

    flags = [active(*piece.place) for piece in pieces]
    score_ref[...] = jnp.full(score_ref.shape, MASKED_SCORE, jnp.float32)
    total_ref[...] = jnp.zeros(total_ref.shape, jnp.float32)
    mass_ref[...] = jnp.zeros(mass_ref.shape, jnp.float32)
    for at, (piece, flag) in enumerate(zip(pieces, flags)):

        @pl.when(flag)
        def _(at=at, piece=piece):
            score_ref[at] = piece.scores(query_ref, inverse_root)

    largest = score_ref[0]
    for at in range(1, len(flags)):
        largest = jnp.maximum(largest, score_ref[at])
    row_max = jnp.max(largest, axis=1, keepdims=True)
    for at, (piece, flag) in enumerate(zip(pieces, flags)):

        @pl.when(flag)
        def _(at=at, piece=piece):
            weights = jnp.exp(score_ref[at] - row_max)
            mass_ref[...] += weights
            weight_high = weights.astype(jnp.bfloat16)
            weight_low = (weights - weight_high.astype(jnp.float32)).astype(jnp.bfloat16)
            values = piece.values(width)
            added = jnp.dot(weight_high, values, preferred_element_type=jnp.float32)
            added = added + jnp.dot(weight_low, values, preferred_element_type=jnp.float32)
            total_ref[...] += added

    return row_max


def visit_kernel(layout, panel_mask, lists_ref, counts_ref, query_ref, *refs):
    pieces, refs = read_pieces(layout, query_ref.shape[1], refs)
    packed_ref, score_ref, total_ref, mass_ref = refs
    row_max = attend(pieces, panel_mask, lists_ref, counts_ref, query_ref, score_ref, total_ref, mass_ref)
    row_sum = jnp.sum(mass_ref[...], axis=1, keepdims=True)
    value_width = total_ref.shape[1]
    divisor = jnp.where(row_sum > 0.0, row_sum, 1.0)
    packed_ref[0:TILE, :] = (total_ref[...] / divisor).astype(jnp.bfloat16)
    row = lax.broadcasted_iota(jnp.int32, (EXTRA, LANES), 0)
    packed = jnp.zeros((EXTRA, LANES), jnp.float32)
    for first, column in ((0, row_max), (3, row_sum)):
        turned = jnp.transpose(jnp.broadcast_to(column, (TILE, LANES)))[0:EXTRA]
        for at, part in enumerate(split_three(turned)):
            packed = jnp.where(row == first + at, part.astype(jnp.float32), packed)
    packed_ref[TILE:, 0:LANES] = packed.astype(jnp.bfloat16)
    packed_ref[TILE:, LANES:] = jnp.zeros((EXTRA, value_width - LANES), jnp.bfloat16)


def home_kernel(layout, lists_ref, counts_ref, query_ref, *refs):
    pieces, refs = read_pieces(layout, query_ref.shape[1], refs)
    total_ref, stats_ref, score_ref, mass_ref = refs
    row_max = attend(pieces, 0, lists_ref, counts_ref, query_ref, score_ref, total_ref, mass_ref)
    row_sum = jnp.sum(mass_ref[...], axis=1, keepdims=True)
    stats_ref[0] = jnp.broadcast_to(row_max, (TILE, LANES))
    stats_ref[1] = jnp.broadcast_to(row_sum, (TILE, LANES))


def merge_kernel(total_ref, stats_ref, *refs):
    packed_refs, out_ref = refs[:-1], refs[-1]
    maxima = [stats_ref[0]]
    sums = [stats_ref[1]]
    for packed_ref in packed_refs:
        packed = packed_ref[TILE:, 0:LANES].astype(jnp.float32)
        for first, kept in ((0, maxima), (3, sums)):
            line = packed[first : first + 1] + packed[first + 1 : first + 2] + packed[first + 2 : first + 3]
            kept.append(jnp.transpose(jnp.broadcast_to(line, (TILE, LANES))))
    top = functools.reduce(jnp.maximum, maxima)
    factors = [jnp.exp(row_max - top) for row_max in maxima]
    masses = [factor * row_sum for factor, row_sum in zip(factors, sums)]
    inverse = 1.0 / functools.reduce(jnp.add, masses)
    scales = [factors[0] * inverse] + [mass * inverse for mass in masses[1:]]
    for at in range(0, total_ref.shape[1], LANES):
        merged = total_ref[:, at : at + LANES] * scales[0]
        for packed_ref, scale in zip(packed_refs, scales[1:]):
            merged = merged + packed_ref[0:TILE, at : at + LANES].astype(jnp.float32) * scale
        out_ref[:, at : at + LANES] = merged.astype(jnp.bfloat16)


def gather_library(keys, values):
    steps = [("qry", 1)]
    mask = lax.axis_size("lib") // 2
    while mask > 1:
        steps.append(("lib", mask))
        mask //= 2
    early, late = [((0, 0), keys, values)], []
    for axis, mask in steps:
        place = (0, mask) if axis == "qry" else (mask, 0)
        near = (place, swap(keys, axis, mask), swap(values, axis, mask))
        relayed = []
        for (lib_mask, qry_mask), far_keys, far_values in early[1:] + late:
            far_keys, _ = tie(far_keys, near[1])
            far_values, _ = tie(far_values, near[2])
            place = (lib_mask | mask, qry_mask)
            relayed.append((place, swap(far_keys, axis, mask), swap(far_values, axis, mask)))
        early, late = early + late + [near], relayed
    return early, late


def body(queries, library_keys, library_values, key_scale, block_list, block_count):
    qry_count = lax.axis_size("qry")
    width = library_keys.shape[1]
    value_width = library_values.shape[1]

    values = pl.pallas_call(
        pack_kernel,
        out_shape=jax.ShapeDtypeStruct((TILE + EXTRA, value_width), jnp.bfloat16),
        in_specs=[VMEM, VMEM],
        out_specs=VMEM,
        compiler_params=params(),
    )(library_values, key_scale.reshape(1, TILE))

    early, late = gather_library(library_keys, values)
    piece_rows = (width // value_width + 1) * TILE + EXTRA
    early_arrays = [array for piece in early for array in piece[1:]]
    bundle = pl.pallas_call(
        bundle_kernel,
        out_shape=jax.ShapeDtypeStruct((len(early) * piece_rows, value_width), jnp.bfloat16),
        in_specs=[VMEM] * len(early_arrays),
        out_specs=VMEM,
        compiler_params=params(2 * len(early) * piece_rows * value_width * 2),
    )(*early_arrays)
    bundle, *_ = tie(bundle, *(piece[1] for piece in late))
    bundle = swap(bundle, "lib", 1)
    layout = [("pair", piece[0]) for piece in early]
    layout.append(("bundle", [(lib_mask | 1, qry_mask) for (lib_mask, qry_mask), *_ in early]))
    arrays = early_arrays + [bundle]
    for (lib_mask, qry_mask), *pair in late:
        layout += [("pair", (lib_mask, qry_mask)), ("pair", (lib_mask | 1, qry_mask))]
        arrays += pair + [swap(array, "lib", 1) for array in pair]

    count = 2 * (len(early) + len(late))
    cost = pl.CostEstimate(flops=2 * TILE * 4 * TILE * width * 2, bytes_accessed=4 * 1024 * 1024, transcendentals=0)
    scratch = [
        pltpu.VMEM((count, TILE, TILE), jnp.float32),
        pltpu.VMEM((TILE, value_width), jnp.float32),
        pltpu.VMEM((TILE, TILE), jnp.float32),
    ]
    attend_params = params(count * piece_rows * value_width * 2)
    in_specs = [SMEM, SMEM] + [VMEM] * (1 + len(arrays))
    returned = []
    for at in range(1, qry_count // 2):
        visitors, *_ = tie(queries, early[1][1], early[1][2])
        visitors = swap(visitors, "qry", 2 * at + 1)
        packed = pl.pallas_call(
            functools.partial(visit_kernel, layout, 2 * at + 1),
            out_shape=jax.ShapeDtypeStruct((TILE + EXTRA, value_width), jnp.bfloat16),
            in_specs=in_specs,
            out_specs=VMEM,
            scratch_shapes=scratch,
            compiler_params=attend_params,
            cost_estimate=cost,
        )(block_list, block_count, visitors, *arrays)
        returned.append(swap(packed, "qry", 2 * at + 1))

    total, stats = pl.pallas_call(
        functools.partial(home_kernel, layout),
        out_shape=(
            jax.ShapeDtypeStruct((TILE, value_width), jnp.float32),
            jax.ShapeDtypeStruct((2, TILE, LANES), jnp.float32),
        ),
        in_specs=in_specs,
        out_specs=(VMEM, VMEM),
        scratch_shapes=[scratch[0], scratch[2]],
        compiler_params=attend_params,
        cost_estimate=cost,
    )(block_list, block_count, queries, *arrays)

    return pl.pallas_call(
        merge_kernel,
        out_shape=jax.ShapeDtypeStruct((TILE, value_width), jnp.bfloat16),
        in_specs=[VMEM] * (2 + len(returned)),
        out_specs=VMEM,
        compiler_params=params(),
    )(total, stats, *returned)


def solution(mesh):
    in_specs = (
        P(("groups", "lib", "qry"), None),
        P(("groups", "lib", "qry"), None),
        P(("groups", "lib", "qry"), None),
        P(("groups", "lib", "qry")),
        P("groups", None),
        P("groups"),
    )
    out_specs = P(("groups", "lib", "qry"), None)
    return jax.shard_map(body, mesh=mesh, in_specs=in_specs, out_specs=out_specs, check_vma=False)
```

```python
import functools
import math

import jax
import jax.numpy as jnp
from jax import lax
from jax.experimental import pallas as pl
from jax.experimental.pallas import tpu as pltpu
from jax.sharding import PartitionSpec as P

TILE = 128
LANES = 128
EXTRA = 16
MASKED_SCORE = -1e30
SMEM = pl.BlockSpec(memory_space=pltpu.SMEM)
VMEM = pl.BlockSpec(memory_space=pltpu.VMEM)


def params(operand_bytes=0):
    return pltpu.CompilerParams(vmem_limit_bytes=operand_bytes * 3 // 2 + 6 * 1024 * 1024)


def swap(value, axis, mask):
    length = lax.axis_size(axis)
    return lax.ppermute(value, axis, [(i, i ^ mask) for i in range(length)])


def swap_some(value, axis, mask, inner):
    length = lax.axis_size(axis)
    pairs = [(i, i ^ mask) for i in range(length) if (abs(i - (i ^ mask)) * 2 <= mask) == inner]
    return lax.ppermute(value, axis, pairs)


def tie(*values):
    return lax.optimization_barrier(values)


def split_three(value):
    high = value.astype(jnp.bfloat16)
    rest = value - high.astype(jnp.float32)
    middle = rest.astype(jnp.bfloat16)
    low = (rest - middle.astype(jnp.float32)).astype(jnp.bfloat16)
    return high, middle, low


def pack_kernel(values_ref, scale_ref, packed_ref, row_ref, sems):
    value_width = values_ref.shape[1]
    copies = (
        pltpu.make_async_copy(values_ref, packed_ref.at[pl.ds(0, TILE)], sems.at[0]),
        pltpu.make_async_copy(scale_ref, row_ref, sems.at[1]),
    )
    for copy in copies:
        copy.start()
    packed_ref[TILE:, TILE:] = jnp.zeros((EXTRA, value_width - TILE), jnp.bfloat16)
    for copy in reversed(copies):
        copy.wait()
    row = row_ref[...].astype(jnp.float32)
    packed_ref[TILE:, 0:TILE] = jnp.broadcast_to(row, (EXTRA, TILE)).astype(jnp.bfloat16)


def bundle_kernel(*refs):
    bundle_ref, at = refs[-1], 0
    width = bundle_ref.shape[1]
    for ref in refs[:-1]:
        rows = ref.shape[0]
        for column in range(0, ref.shape[1], width):
            bundle_ref[at : at + rows, :] = ref[:, column : column + width]
            at += rows


class Piece:
    def __init__(self, place, keys_ref=None, values_ref=None, bundle_ref=None, first_row=0):
        self.place = place
        self.refs = (keys_ref, values_ref, bundle_ref)
        self.first_row = first_row

    def scores(self, query_ref, inverse_root):
        keys_ref, values_ref, bundle_ref = self.refs
        width = query_ref.shape[1]
        dims = (((1,), (1,)), ((), ()))
        if bundle_ref is None:
            product = lax.dot_general(query_ref[...], keys_ref[...], dims, preferred_element_type=jnp.float32)
            scale = values_ref[TILE : TILE + EXTRA, 0:TILE]
        else:
            group = bundle_ref.shape[1]
            product = 0.0
            for at in range(width // group):
                rows = pl.ds(self.first_row + at * TILE, TILE)
                product = product + lax.dot_general(
                    query_ref[:, at * group : (at + 1) * group],
                    bundle_ref[rows, :],
                    dims,
                    preferred_element_type=jnp.float32,
                )
            scale = bundle_ref[pl.ds(self.first_row + width // group * TILE + TILE, EXTRA), 0:TILE]
        return product * (scale.astype(jnp.float32)[0:1] * inverse_root)

    def values(self, width):
        keys_ref, values_ref, bundle_ref = self.refs
        if bundle_ref is None:
            return values_ref[0:TILE, :]
        return bundle_ref[pl.ds(self.first_row + width // bundle_ref.shape[1] * TILE, TILE), :]


def read_pieces(layout, width, refs):
    pieces = []
    for entry in layout:
        if entry[0] == "pair":
            pieces.append(Piece(entry[1], refs[0], refs[1]))
            refs = refs[2:]
        else:
            for at, place in enumerate(entry[1]):
                group = refs[0].shape[1]
                rows = (width // group + 1) * TILE + EXTRA
                pieces.append(Piece(place, bundle_ref=refs[0], first_row=at * rows))
            refs = refs[1:]
    return pieces, refs


def attend(pieces, panel_mask, lists_ref, counts_ref, query_ref, score_ref, total_ref, mass_ref, before=None):
    lib_index = lax.axis_index("lib")
    qry_index = lax.axis_index("qry")
    qry_count = lax.axis_size("qry")
    block_total = lax.axis_size("lib") * qry_count
    panel = lib_index * qry_count + lax.bitwise_xor(qry_index, panel_mask)
    first = lists_ref[panel, 0]
    count = counts_ref[panel]
    width = query_ref.shape[1]
    inverse_root = 1.0 / math.sqrt(width)

    def active(lib_mask, qry_mask):
        block = lax.bitwise_xor(lib_index, lib_mask) * qry_count + lax.bitwise_xor(qry_index, qry_mask)
        return lax.rem(block - first + block_total, block_total) < count

    flags = [active(*piece.place) for piece in pieces]
    score_ref[...] = jnp.full(score_ref.shape, MASKED_SCORE, jnp.float32)
    for at, (piece, flag) in enumerate(zip(pieces, flags)):

        @pl.when(flag)
        def _(at=at, piece=piece):
            score_ref[at] = piece.scores(query_ref, inverse_root)

    largest = score_ref[0]
    for at in range(1, len(flags)):
        largest = jnp.maximum(largest, score_ref[at])
    row_max = jnp.max(largest, axis=1, keepdims=True)
    if before is None:
        total_ref[...] = jnp.zeros(total_ref.shape, jnp.float32)
        mass_ref[...] = jnp.zeros(mass_ref.shape, jnp.float32)
    else:
        old_total_ref, old_mass_ref, old_max_ref = before
        old_max = old_max_ref[...]
        new_max = jnp.maximum(old_max, row_max)
        shrink = jnp.exp(old_max - new_max)
        row_max = new_max[:, 0:1]
        mass_ref[...] = old_mass_ref[...] * shrink
        for at in range(0, total_ref.shape[1], LANES):
            total_ref[:, at : at + LANES] = old_total_ref[:, at : at + LANES] * shrink
    for at, (piece, flag) in enumerate(zip(pieces, flags)):

        @pl.when(flag)
        def _(at=at, piece=piece):
            weights = jnp.exp(score_ref[at] - row_max)
            mass_ref[...] += weights
            weight_high = weights.astype(jnp.bfloat16)
            weight_low = (weights - weight_high.astype(jnp.float32)).astype(jnp.bfloat16)
            values = piece.values(width)
            added = jnp.dot(weight_high, values, preferred_element_type=jnp.float32)
            added = added + jnp.dot(weight_low, values, preferred_element_type=jnp.float32)
            total_ref[...] += added

    return row_max


def is_inner(mask):
    index = lax.axis_index("qry")
    return jnp.abs(index - lax.bitwise_xor(index, mask)) * 2 <= mask


def early_kernel(layout, panel_mask, lists_ref, counts_ref, inner_ref, outer_ref, *refs):
    pieces, refs = read_pieces(layout, inner_ref.shape[1], refs)
    query_ref, total_ref, mass_ref, max_ref, score_ref = refs
    inner = is_inner(panel_mask)

    @pl.when(inner)
    def _():
        query_ref[...] = inner_ref[...]

    @pl.when(jnp.logical_not(inner))
    def _():
        query_ref[...] = outer_ref[...]

    row_max = attend(pieces, panel_mask, lists_ref, counts_ref, query_ref, score_ref, total_ref, mass_ref)
    max_ref[...] = jnp.broadcast_to(row_max, max_ref.shape)


def late_kernel(layout, panel_mask, lists_ref, counts_ref, query_ref, *refs):
    before, refs = refs[:3], refs[3:]
    pieces, refs = read_pieces(layout, query_ref.shape[1], refs)
    packed_ref, score_ref, total_ref, mass_ref = refs
    row_max = attend(pieces, panel_mask, lists_ref, counts_ref, query_ref, score_ref, total_ref, mass_ref, before)
    row_sum = jnp.sum(mass_ref[...], axis=1, keepdims=True)
    value_width = total_ref.shape[1]
    inverse = 1.0 / jnp.where(row_sum > 0.0, row_sum, 1.0)
    packed_ref[0:TILE, :] = (total_ref[...] * inverse).astype(jnp.bfloat16)
    row = lax.broadcasted_iota(jnp.int32, (EXTRA, LANES), 0)
    packed = jnp.zeros((EXTRA, LANES), jnp.float32)
    for first, column in ((0, row_max), (3, row_sum)):
        turned = jnp.transpose(jnp.broadcast_to(column, (TILE, LANES)))[0:EXTRA]
        for at, part in enumerate(split_three(turned)):
            packed = jnp.where(row == first + at, part.astype(jnp.float32), packed)
    packed_ref[TILE:, 0:LANES] = packed.astype(jnp.bfloat16)
    packed_ref[TILE:, LANES:] = jnp.zeros((EXTRA, value_width - LANES), jnp.bfloat16)


def home_kernel(layout, lists_ref, counts_ref, query_ref, *refs):
    pieces, refs = read_pieces(layout, query_ref.shape[1], refs)
    total_ref, stats_ref, score_ref, mass_ref = refs
    row_max = attend(pieces, 0, lists_ref, counts_ref, query_ref, score_ref, total_ref, mass_ref)
    row_sum = jnp.sum(mass_ref[...], axis=1, keepdims=True)
    stats_ref[0] = jnp.broadcast_to(row_max, (TILE, LANES))
    stats_ref[1] = jnp.broadcast_to(row_sum, (TILE, LANES))


def merge_kernel(total_ref, stats_ref, *refs):
    packed_refs, out_ref = refs[:-1], refs[-1]
    maxima = [stats_ref[0]]
    sums = [stats_ref[1]]
    for packed_ref in packed_refs:
        packed = packed_ref[TILE:, 0:LANES].astype(jnp.float32)
        for first, kept in ((0, maxima), (3, sums)):
            line = packed[first : first + 1] + packed[first + 1 : first + 2] + packed[first + 2 : first + 3]
            kept.append(jnp.transpose(jnp.broadcast_to(line, (TILE, LANES))))
    top = functools.reduce(jnp.maximum, maxima)
    factors = [jnp.exp(row_max - top) for row_max in maxima]
    masses = [factor * row_sum for factor, row_sum in zip(factors, sums)]
    inverse = 1.0 / functools.reduce(jnp.add, masses)
    scales = [factors[0] * inverse] + [mass * inverse for mass in masses[1:]]
    for at in range(0, total_ref.shape[1], LANES):
        merged = total_ref[:, at : at + LANES] * scales[0]
        for packed_ref, scale in zip(packed_refs, scales[1:]):
            merged = merged + packed_ref[0:TILE, at : at + LANES].astype(jnp.float32) * scale
        out_ref[:, at : at + LANES] = merged.astype(jnp.bfloat16)


def gather_library(keys, values, first_arrivals):
    steps = [("qry", 1)]
    mask = lax.axis_size("lib") // 2
    while mask > 1:
        steps.append(("lib", mask))
        mask //= 2
    early, late = [((0, 0), keys, values)], []
    for axis, mask in steps:
        place = (0, mask) if axis == "qry" else (mask, 0)
        near = (place, swap(keys, axis, mask), swap(values, axis, mask))
        relayed = []
        for (lib_mask, qry_mask), far_keys, far_values in early[1:] + late:
            far_keys, far_values, *_ = tie(far_keys, far_values, near[1], near[2], *first_arrivals)
            place = (lib_mask | mask, qry_mask)
            relayed.append((place, swap(far_keys, axis, mask), swap(far_values, axis, mask)))
        early, late = early + late + [near], relayed
    return early, late


def both_cores(pieces):
    layout, arrays = [], []
    for (lib_mask, qry_mask), *pair in pieces:
        layout += [("pair", (lib_mask, qry_mask)), ("pair", (lib_mask | 1, qry_mask))]
        arrays += pair + [swap(array, "lib", 1) for array in pair]
    return layout, arrays


def body(queries, library_keys, library_values, key_scale, block_list, block_count):
    qry_count = lax.axis_size("qry")
    width = library_keys.shape[1]
    value_width = library_values.shape[1]

    values = pl.pallas_call(
        pack_kernel,
        out_shape=jax.ShapeDtypeStruct((TILE + EXTRA, value_width), jnp.bfloat16),
        in_specs=[pl.BlockSpec(memory_space=pl.ANY)] * 2,
        out_specs=VMEM,
        scratch_shapes=[pltpu.VMEM((1, TILE), jnp.bfloat16), pltpu.SemaphoreType.DMA((2,))],
        compiler_params=params(),
    )(library_values, key_scale.reshape(1, TILE))

    masks = [2 * at + 1 for at in range(1, qry_count // 2)]
    inner = [swap_some(queries, "qry", mask, True) for mask in masks]
    early, late = gather_library(library_keys, values, inner)
    piece_rows = (width // value_width + 1) * TILE + EXTRA
    (early_layout, early_arrays), (late_layout, late_arrays) = both_cores(early), both_cores(late)
    count_early, count_late = 2 * len(early), 2 * len(late)

    cost = pl.CostEstimate(flops=2 * TILE * 4 * TILE * width * 2, bytes_accessed=4 * 1024 * 1024, transcendentals=0)
    total_shape = jax.ShapeDtypeStruct((TILE, value_width), jnp.float32)
    line_shape = jax.ShapeDtypeStruct((TILE, LANES), jnp.float32)
    attend_params = params((count_early + count_late) * piece_rows * value_width * 2)
    returned = []
    for mask, inner_queries in zip(masks, inner):
        waiting, *_ = tie(queries, early[1][1], early[1][2])
        *state, = pl.pallas_call(
            functools.partial(early_kernel, early_layout, mask),
            out_shape=(jax.ShapeDtypeStruct(queries.shape, queries.dtype), total_shape, line_shape, line_shape),
            in_specs=[SMEM, SMEM] + [VMEM] * (2 + len(early_arrays)),
            out_specs=(VMEM,) * 4,
            scratch_shapes=[pltpu.VMEM((count_early, TILE, TILE), jnp.float32)],
            compiler_params=attend_params,
            cost_estimate=cost,
        )(
            block_list,
            block_count,
            inner_queries,
            swap_some(waiting, "qry", mask, False),
            *early_arrays,
        )
        packed = pl.pallas_call(
            functools.partial(late_kernel, late_layout, mask),
            out_shape=jax.ShapeDtypeStruct((TILE + EXTRA, value_width), jnp.bfloat16),
            in_specs=[SMEM, SMEM] + [VMEM] * (4 + len(late_arrays)),
            out_specs=VMEM,
            scratch_shapes=[
                pltpu.VMEM((count_late, TILE, TILE), jnp.float32),
                pltpu.VMEM((TILE, value_width), jnp.float32),
                pltpu.VMEM((TILE, TILE), jnp.float32),
            ],
            compiler_params=attend_params,
            cost_estimate=cost,
        )(block_list, block_count, *state, *late_arrays)
        returned.append(swap(packed, "qry", mask))

    total, stats = pl.pallas_call(
        functools.partial(home_kernel, early_layout + late_layout),
        out_shape=(total_shape, jax.ShapeDtypeStruct((2, TILE, LANES), jnp.float32)),
        in_specs=[SMEM, SMEM] + [VMEM] * (1 + len(early_arrays) + len(late_arrays)),
        out_specs=(VMEM, VMEM),
        scratch_shapes=[
            pltpu.VMEM((count_early + count_late, TILE, TILE), jnp.float32),
            pltpu.VMEM((TILE, TILE), jnp.float32),
        ],
        compiler_params=attend_params,
        cost_estimate=cost,
    )(block_list, block_count, queries, *early_arrays, *late_arrays)

    return pl.pallas_call(
        merge_kernel,
        out_shape=jax.ShapeDtypeStruct((TILE, value_width), jnp.bfloat16),
        in_specs=[VMEM] * (2 + len(returned)),
        out_specs=VMEM,
        compiler_params=params(),
    )(total, stats, *returned)


def solution(mesh):
    in_specs = (
        P(("groups", "lib", "qry"), None),
        P(("groups", "lib", "qry"), None),
        P(("groups", "lib", "qry"), None),
        P(("groups", "lib", "qry")),
        P("groups", None),
        P("groups"),
    )
    out_specs = P(("groups", "lib", "qry"), None)
    return jax.shard_map(body, mesh=mesh, in_specs=in_specs, out_specs=out_specs, check_vma=False)
```

```python
import functools
import math

import jax
import jax.numpy as jnp
from jax import lax
from jax.experimental import pallas as pl
from jax.experimental.pallas import tpu as pltpu
from jax.sharding import PartitionSpec as P

TILE = 128
LANES = 128
EXTRA = 16
MASKED_SCORE = -1e30
SMEM = pl.BlockSpec(memory_space=pltpu.SMEM)
VMEM = pl.BlockSpec(memory_space=pltpu.VMEM)


def params(operand_bytes=0):
    return pltpu.CompilerParams(vmem_limit_bytes=operand_bytes * 3 // 2 + 6 * 1024 * 1024)


def swap(value, axis, mask):
    length = lax.axis_size(axis)
    return lax.ppermute(value, axis, [(i, i ^ mask) for i in range(length)])


def swap_some(value, axis, mask, inner):
    length = lax.axis_size(axis)
    pairs = [(i, i ^ mask) for i in range(length) if (abs(i - (i ^ mask)) * 2 <= mask) == inner]
    return lax.ppermute(value, axis, pairs)


def tie(*values):
    return lax.optimization_barrier(values)


def split_three(value):
    high = value.astype(jnp.bfloat16)
    rest = value - high.astype(jnp.float32)
    middle = rest.astype(jnp.bfloat16)
    low = (rest - middle.astype(jnp.float32)).astype(jnp.bfloat16)
    return high, middle, low


def pack_kernel(keys_ref, values_ref, scale_ref, packed_ref, row_ref, last_ref, sems):
    width = packed_ref.shape[1]
    groups = keys_ref.shape[1] // width
    row_copy = pltpu.make_async_copy(scale_ref, row_ref, sems.at[0])
    row_copy.start()
    copies = []
    for at in range(groups):
        columns = keys_ref.at[:, pl.ds(at * width, width)]
        copies.append(pltpu.make_async_copy(columns, packed_ref.at[pl.ds(at * TILE, TILE)], sems.at[1 + at]))
    copies.append(pltpu.make_async_copy(values_ref, packed_ref.at[pl.ds(groups * TILE, TILE)], sems.at[1 + groups]))
    for copy in copies:
        copy.start()
    last_ref[:, TILE:] = jnp.zeros((EXTRA, width - TILE), jnp.bfloat16)
    row_copy.wait()
    row = row_ref[...].astype(jnp.float32)
    last_ref[:, 0:TILE] = jnp.broadcast_to(row, (EXTRA, TILE)).astype(jnp.bfloat16)
    last_rows = packed_ref.at[pl.ds((groups + 1) * TILE, EXTRA)]
    last_copy = pltpu.make_async_copy(last_ref, last_rows, sems.at[2 + groups])
    last_copy.start()
    for copy in copies + [last_copy]:
        copy.wait()


class Piece:
    def __init__(self, place, ref):
        self.place = place
        self.ref = ref

    def scores(self, query_ref, inverse_root):
        group = self.ref.shape[1]
        groups = query_ref.shape[1] // group
        product = 0.0
        for at in range(groups):
            product = product + lax.dot_general(
                query_ref[:, at * group : (at + 1) * group],
                self.ref[at * TILE : (at + 1) * TILE, :],
                (((1,), (1,)), ((), ())),
                preferred_element_type=jnp.float32,
            )
        scale = self.ref[(groups + 1) * TILE :, 0:TILE].astype(jnp.float32)[0:1]
        return product * (scale * inverse_root)

    def values(self, width):
        first = width // self.ref.shape[1] * TILE
        return self.ref[first : first + TILE, :]


def attend(pieces, panel_mask, lists_ref, counts_ref, query_ref, score_ref, total_ref, mass_ref, before=None):
    lib_index = lax.axis_index("lib")
    qry_index = lax.axis_index("qry")
    qry_count = lax.axis_size("qry")
    block_total = lax.axis_size("lib") * qry_count
    panel = lib_index * qry_count + lax.bitwise_xor(qry_index, panel_mask)
    first = lists_ref[panel, 0]
    count = counts_ref[panel]
    width = query_ref.shape[1]
    inverse_root = 1.0 / math.sqrt(width)

    def active(lib_mask, qry_mask):
        block = lax.bitwise_xor(lib_index, lib_mask) * qry_count + lax.bitwise_xor(qry_index, qry_mask)
        return lax.rem(block - first + block_total, block_total) < count

    flags = [active(*piece.place) for piece in pieces]
    score_ref[...] = jnp.full(score_ref.shape, MASKED_SCORE, jnp.float32)
    for at, (piece, flag) in enumerate(zip(pieces, flags)):

        @pl.when(flag)
        def _(at=at, piece=piece):
            score_ref[at] = piece.scores(query_ref, inverse_root)

    largest = score_ref[0]
    for at in range(1, len(flags)):
        largest = jnp.maximum(largest, score_ref[at])
    row_max = jnp.max(largest, axis=1, keepdims=True)
    if before is None:
        total_ref[...] = jnp.zeros(total_ref.shape, jnp.float32)
        mass_ref[...] = jnp.zeros(mass_ref.shape, jnp.float32)
    else:
        old_total_ref, old_mass_ref, old_max_ref = before
        old_max = old_max_ref[...]
        new_max = jnp.maximum(old_max, row_max)
        shrink = jnp.exp(old_max - new_max)
        row_max = new_max[:, 0:1]
        mass_ref[...] = old_mass_ref[...] * shrink
        for at in range(0, total_ref.shape[1], LANES):
            total_ref[:, at : at + LANES] = old_total_ref[:, at : at + LANES] * shrink
    for at, (piece, flag) in enumerate(zip(pieces, flags)):

        @pl.when(flag)
        def _(at=at, piece=piece):
            weights = jnp.exp(score_ref[at] - row_max)
            mass_ref[...] += weights
            weight_high = weights.astype(jnp.bfloat16)
            weight_low = (weights - weight_high.astype(jnp.float32)).astype(jnp.bfloat16)
            values = piece.values(width)
            added = jnp.dot(weight_high, values, preferred_element_type=jnp.float32)
            added = added + jnp.dot(weight_low, values, preferred_element_type=jnp.float32)
            total_ref[...] += added

    return row_max


def is_inner(mask):
    index = lax.axis_index("qry")
    return jnp.abs(index - lax.bitwise_xor(index, mask)) * 2 <= mask


def read_pieces(places, refs):
    count = len(places)
    return [Piece(place, ref) for place, ref in zip(places, refs)], refs[count:]


def early_kernel(places, panel_mask, lists_ref, counts_ref, inner_ref, outer_ref, *refs):
    pieces, refs = read_pieces(places, refs)
    query_ref, total_ref, mass_ref, max_ref, score_ref = refs
    inner = is_inner(panel_mask)

    @pl.when(inner)
    def _():
        query_ref[...] = inner_ref[...]

    @pl.when(jnp.logical_not(inner))
    def _():
        query_ref[...] = outer_ref[...]

    row_max = attend(pieces, panel_mask, lists_ref, counts_ref, query_ref, score_ref, total_ref, mass_ref)
    max_ref[...] = jnp.broadcast_to(row_max, max_ref.shape)


def late_kernel(places, panel_mask, lists_ref, counts_ref, query_ref, *refs):
    before, refs = refs[:3], refs[3:]
    pieces, refs = read_pieces(places, refs)
    packed_ref, score_ref, total_ref, mass_ref = refs
    row_max = attend(pieces, panel_mask, lists_ref, counts_ref, query_ref, score_ref, total_ref, mass_ref, before)
    row_sum = jnp.sum(mass_ref[...], axis=1, keepdims=True)
    value_width = total_ref.shape[1]
    inverse = 1.0 / jnp.where(row_sum > 0.0, row_sum, 1.0)
    packed_ref[0:TILE, :] = (total_ref[...] * inverse).astype(jnp.bfloat16)
    row = lax.broadcasted_iota(jnp.int32, (EXTRA, LANES), 0)
    packed = jnp.zeros((EXTRA, LANES), jnp.float32)
    for first, column in ((0, row_max), (3, row_sum)):
        turned = jnp.transpose(jnp.broadcast_to(column, (TILE, LANES)))[0:EXTRA]
        for at, part in enumerate(split_three(turned)):
            packed = jnp.where(row == first + at, part.astype(jnp.float32), packed)
    packed_ref[TILE:, 0:LANES] = packed.astype(jnp.bfloat16)
    packed_ref[TILE:, LANES:] = jnp.zeros((EXTRA, value_width - LANES), jnp.bfloat16)


def home_kernel(places, lists_ref, counts_ref, query_ref, *refs):
    pieces, refs = read_pieces(places, refs)
    total_ref, stats_ref, score_ref, mass_ref = refs
    row_max = attend(pieces, 0, lists_ref, counts_ref, query_ref, score_ref, total_ref, mass_ref)
    row_sum = jnp.sum(mass_ref[...], axis=1, keepdims=True)
    stats_ref[0] = jnp.broadcast_to(row_max, (TILE, LANES))
    stats_ref[1] = jnp.broadcast_to(row_sum, (TILE, LANES))


def merge_kernel(total_ref, stats_ref, *refs):
    packed_refs, out_ref = refs[:-1], refs[-1]
    maxima = [stats_ref[0]]
    sums = [stats_ref[1]]
    for packed_ref in packed_refs:
        packed = packed_ref[TILE:, 0:LANES].astype(jnp.float32)
        for first, kept in ((0, maxima), (3, sums)):
            line = packed[first : first + 1] + packed[first + 1 : first + 2] + packed[first + 2 : first + 3]
            kept.append(jnp.transpose(jnp.broadcast_to(line, (TILE, LANES))))
    top = functools.reduce(jnp.maximum, maxima)
    factors = [jnp.exp(row_max - top) for row_max in maxima]
    masses = [factor * row_sum for factor, row_sum in zip(factors, sums)]
    inverse = 1.0 / functools.reduce(jnp.add, masses)
    scales = [factors[0] * inverse] + [mass * inverse for mass in masses[1:]]
    for at in range(0, total_ref.shape[1], LANES):
        merged = total_ref[:, at : at + LANES] * scales[0]
        for packed_ref, scale in zip(packed_refs, scales[1:]):
            merged = merged + packed_ref[0:TILE, at : at + LANES].astype(jnp.float32) * scale
        out_ref[:, at : at + LANES] = merged.astype(jnp.bfloat16)


def gather_library(block, queries, masks):
    steps = [("qry", 1)]
    mask = lax.axis_size("lib") // 2
    while mask > 1:
        steps.append(("lib", mask))
        mask //= 2
    own_places, own_arrays = both_cores([((0, 0), block)])
    nearer, _ = tie(queries, own_arrays[1])
    inner = [swap_some(nearer, "qry", mask, True) for mask in masks]
    early, late = [], []
    for axis, mask in steps:
        place = (0, mask) if axis == "qry" else (mask, 0)
        near = (place, swap(block, axis, mask))
        relayed = []
        for (lib_mask, qry_mask), far in early + late:
            far, *_ = tie(far, near[1], *inner)
            relayed.append(((lib_mask | mask, qry_mask), swap(far, axis, mask)))
        early, late = early + late + [near], relayed
    farther, _ = tie(queries, early[0][1])
    outer = [swap_some(farther, "qry", mask, False) for mask in masks]
    early_places, early_arrays = both_cores(early)
    late_places, late_arrays = both_cores(late, outer)
    early = (own_places + early_places, own_arrays + early_arrays)
    return early, (late_places, late_arrays), list(zip(masks, inner, outer))


def both_cores(pieces, arrivals=()):
    places, arrays = [], []
    for (lib_mask, qry_mask), block in pieces:
        sent, *_ = tie(block, *arrivals)
        places += [(lib_mask, qry_mask), (lib_mask | 1, qry_mask)]
        arrays += [block, swap(sent, "lib", 1)]
    return places, arrays


def body(queries, library_keys, library_values, key_scale, block_list, block_count):
    qry_count = lax.axis_size("qry")
    width = library_keys.shape[1]
    value_width = library_values.shape[1]
    piece_rows = (width // value_width + 1) * TILE + EXTRA
    piece_bytes = piece_rows * value_width * 2

    block = pl.pallas_call(
        pack_kernel,
        out_shape=jax.ShapeDtypeStruct((piece_rows, value_width), jnp.bfloat16),
        in_specs=[pl.BlockSpec(memory_space=pl.ANY)] * 3,
        out_specs=pl.BlockSpec(memory_space=pl.ANY),
        scratch_shapes=[
            pltpu.VMEM((1, TILE), jnp.bfloat16),
            pltpu.VMEM((EXTRA, value_width), jnp.bfloat16),
            pltpu.SemaphoreType.DMA((width // value_width + 3,)),
        ],
        compiler_params=pltpu.CompilerParams(vmem_limit_bytes=60 * 1024 * 1024),
    )(library_keys, library_values, key_scale.reshape(1, TILE))

    masks = [2 * at + 1 for at in range(1, qry_count // 2)]
    (early_places, early_arrays), (late_places, late_arrays), visitors = gather_library(block, queries, masks)
    count_early, count_late = len(early_places), len(late_places)

    cost = pl.CostEstimate(flops=2 * TILE * 4 * TILE * width * 2, bytes_accessed=4 * 1024 * 1024, transcendentals=0)
    total_shape = jax.ShapeDtypeStruct((TILE, value_width), jnp.float32)
    line_shape = jax.ShapeDtypeStruct((TILE, LANES), jnp.float32)
    attend_params = params((count_early + count_late) * piece_bytes)
    returned = []
    for mask, inner_queries, outer_queries in visitors:
        *state, = pl.pallas_call(
            functools.partial(early_kernel, early_places, mask),
            out_shape=(jax.ShapeDtypeStruct(queries.shape, queries.dtype), total_shape, line_shape, line_shape),
            in_specs=[SMEM, SMEM] + [VMEM] * (2 + len(early_arrays)),
            out_specs=(VMEM,) * 4,
            scratch_shapes=[pltpu.VMEM((count_early, TILE, TILE), jnp.float32)],
            compiler_params=attend_params,
            cost_estimate=cost,
        )(
            block_list,
            block_count,
            inner_queries,
            outer_queries,
            *early_arrays,
        )
        packed = pl.pallas_call(
            functools.partial(late_kernel, late_places, mask),
            out_shape=jax.ShapeDtypeStruct((TILE + EXTRA, value_width), jnp.bfloat16),
            in_specs=[SMEM, SMEM] + [VMEM] * (4 + len(late_arrays)),
            out_specs=VMEM,
            scratch_shapes=[
                pltpu.VMEM((count_late, TILE, TILE), jnp.float32),
                pltpu.VMEM((TILE, value_width), jnp.float32),
                pltpu.VMEM((TILE, TILE), jnp.float32),
            ],
            compiler_params=attend_params,
            cost_estimate=cost,
        )(block_list, block_count, *state, *late_arrays)
        returned.append(swap(packed, "qry", mask))

    total, stats = pl.pallas_call(
        functools.partial(home_kernel, early_places + late_places),
        out_shape=(total_shape, jax.ShapeDtypeStruct((2, TILE, LANES), jnp.float32)),
        in_specs=[SMEM, SMEM] + [VMEM] * (1 + len(early_arrays) + len(late_arrays)),
        out_specs=(VMEM, VMEM),
        scratch_shapes=[
            pltpu.VMEM((count_early + count_late, TILE, TILE), jnp.float32),
            pltpu.VMEM((TILE, TILE), jnp.float32),
        ],
        compiler_params=attend_params,
        cost_estimate=cost,
    )(block_list, block_count, queries, *early_arrays, *late_arrays)

    return pl.pallas_call(
        merge_kernel,
        out_shape=jax.ShapeDtypeStruct((TILE, value_width), jnp.bfloat16),
        in_specs=[VMEM] * (2 + len(returned)),
        out_specs=VMEM,
        compiler_params=params(),
    )(total, stats, *returned)


def solution(mesh):
    in_specs = (
        P(("groups", "lib", "qry"), None),
        P(("groups", "lib", "qry"), None),
        P(("groups", "lib", "qry"), None),
        P(("groups", "lib", "qry")),
        P("groups", None),
        P("groups"),
    )
    out_specs = P(("groups", "lib", "qry"), None)
    return jax.shard_map(body, mesh=mesh, in_specs=in_specs, out_specs=out_specs, check_vma=False)
```

```python
import functools
import math

import jax
import jax.numpy as jnp
from jax import lax
from jax.experimental import pallas as pl
from jax.experimental.pallas import tpu as pltpu
from jax.sharding import PartitionSpec as P

TILE = 128
LANES = 128
EXTRA = 16
MASKED_SCORE = -1e30
SMEM = pl.BlockSpec(memory_space=pltpu.SMEM)
VMEM = pl.BlockSpec(memory_space=pltpu.VMEM)


def params(operand_bytes=0):
    return pltpu.CompilerParams(vmem_limit_bytes=operand_bytes * 3 // 2 + 6 * 1024 * 1024)


def swap(value, axis, mask):
    length = lax.axis_size(axis)
    return lax.ppermute(value, axis, [(i, i ^ mask) for i in range(length)])


def swap_some(value, axis, mask, inner):
    length = lax.axis_size(axis)
    pairs = [(i, i ^ mask) for i in range(length) if (abs(i - (i ^ mask)) * 2 <= mask) == inner]
    return lax.ppermute(value, axis, pairs)


def tie(*values):
    return lax.optimization_barrier(values)


def split_three(value):
    high = value.astype(jnp.bfloat16)
    rest = value - high.astype(jnp.float32)
    middle = rest.astype(jnp.bfloat16)
    low = (rest - middle.astype(jnp.float32)).astype(jnp.bfloat16)
    return high, middle, low


def pack_kernel(values_ref, scale_ref, packed_ref, row_ref, sems):
    value_width = values_ref.shape[1]
    copies = (
        pltpu.make_async_copy(values_ref, packed_ref.at[pl.ds(0, TILE)], sems.at[0]),
        pltpu.make_async_copy(scale_ref, row_ref, sems.at[1]),
    )
    for copy in copies:
        copy.start()
    packed_ref[TILE:, TILE:] = jnp.zeros((EXTRA, value_width - TILE), jnp.bfloat16)
    for copy in reversed(copies):
        copy.wait()
    row = row_ref[...].astype(jnp.float32)
    packed_ref[TILE:, 0:TILE] = jnp.broadcast_to(row, (EXTRA, TILE)).astype(jnp.bfloat16)


def bundle_kernel(*refs):
    bundle_ref, at = refs[-1], 0
    width = bundle_ref.shape[1]
    for ref in refs[:-1]:
        rows = ref.shape[0]
        for column in range(0, ref.shape[1], width):
            bundle_ref[at : at + rows, :] = ref[:, column : column + width]
            at += rows


class Piece:
    def __init__(self, place, keys_ref=None, values_ref=None, bundle_ref=None, first_row=0):
        self.place = place
        self.refs = (keys_ref, values_ref, bundle_ref)
        self.first_row = first_row

    def scores(self, query_ref, inverse_root):
        keys_ref, values_ref, bundle_ref = self.refs
        width = query_ref.shape[1]
        dims = (((1,), (1,)), ((), ()))
        if bundle_ref is None:
            product = lax.dot_general(query_ref[...], keys_ref[...], dims, preferred_element_type=jnp.float32)
            scale = values_ref[TILE : TILE + EXTRA, 0:TILE]
        else:
            group = bundle_ref.shape[1]
            product = 0.0
            for at in range(width // group):
                rows = pl.ds(self.first_row + at * TILE, TILE)
                product = product + lax.dot_general(
                    query_ref[:, at * group : (at + 1) * group],
                    bundle_ref[rows, :],
                    dims,
                    preferred_element_type=jnp.float32,
                )
            scale = bundle_ref[pl.ds(self.first_row + width // group * TILE + TILE, EXTRA), 0:TILE]
        return product * (scale.astype(jnp.float32)[0:1] * inverse_root)

    def values(self, width):
        keys_ref, values_ref, bundle_ref = self.refs
        if bundle_ref is None:
            return values_ref[0:TILE, :]
        return bundle_ref[pl.ds(self.first_row + width // bundle_ref.shape[1] * TILE, TILE), :]


def read_pieces(layout, width, refs):
    pieces = []
    for entry in layout:
        if entry[0] == "pair":
            pieces.append(Piece(entry[1], refs[0], refs[1]))
            refs = refs[2:]
        else:
            for at, place in enumerate(entry[1]):
                group = refs[0].shape[1]
                rows = (width // group + 1) * TILE + EXTRA
                pieces.append(Piece(place, bundle_ref=refs[0], first_row=at * rows))
            refs = refs[1:]
    return pieces, refs


def attend(pieces, panel_mask, lists_ref, counts_ref, query_ref, score_ref, total_ref, mass_ref, before=None):
    lib_index = lax.axis_index("lib")
    qry_index = lax.axis_index("qry")
    qry_count = lax.axis_size("qry")
    block_total = lax.axis_size("lib") * qry_count
    panel = lib_index * qry_count + lax.bitwise_xor(qry_index, panel_mask)
    first = lists_ref[panel, 0]
    count = counts_ref[panel]
    width = query_ref.shape[1]
    inverse_root = 1.0 / math.sqrt(width)

    def active(lib_mask, qry_mask):
        block = lax.bitwise_xor(lib_index, lib_mask) * qry_count + lax.bitwise_xor(qry_index, qry_mask)
        return lax.rem(block - first + block_total, block_total) < count

    flags = [active(*piece.place) for piece in pieces]
    score_ref[...] = jnp.full(score_ref.shape, MASKED_SCORE, jnp.float32)
    for at, (piece, flag) in enumerate(zip(pieces, flags)):

        @pl.when(flag)
        def _(at=at, piece=piece):
            score_ref[at] = piece.scores(query_ref, inverse_root)

    largest = score_ref[0]
    for at in range(1, len(flags)):
        largest = jnp.maximum(largest, score_ref[at])
    row_max = jnp.max(largest, axis=1, keepdims=True)
    if before is None:
        total_ref[...] = jnp.zeros(total_ref.shape, jnp.float32)
        mass_ref[...] = jnp.zeros(mass_ref.shape, jnp.float32)
    else:
        old_total_ref, old_mass_ref, old_max_ref = before
        old_max = old_max_ref[...]
        new_max = jnp.maximum(old_max, row_max)
        shrink = jnp.exp(old_max - new_max)
        row_max = new_max[:, 0:1]
        mass_ref[...] = old_mass_ref[...] * shrink
        for at in range(0, total_ref.shape[1], LANES):
            total_ref[:, at : at + LANES] = old_total_ref[:, at : at + LANES] * shrink
    for at, (piece, flag) in enumerate(zip(pieces, flags)):

        @pl.when(flag)
        def _(at=at, piece=piece):
            weights = jnp.exp(score_ref[at] - row_max)
            mass_ref[...] += weights
            weight_high = weights.astype(jnp.bfloat16)
            weight_low = (weights - weight_high.astype(jnp.float32)).astype(jnp.bfloat16)
            values = piece.values(width)
            added = jnp.dot(weight_high, values, preferred_element_type=jnp.float32)
            added = added + jnp.dot(weight_low, values, preferred_element_type=jnp.float32)
            total_ref[...] += added

    return row_max


def is_inner(mask):
    index = lax.axis_index("qry")
    return jnp.abs(index - lax.bitwise_xor(index, mask)) * 2 <= mask


def early_kernel(layout, panel_mask, lists_ref, counts_ref, inner_ref, outer_ref, *refs):
    pieces, refs = read_pieces(layout, inner_ref.shape[1], refs)
    query_ref, total_ref, mass_ref, max_ref, score_ref = refs
    inner = is_inner(panel_mask)

    @pl.when(inner)
    def _():
        query_ref[...] = inner_ref[...]

    @pl.when(jnp.logical_not(inner))
    def _():
        query_ref[...] = outer_ref[...]

    row_max = attend(pieces, panel_mask, lists_ref, counts_ref, query_ref, score_ref, total_ref, mass_ref)
    max_ref[...] = jnp.broadcast_to(row_max, max_ref.shape)


def late_kernel(layout, panel_mask, lists_ref, counts_ref, query_ref, *refs):
    before, refs = refs[:3], refs[3:]
    pieces, refs = read_pieces(layout, query_ref.shape[1], refs)
    packed_ref, score_ref, total_ref, mass_ref = refs
    row_max = attend(pieces, panel_mask, lists_ref, counts_ref, query_ref, score_ref, total_ref, mass_ref, before)
    row_sum = jnp.sum(mass_ref[...], axis=1, keepdims=True)
    value_width = total_ref.shape[1]
    inverse = 1.0 / jnp.where(row_sum > 0.0, row_sum, 1.0)
    packed_ref[0:TILE, :] = (total_ref[...] * inverse).astype(jnp.bfloat16)
    row = lax.broadcasted_iota(jnp.int32, (EXTRA, LANES), 0)
    packed = jnp.zeros((EXTRA, LANES), jnp.float32)
    for first, column in ((0, row_max), (3, row_sum)):
        turned = jnp.transpose(jnp.broadcast_to(column, (TILE, LANES)))[0:EXTRA]
        for at, part in enumerate(split_three(turned)):
            packed = jnp.where(row == first + at, part.astype(jnp.float32), packed)
    packed_ref[TILE:, 0:LANES] = packed.astype(jnp.bfloat16)
    packed_ref[TILE:, LANES:] = jnp.zeros((EXTRA, value_width - LANES), jnp.bfloat16)


def home_kernel(layout, lists_ref, counts_ref, query_ref, *refs):
    pieces, refs = read_pieces(layout, query_ref.shape[1], refs)
    total_ref, stats_ref, score_ref, mass_ref = refs
    row_max = attend(pieces, 0, lists_ref, counts_ref, query_ref, score_ref, total_ref, mass_ref)
    row_sum = jnp.sum(mass_ref[...], axis=1, keepdims=True)
    stats_ref[0] = jnp.broadcast_to(row_max, (TILE, LANES))
    stats_ref[1] = jnp.broadcast_to(row_sum, (TILE, LANES))


def merge_kernel(total_ref, stats_ref, *refs):
    packed_refs, out_ref = refs[:-1], refs[-1]
    maxima = [stats_ref[0]]
    sums = [stats_ref[1]]
    for packed_ref in packed_refs:
        packed = packed_ref[TILE:, 0:LANES].astype(jnp.float32)
        for first, kept in ((0, maxima), (3, sums)):
            line = packed[first : first + 1] + packed[first + 1 : first + 2] + packed[first + 2 : first + 3]
            kept.append(jnp.transpose(jnp.broadcast_to(line, (TILE, LANES))))
    top = functools.reduce(jnp.maximum, maxima)
    factors = [jnp.exp(row_max - top) for row_max in maxima]
    masses = [factor * row_sum for factor, row_sum in zip(factors, sums)]
    inverse = 1.0 / functools.reduce(jnp.add, masses)
    scales = [factors[0] * inverse] + [mass * inverse for mass in masses[1:]]
    for at in range(0, total_ref.shape[1], LANES):
        merged = total_ref[:, at : at + LANES] * scales[0]
        for packed_ref, scale in zip(packed_refs, scales[1:]):
            merged = merged + packed_ref[0:TILE, at : at + LANES].astype(jnp.float32) * scale
        out_ref[:, at : at + LANES] = merged.astype(jnp.bfloat16)


def both_cores(pieces, arrivals=()):
    places, arrays = [], []
    for (lib_mask, qry_mask), *pair in pieces:
        sent = tie(*pair, *arrivals)[:2]
        places += [("pair", (lib_mask, qry_mask)), ("pair", (lib_mask | 1, qry_mask))]
        arrays += pair + [swap(array, "lib", 1) for array in sent]
    return places, arrays


def gather_library(keys, partner_keys, values, queries, masks):
    steps = [("qry", 1)]
    mask = lax.axis_size("lib") // 2
    while mask > 1:
        steps.append(("lib", mask))
        mask //= 2
    own_places = [("pair", (0, 0)), ("pair", (1, 0))]
    own_arrays = [keys, values, partner_keys, swap(values, "lib", 1)]
    nearer, _ = tie(queries, values)
    inner = [swap_some(nearer, "qry", mask, True) for mask in masks]
    early, late = [], []
    for axis, mask in steps:
        place = (0, mask) if axis == "qry" else (mask, 0)
        near = (place, swap(keys, axis, mask), swap(values, axis, mask))
        relayed = []
        for (lib_mask, qry_mask), far_keys, far_values in early + late:
            far_keys, _ = tie(far_keys, near[1])
            far_values, *_ = tie(far_values, near[2], *inner)
            place = (lib_mask | mask, qry_mask)
            relayed.append((place, swap(far_keys, axis, mask), swap(far_values, axis, mask)))
        early, late = early + late + [near], relayed
    farther, *_ = tie(queries, *early[0][1:])
    outer = [swap_some(farther, "qry", mask, False) for mask in masks]
    early_places, early_arrays = both_cores(early)
    late_places, late_arrays = both_cores(late, outer)
    early = (own_places + early_places, own_arrays + early_arrays)
    return early, (late_places, late_arrays), list(zip(masks, inner, outer))


def body(queries, library_keys, library_values, key_scale, block_list, block_count):
    qry_count = lax.axis_size("qry")
    width = library_keys.shape[1]
    value_width = library_values.shape[1]

    partner_keys = swap(library_keys, "lib", 1)
    own_values, _ = tie(library_values, partner_keys)
    values = pl.pallas_call(
        pack_kernel,
        out_shape=jax.ShapeDtypeStruct((TILE + EXTRA, value_width), jnp.bfloat16),
        in_specs=[pl.BlockSpec(memory_space=pl.ANY)] * 2,
        out_specs=VMEM,
        scratch_shapes=[pltpu.VMEM((1, TILE), jnp.bfloat16), pltpu.SemaphoreType.DMA((2,))],
        compiler_params=params(),
    )(own_values, key_scale.reshape(1, TILE))

    masks = [2 * at + 1 for at in range(1, qry_count // 2)]
    (early_places, early_arrays), (late_places, late_arrays), visitors = gather_library(
        library_keys, partner_keys, values, queries, masks
    )
    piece_rows = (width // value_width + 1) * TILE + EXTRA
    count_early, count_late = len(early_places), len(late_places)

    cost = pl.CostEstimate(flops=2 * TILE * 4 * TILE * width * 2, bytes_accessed=4 * 1024 * 1024, transcendentals=0)
    total_shape = jax.ShapeDtypeStruct((TILE, value_width), jnp.float32)
    line_shape = jax.ShapeDtypeStruct((TILE, LANES), jnp.float32)
    attend_params = params((count_early + count_late) * piece_rows * value_width * 2)
    returned = []
    for mask, inner_queries, outer_queries in visitors:
        *state, = pl.pallas_call(
            functools.partial(early_kernel, early_places, mask),
            out_shape=(jax.ShapeDtypeStruct(queries.shape, queries.dtype), total_shape, line_shape, line_shape),
            in_specs=[SMEM, SMEM] + [VMEM] * (2 + len(early_arrays)),
            out_specs=(VMEM,) * 4,
            scratch_shapes=[pltpu.VMEM((count_early, TILE, TILE), jnp.float32)],
            compiler_params=attend_params,
            cost_estimate=cost,
        )(
            block_list,
            block_count,
            inner_queries,
            outer_queries,
            *early_arrays,
        )
        packed = pl.pallas_call(
            functools.partial(late_kernel, late_places, mask),
            out_shape=jax.ShapeDtypeStruct((TILE + EXTRA, value_width), jnp.bfloat16),
            in_specs=[SMEM, SMEM] + [VMEM] * (4 + len(late_arrays)),
            out_specs=VMEM,
            scratch_shapes=[
                pltpu.VMEM((count_late, TILE, TILE), jnp.float32),
                pltpu.VMEM((TILE, value_width), jnp.float32),
                pltpu.VMEM((TILE, TILE), jnp.float32),
            ],
            compiler_params=attend_params,
            cost_estimate=cost,
        )(block_list, block_count, *state, *late_arrays)
        returned.append(swap(packed, "qry", mask))

    total, stats = pl.pallas_call(
        functools.partial(home_kernel, early_places + late_places),
        out_shape=(total_shape, jax.ShapeDtypeStruct((2, TILE, LANES), jnp.float32)),
        in_specs=[SMEM, SMEM] + [VMEM] * (1 + len(early_arrays) + len(late_arrays)),
        out_specs=(VMEM, VMEM),
        scratch_shapes=[
            pltpu.VMEM((count_early + count_late, TILE, TILE), jnp.float32),
            pltpu.VMEM((TILE, TILE), jnp.float32),
        ],
        compiler_params=attend_params,
        cost_estimate=cost,
    )(block_list, block_count, queries, *early_arrays, *late_arrays)

    return pl.pallas_call(
        merge_kernel,
        out_shape=jax.ShapeDtypeStruct((TILE, value_width), jnp.bfloat16),
        in_specs=[VMEM] * (2 + len(returned)),
        out_specs=VMEM,
        compiler_params=params(),
    )(total, stats, *returned)


def solution(mesh):
    in_specs = (
        P(("groups", "lib", "qry"), None),
        P(("groups", "lib", "qry"), None),
        P(("groups", "lib", "qry"), None),
        P(("groups", "lib", "qry")),
        P("groups", None),
        P("groups"),
    )
    out_specs = P(("groups", "lib", "qry"), None)
    return jax.shard_map(body, mesh=mesh, in_specs=in_specs, out_specs=out_specs, check_vma=False)
```

```python
import functools
import math

import jax
import jax.numpy as jnp
from jax import lax
from jax.experimental import pallas as pl
from jax.experimental.pallas import tpu as pltpu
from jax.sharding import PartitionSpec as P

TILE = 128
LANES = 128
EXTRA = 16
MASKED_SCORE = -1e30
SMEM = pl.BlockSpec(memory_space=pltpu.SMEM)
VMEM = pl.BlockSpec(memory_space=pltpu.VMEM)


def params(operand_bytes=0):
    return pltpu.CompilerParams(vmem_limit_bytes=operand_bytes * 3 // 2 + 6 * 1024 * 1024)


def swap(value, axis, mask):
    length = lax.axis_size(axis)
    return lax.ppermute(value, axis, [(i, i ^ mask) for i in range(length)])


def visits(qry_count, turn, near):
    pairs = []
    for pair in range(qry_count // 2):
        other = pair ^ turn
        right = int(other > pair)
        pairs.append((2 * pair + (right if near else 1 - right), 2 * other + 1 - right))
    return pairs


def send_visitors(queries, turn, near):
    return lax.ppermute(queries, "qry", visits(lax.axis_size("qry"), turn, near))


def send_back(partial, turn, near):
    return lax.ppermute(partial, "qry", [(host, guest) for guest, host in visits(lax.axis_size("qry"), turn, near)])


def turn_roles(turn):
    index = lax.axis_index("qry")
    pair = index // 2
    other = lax.bitwise_xor(pair, turn)
    right = (other > pair).astype(jnp.int32)
    return index == 2 * pair + right, 2 * other + 1 - right, 2 * other + right


def tie(*values):
    return lax.optimization_barrier(values)


def split_three(value):
    high = value.astype(jnp.bfloat16)
    rest = value - high.astype(jnp.float32)
    middle = rest.astype(jnp.bfloat16)
    low = (rest - middle.astype(jnp.float32)).astype(jnp.bfloat16)
    return high, middle, low


def pack_kernel(values_ref, scale_ref, packed_ref, row_ref, sems):
    value_width = values_ref.shape[1]
    copies = (
        pltpu.make_async_copy(values_ref, packed_ref.at[pl.ds(0, TILE)], sems.at[0]),
        pltpu.make_async_copy(scale_ref, row_ref, sems.at[1]),
    )
    for copy in copies:
        copy.start()
    packed_ref[TILE:, TILE:] = jnp.zeros((EXTRA, value_width - TILE), jnp.bfloat16)
    for copy in reversed(copies):
        copy.wait()
    row = row_ref[...].astype(jnp.float32)
    packed_ref[TILE:, 0:TILE] = jnp.broadcast_to(row, (EXTRA, TILE)).astype(jnp.bfloat16)


def bundle_kernel(*refs):
    bundle_ref, at = refs[-1], 0
    width = bundle_ref.shape[1]
    for ref in refs[:-1]:
        rows = ref.shape[0]
        for column in range(0, ref.shape[1], width):
            bundle_ref[at : at + rows, :] = ref[:, column : column + width]
            at += rows


class Piece:
    def __init__(self, place, keys_ref=None, values_ref=None, bundle_ref=None, first_row=0):
        self.place = place
        self.refs = (keys_ref, values_ref, bundle_ref)
        self.first_row = first_row

    def scores(self, query_ref, inverse_root):
        keys_ref, values_ref, bundle_ref = self.refs
        width = query_ref.shape[1]
        dims = (((1,), (1,)), ((), ()))
        if bundle_ref is None:
            product = lax.dot_general(query_ref[...], keys_ref[...], dims, preferred_element_type=jnp.float32)
            scale = values_ref[TILE : TILE + EXTRA, 0:TILE]
        else:
            group = bundle_ref.shape[1]
            product = 0.0
            for at in range(width // group):
                rows = pl.ds(self.first_row + at * TILE, TILE)
                product = product + lax.dot_general(
                    query_ref[:, at * group : (at + 1) * group],
                    bundle_ref[rows, :],
                    dims,
                    preferred_element_type=jnp.float32,
                )
            scale = bundle_ref[pl.ds(self.first_row + width // group * TILE + TILE, EXTRA), 0:TILE]
        return product * (scale.astype(jnp.float32)[0:1] * inverse_root)

    def values(self, width):
        keys_ref, values_ref, bundle_ref = self.refs
        if bundle_ref is None:
            return values_ref[0:TILE, :]
        return bundle_ref[pl.ds(self.first_row + width // bundle_ref.shape[1] * TILE, TILE), :]


def read_pieces(layout, width, refs):
    pieces = []
    for entry in layout:
        if entry[0] == "pair":
            pieces.append(Piece(entry[1], refs[0], refs[1]))
            refs = refs[2:]
        else:
            for at, place in enumerate(entry[1]):
                group = refs[0].shape[1]
                rows = (width // group + 1) * TILE + EXTRA
                pieces.append(Piece(place, bundle_ref=refs[0], first_row=at * rows))
            refs = refs[1:]
    return pieces, refs


def attend(pieces, panel_qry, gate, lists_ref, counts_ref, query_ref, score_ref, total_ref, mass_ref, before=None):
    lib_index = lax.axis_index("lib")
    qry_index = lax.axis_index("qry")
    qry_count = lax.axis_size("qry")
    block_total = lax.axis_size("lib") * qry_count
    panel = lib_index * qry_count + panel_qry
    first = lists_ref[panel, 0]
    count = counts_ref[panel]
    width = query_ref.shape[1]
    inverse_root = 1.0 / math.sqrt(width)

    def active(lib_mask, qry_mask):
        block = lax.bitwise_xor(lib_index, lib_mask) * qry_count + lax.bitwise_xor(qry_index, qry_mask)
        return lax.rem(block - first + block_total, block_total) < count

    flags = [active(*piece.place) for piece in pieces]
    if gate is not None:
        flags = [jnp.logical_and(flag, gate) for flag in flags]
    score_ref[...] = jnp.full(score_ref.shape, MASKED_SCORE, jnp.float32)
    for at, (piece, flag) in enumerate(zip(pieces, flags)):

        @pl.when(flag)
        def _(at=at, piece=piece):
            score_ref[at] = piece.scores(query_ref, inverse_root)

    largest = score_ref[0]
    for at in range(1, len(flags)):
        largest = jnp.maximum(largest, score_ref[at])
    row_max = jnp.max(largest, axis=1, keepdims=True)
    if before is None:
        total_ref[...] = jnp.zeros(total_ref.shape, jnp.float32)
        mass_ref[...] = jnp.zeros(mass_ref.shape, jnp.float32)
    else:
        old_total_ref, old_mass_ref, old_max_ref = before
        old_max = old_max_ref[...]
        new_max = jnp.maximum(old_max, row_max)
        shrink = jnp.exp(old_max - new_max)
        row_max = new_max[:, 0:1]
        mass_ref[...] = old_mass_ref[...] * shrink
        for at in range(0, total_ref.shape[1], LANES):
            total_ref[:, at : at + LANES] = old_total_ref[:, at : at + LANES] * shrink
    for at, (piece, flag) in enumerate(zip(pieces, flags)):

        @pl.when(flag)
        def _(at=at, piece=piece):
            weights = jnp.exp(score_ref[at] - row_max)
            mass_ref[...] += weights
            weight_high = weights.astype(jnp.bfloat16)
            weight_low = (weights - weight_high.astype(jnp.float32)).astype(jnp.bfloat16)
            values = piece.values(width)
            added = jnp.dot(weight_high, values, preferred_element_type=jnp.float32)
            added = added + jnp.dot(weight_low, values, preferred_element_type=jnp.float32)
            total_ref[...] += added

    return row_max


def early_kernel(layout, turn, near, lists_ref, counts_ref, query_ref, *refs):
    pieces, refs = read_pieces(layout, query_ref.shape[1], refs)
    total_ref, mass_ref, max_ref, score_ref = refs
    host, *guests = turn_roles(turn)
    guest = guests[0] if near else guests[1]
    row_max = attend(pieces, guest, host, lists_ref, counts_ref, query_ref, score_ref, total_ref, mass_ref)
    max_ref[...] = jnp.broadcast_to(row_max, max_ref.shape)


def late_kernel(layout, turn, near, lists_ref, counts_ref, query_ref, *refs):
    before, refs = refs[:3], refs[3:]
    pieces, refs = read_pieces(layout, query_ref.shape[1], refs)
    packed_ref, score_ref, total_ref, mass_ref = refs
    host, *guests = turn_roles(turn)
    guest = guests[0] if near else guests[1]
    row_max = attend(pieces, guest, host, lists_ref, counts_ref, query_ref, score_ref, total_ref, mass_ref, before)
    row_sum = jnp.sum(mass_ref[...], axis=1, keepdims=True)
    value_width = total_ref.shape[1]
    inverse = 1.0 / jnp.where(row_sum > 0.0, row_sum, 1.0)
    packed_ref[0:TILE, :] = (total_ref[...] * inverse).astype(jnp.bfloat16)
    row = lax.broadcasted_iota(jnp.int32, (EXTRA, LANES), 0)
    packed = jnp.zeros((EXTRA, LANES), jnp.float32)
    for first, column in ((0, row_max), (3, row_sum)):
        turned = jnp.transpose(jnp.broadcast_to(column, (TILE, LANES)))[0:EXTRA]
        for at, part in enumerate(split_three(turned)):
            packed = jnp.where(row == first + at, part.astype(jnp.float32), packed)
    packed_ref[TILE:, 0:LANES] = packed.astype(jnp.bfloat16)
    packed_ref[TILE:, LANES:] = jnp.zeros((EXTRA, value_width - LANES), jnp.bfloat16)


def home_kernel(layout, lists_ref, counts_ref, query_ref, *refs):
    pieces, refs = read_pieces(layout, query_ref.shape[1], refs)
    total_ref, stats_ref, score_ref, mass_ref = refs
    own = lax.axis_index("qry")
    row_max = attend(pieces, own, None, lists_ref, counts_ref, query_ref, score_ref, total_ref, mass_ref)
    row_sum = jnp.sum(mass_ref[...], axis=1, keepdims=True)
    stats_ref[0] = jnp.broadcast_to(row_max, (TILE, LANES))
    stats_ref[1] = jnp.broadcast_to(row_sum, (TILE, LANES))


def merge_kernel(total_ref, stats_ref, *refs):
    *packed_refs, out_ref, picked_ref = refs
    for turn in range(len(packed_refs) // 2):
        near, *_ = turn_roles(turn + 1)
        for flag, packed_ref in ((near, packed_refs[2 * turn]), (jnp.logical_not(near), packed_refs[2 * turn + 1])):

            @pl.when(flag)
            def _(turn=turn, packed_ref=packed_ref):
                picked_ref[turn] = packed_ref[...]

    packed_refs = [picked_ref.at[turn] for turn in range(len(packed_refs) // 2)]
    maxima = [stats_ref[0]]
    sums = [stats_ref[1]]
    for packed_ref in packed_refs:
        packed = packed_ref[TILE:, 0:LANES].astype(jnp.float32)
        for first, kept in ((0, maxima), (3, sums)):
            line = packed[first : first + 1] + packed[first + 1 : first + 2] + packed[first + 2 : first + 3]
            kept.append(jnp.transpose(jnp.broadcast_to(line, (TILE, LANES))))
    top = functools.reduce(jnp.maximum, maxima)
    factors = [jnp.exp(row_max - top) for row_max in maxima]
    masses = [factor * row_sum for factor, row_sum in zip(factors, sums)]
    inverse = 1.0 / functools.reduce(jnp.add, masses)
    scales = [factors[0] * inverse] + [mass * inverse for mass in masses[1:]]
    for at in range(0, total_ref.shape[1], LANES):
        merged = total_ref[:, at : at + LANES] * scales[0]
        for packed_ref, scale in zip(packed_refs, scales[1:]):
            merged = merged + packed_ref[0:TILE, at : at + LANES].astype(jnp.float32) * scale
        out_ref[:, at : at + LANES] = merged.astype(jnp.bfloat16)


def both_cores(pieces, arrivals=()):
    places, arrays = [], []
    for (lib_mask, qry_mask), *pair in pieces:
        sent = tie(*pair, *arrivals)[:2]
        places += [("pair", (lib_mask, qry_mask)), ("pair", (lib_mask | 1, qry_mask))]
        arrays += pair + [swap(array, "lib", 1) for array in sent]
    return places, arrays


def gather_library(keys, partner_keys, values, queries):
    steps = [("qry", 1)]
    mask = lax.axis_size("lib") // 2
    while mask > 1:
        steps.append(("lib", mask))
        mask //= 2
    turns = range(1, lax.axis_size("qry") // 2)
    own_places = [("pair", (0, 0)), ("pair", (1, 0))]
    own_arrays = [keys, values, partner_keys, swap(values, "lib", 1)]
    early, late = [], []
    for axis, mask in steps:
        place = (0, mask) if axis == "qry" else (mask, 0)
        own = (place, swap(keys, axis, mask), swap(values, axis, mask))
        relayed = []
        for (lib_mask, qry_mask), far_keys, far_values in early + late:
            far_keys, far_values, *_ = tie(far_keys, far_values, *own[1:])
            place = (lib_mask | mask, qry_mask)
            relayed.append((place, swap(far_keys, axis, mask), swap(far_values, axis, mask)))
        early, late = early + late + [own], relayed
    leaving, _ = tie(queries, early[0][1])
    near, far = ([send_visitors(leaving, turn, at) for turn in turns] for at in (True, False))
    early_places, early_arrays = both_cores(early)
    early_places, early_arrays = own_places + early_places, own_arrays + early_arrays
    late_places, late_arrays = both_cores(late, far + near)
    return (early_places, early_arrays), (late_places, late_arrays), list(zip(turns, near, far))


def body(queries, library_keys, library_values, key_scale, block_list, block_count):
    qry_count = lax.axis_size("qry")
    width = library_keys.shape[1]
    value_width = library_values.shape[1]

    partner_keys = swap(library_keys, "lib", 1)
    own_values, _ = tie(library_values, partner_keys)
    values = pl.pallas_call(
        pack_kernel,
        out_shape=jax.ShapeDtypeStruct((TILE + EXTRA, value_width), jnp.bfloat16),
        in_specs=[pl.BlockSpec(memory_space=pl.ANY)] * 2,
        out_specs=VMEM,
        scratch_shapes=[pltpu.VMEM((1, TILE), jnp.bfloat16), pltpu.SemaphoreType.DMA((2,))],
        compiler_params=params(),
    )(own_values, key_scale.reshape(1, TILE))

    (early_places, early_arrays), (late_places, late_arrays), visitors = gather_library(
        library_keys, partner_keys, values, queries
    )
    piece_rows = (width // value_width + 1) * TILE + EXTRA
    count_early, count_late = len(early_places), len(late_places)

    cost = pl.CostEstimate(flops=2 * TILE * 4 * TILE * width * 2, bytes_accessed=4 * 1024 * 1024, transcendentals=0)
    total_shape = jax.ShapeDtypeStruct((TILE, value_width), jnp.float32)
    line_shape = jax.ShapeDtypeStruct((TILE, LANES), jnp.float32)
    attend_params = params((count_early + count_late) * piece_rows * value_width * 2)
    returned = []
    for turn, near_queries, far_queries in visitors:
        packed = []
        for near, visiting in ((False, far_queries), (True, near_queries)):
            state = pl.pallas_call(
                functools.partial(early_kernel, early_places, turn, near),
                out_shape=(total_shape, line_shape, line_shape),
                in_specs=[SMEM, SMEM] + [VMEM] * (1 + len(early_arrays)),
                out_specs=(VMEM,) * 3,
                scratch_shapes=[pltpu.VMEM((count_early, TILE, TILE), jnp.float32)],
                compiler_params=attend_params,
                cost_estimate=cost,
            )(block_list, block_count, visiting, *early_arrays)
            partial = pl.pallas_call(
                functools.partial(late_kernel, late_places, turn, near),
                out_shape=jax.ShapeDtypeStruct((TILE + EXTRA, value_width), jnp.bfloat16),
                in_specs=[SMEM, SMEM] + [VMEM] * (4 + len(late_arrays)),
                out_specs=VMEM,
                scratch_shapes=[
                    pltpu.VMEM((count_late, TILE, TILE), jnp.float32),
                    pltpu.VMEM((TILE, value_width), jnp.float32),
                    pltpu.VMEM((TILE, TILE), jnp.float32),
                ],
                compiler_params=attend_params,
                cost_estimate=cost,
            )(block_list, block_count, visiting, *state, *late_arrays)
            packed.append(send_back(partial, turn, near))
        returned += packed[::-1]

    total, stats = pl.pallas_call(
        functools.partial(home_kernel, early_places + late_places),
        out_shape=(total_shape, jax.ShapeDtypeStruct((2, TILE, LANES), jnp.float32)),
        in_specs=[SMEM, SMEM] + [VMEM] * (1 + len(early_arrays) + len(late_arrays)),
        out_specs=(VMEM, VMEM),
        scratch_shapes=[
            pltpu.VMEM((count_early + count_late, TILE, TILE), jnp.float32),
            pltpu.VMEM((TILE, TILE), jnp.float32),
        ],
        compiler_params=attend_params,
        cost_estimate=cost,
    )(block_list, block_count, queries, *early_arrays, *late_arrays)

    return pl.pallas_call(
        merge_kernel,
        out_shape=jax.ShapeDtypeStruct((TILE, value_width), jnp.bfloat16),
        in_specs=[VMEM] * (2 + len(returned)),
        out_specs=VMEM,
        scratch_shapes=[pltpu.VMEM((len(returned) // 2, TILE + EXTRA, value_width), jnp.bfloat16)],
        compiler_params=params(),
    )(total, stats, *returned)


def solution(mesh):
    in_specs = (
        P(("groups", "lib", "qry"), None),
        P(("groups", "lib", "qry"), None),
        P(("groups", "lib", "qry"), None),
        P(("groups", "lib", "qry")),
        P("groups", None),
        P("groups"),
    )
    out_specs = P(("groups", "lib", "qry"), None)
    return jax.shard_map(body, mesh=mesh, in_specs=in_specs, out_specs=out_specs, check_vma=False)
```

```python
import functools
import math

import jax
import jax.numpy as jnp
from jax import lax
from jax.experimental import pallas as pl
from jax.experimental.pallas import tpu as pltpu
from jax.sharding import PartitionSpec as P

TILE = 128
LANES = 128
EXTRA = 16
MASKED_SCORE = -1e30
SMEM = pl.BlockSpec(memory_space=pltpu.SMEM)
VMEM = pl.BlockSpec(memory_space=pltpu.VMEM)


def params(operand_bytes=0):
    return pltpu.CompilerParams(vmem_limit_bytes=operand_bytes * 3 // 2 + 6 * 1024 * 1024)


def swap(value, axis, mask):
    length = lax.axis_size(axis)
    return lax.ppermute(value, axis, [(i, i ^ mask) for i in range(length)])


def tie(*values):
    return lax.optimization_barrier(values)


def split_three(value):
    high = value.astype(jnp.bfloat16)
    rest = value - high.astype(jnp.float32)
    middle = rest.astype(jnp.bfloat16)
    low = (rest - middle.astype(jnp.float32)).astype(jnp.bfloat16)
    return high, middle, low


def pack_kernel(values_ref, scale_ref, packed_ref, row_ref, sems):
    value_width = values_ref.shape[1]
    copies = (
        pltpu.make_async_copy(values_ref, packed_ref.at[pl.ds(0, TILE)], sems.at[0]),
        pltpu.make_async_copy(scale_ref, row_ref, sems.at[1]),
    )
    for copy in copies:
        copy.start()
    packed_ref[TILE:, TILE:] = jnp.zeros((EXTRA, value_width - TILE), jnp.bfloat16)
    for copy in reversed(copies):
        copy.wait()
    row = row_ref[...].astype(jnp.float32)
    packed_ref[TILE:, 0:TILE] = jnp.broadcast_to(row, (EXTRA, TILE)).astype(jnp.bfloat16)


class Piece:
    def __init__(self, place, keys_ref, values_ref, copy=None):
        self.place = place
        self.refs = (keys_ref, values_ref)
        self.copy = copy

    def scores(self, query_ref, inverse_root):
        keys_ref, values_ref = self.refs
        product = lax.dot_general(
            query_ref[...], keys_ref[...], (((1,), (1,)), ((), ())), preferred_element_type=jnp.float32
        )
        scale = values_ref[TILE : TILE + EXTRA, 0:TILE]
        return product * (scale.astype(jnp.float32)[0:1] * inverse_root)

    def values(self):
        return self.refs[1][0:TILE, :]


def read_pieces(places, refs, own=None):
    pieces = [Piece(place, refs[2 * at], refs[2 * at + 1]) for at, place in enumerate(places)]
    refs = refs[2 * len(places) :]
    if own is not None:
        keys_ref, values_ref, *refs, held_ref, sem = refs
        copy = pltpu.make_async_copy(keys_ref, held_ref, sem)
        copy.start()
        pieces.append(Piece((0, 0), held_ref, values_ref, copy))
    return pieces, refs


def attend(pieces, panel_mask, lists_ref, counts_ref, query_ref, score_ref, total_ref, mass_ref, before=None):
    lib_index = lax.axis_index("lib")
    qry_index = lax.axis_index("qry")
    qry_count = lax.axis_size("qry")
    block_total = lax.axis_size("lib") * qry_count
    panel = lib_index * qry_count + lax.bitwise_xor(qry_index, panel_mask)
    first = lists_ref[panel, 0]
    count = counts_ref[panel]
    width = query_ref.shape[1]
    inverse_root = 1.0 / math.sqrt(width)

    def active(lib_mask, qry_mask):
        block = lax.bitwise_xor(lib_index, lib_mask) * qry_count + lax.bitwise_xor(qry_index, qry_mask)
        return lax.rem(block - first + block_total, block_total) < count

    flags = [active(*piece.place) for piece in pieces]
    score_ref[...] = jnp.full(score_ref.shape, MASKED_SCORE, jnp.float32)
    for at, (piece, flag) in enumerate(zip(pieces, flags)):
        if piece.copy is not None:
            piece.copy.wait()

        @pl.when(flag)
        def _(at=at, piece=piece):
            score_ref[at] = piece.scores(query_ref, inverse_root)

    largest = score_ref[0]
    for at in range(1, len(flags)):
        largest = jnp.maximum(largest, score_ref[at])
    row_max = jnp.max(largest, axis=1, keepdims=True)
    if before is None:
        total_ref[...] = jnp.zeros(total_ref.shape, jnp.float32)
        mass_ref[...] = jnp.zeros(mass_ref.shape, jnp.float32)
    else:
        old_total_ref, old_mass_ref, old_max_ref = before
        old_max = old_max_ref[...]
        new_max = jnp.maximum(old_max, row_max)
        shrink = jnp.exp(old_max - new_max)
        row_max = new_max[:, 0:1]
        mass_ref[...] = old_mass_ref[...] * shrink
        for at in range(0, total_ref.shape[1], LANES):
            total_ref[:, at : at + LANES] = old_total_ref[:, at : at + LANES] * shrink
    for at, (piece, flag) in enumerate(zip(pieces, flags)):

        @pl.when(flag)
        def _(at=at, piece=piece):
            weights = jnp.exp(score_ref[at] - row_max)
            mass_ref[...] += weights
            weight_high = weights.astype(jnp.bfloat16)
            weight_low = (weights - weight_high.astype(jnp.float32)).astype(jnp.bfloat16)
            values = piece.values()
            added = jnp.dot(weight_high, values, preferred_element_type=jnp.float32)
            added = added + jnp.dot(weight_low, values, preferred_element_type=jnp.float32)
            total_ref[...] += added

    return row_max


def early_kernel(places, panel_mask, lists_ref, counts_ref, query_ref, *refs):
    pieces, refs = read_pieces(places, refs, own=True)
    total_ref, mass_ref, max_ref, score_ref = refs
    row_max = attend(pieces, panel_mask, lists_ref, counts_ref, query_ref, score_ref, total_ref, mass_ref)
    max_ref[...] = jnp.broadcast_to(row_max, max_ref.shape)


def late_kernel(places, panel_mask, lists_ref, counts_ref, query_ref, *refs):
    before, refs = refs[:3], refs[3:]
    pieces, refs = read_pieces(places, refs)
    packed_ref, score_ref, total_ref, mass_ref = refs
    row_max = attend(pieces, panel_mask, lists_ref, counts_ref, query_ref, score_ref, total_ref, mass_ref, before)
    row_sum = jnp.sum(mass_ref[...], axis=1, keepdims=True)
    value_width = total_ref.shape[1]
    inverse = 1.0 / jnp.where(row_sum > 0.0, row_sum, 1.0)
    packed_ref[0:TILE, :] = (total_ref[...] * inverse).astype(jnp.bfloat16)
    row = lax.broadcasted_iota(jnp.int32, (EXTRA, LANES), 0)
    packed = jnp.zeros((EXTRA, LANES), jnp.float32)
    for first, column in ((0, row_max), (3, row_sum)):
        turned = jnp.transpose(jnp.broadcast_to(column, (TILE, LANES)))[0:EXTRA]
        for at, part in enumerate(split_three(turned)):
            packed = jnp.where(row == first + at, part.astype(jnp.float32), packed)
    packed_ref[TILE:, 0:LANES] = packed.astype(jnp.bfloat16)
    packed_ref[TILE:, LANES:] = jnp.zeros((EXTRA, value_width - LANES), jnp.bfloat16)


def home_kernel(places, lists_ref, counts_ref, query_ref, *refs):
    pieces, refs = read_pieces(places, refs, own=True)
    total_ref, stats_ref, score_ref, mass_ref = refs
    row_max = attend(pieces, 0, lists_ref, counts_ref, query_ref, score_ref, total_ref, mass_ref)
    row_sum = jnp.sum(mass_ref[...], axis=1, keepdims=True)
    stats_ref[0] = jnp.broadcast_to(row_max, (TILE, LANES))
    stats_ref[1] = jnp.broadcast_to(row_sum, (TILE, LANES))


def merge_kernel(total_ref, stats_ref, *refs):
    packed_refs, out_ref = refs[:-1], refs[-1]
    maxima = [stats_ref[0]]
    sums = [stats_ref[1]]
    for packed_ref in packed_refs:
        packed = packed_ref[TILE:, 0:LANES].astype(jnp.float32)
        for first, kept in ((0, maxima), (3, sums)):
            line = packed[first : first + 1] + packed[first + 1 : first + 2] + packed[first + 2 : first + 3]
            kept.append(jnp.transpose(jnp.broadcast_to(line, (TILE, LANES))))
    top = functools.reduce(jnp.maximum, maxima)
    factors = [jnp.exp(row_max - top) for row_max in maxima]
    masses = [factor * row_sum for factor, row_sum in zip(factors, sums)]
    inverse = 1.0 / functools.reduce(jnp.add, masses)
    scales = [factors[0] * inverse] + [mass * inverse for mass in masses[1:]]
    for at in range(0, total_ref.shape[1], LANES):
        merged = total_ref[:, at : at + LANES] * scales[0]
        for packed_ref, scale in zip(packed_refs, scales[1:]):
            merged = merged + packed_ref[0:TILE, at : at + LANES].astype(jnp.float32) * scale
        out_ref[:, at : at + LANES] = merged.astype(jnp.bfloat16)


def both_cores(pieces, arrivals=()):
    places, arrays = [], []
    for (lib_mask, qry_mask), *pair in pieces:
        sent = tie(*pair, *arrivals)[:2]
        places += [(lib_mask, qry_mask), (lib_mask | 1, qry_mask)]
        arrays += pair + [swap(array, "lib", 1) for array in sent]
    return places, arrays


def gather_library(keys, partner_keys, values, queries, masks):
    steps = [("qry", 1)]
    mask = lax.axis_size("lib") // 2
    while mask > 1:
        steps.append(("lib", mask))
        mask //= 2
    own_places = [(1, 0)]
    own_arrays = [partner_keys, swap(values, "lib", 1)]
    leaving, _ = tie(queries, values)
    visitors = [swap(leaving, "qry", mask) for mask in masks]
    early, late = [], []
    for axis, mask in steps:
        place = (0, mask) if axis == "qry" else (mask, 0)
        near = (place, swap(keys, axis, mask), swap(values, axis, mask))
        relayed = []
        for (lib_mask, qry_mask), far_keys, far_values in early + late:
            far_keys, far_values, *_ = tie(far_keys, far_values, *near[1:])
            place = (lib_mask | mask, qry_mask)
            relayed.append((place, swap(far_keys, axis, mask), swap(far_values, axis, mask)))
        early, late = early + late + [near], relayed
    early_places, early_arrays = both_cores(early)
    late_places, late_arrays = both_cores(late, visitors)
    early = (own_places + early_places, own_arrays + early_arrays)
    return early, (late_places, late_arrays), list(zip(masks, visitors))


def body(queries, library_keys, library_values, key_scale, block_list, block_count):
    qry_count = lax.axis_size("qry")
    width = library_keys.shape[1]
    value_width = library_values.shape[1]

    partner_keys = swap(library_keys, "lib", 1)
    own_values, _ = tie(library_values, partner_keys)
    values = pl.pallas_call(
        pack_kernel,
        out_shape=jax.ShapeDtypeStruct((TILE + EXTRA, value_width), jnp.bfloat16),
        in_specs=[pl.BlockSpec(memory_space=pl.ANY)] * 2,
        out_specs=VMEM,
        scratch_shapes=[pltpu.VMEM((1, TILE), jnp.bfloat16), pltpu.SemaphoreType.DMA((2,))],
        compiler_params=params(),
    )(own_values, key_scale.reshape(1, TILE))

    masks = [2 * at + 1 for at in range(1, qry_count // 2)]
    (early_places, early_arrays), (late_places, late_arrays), visitors = gather_library(
        library_keys, partner_keys, values, queries, masks
    )
    piece_rows = (width // value_width + 1) * TILE + EXTRA
    count_early, count_late = len(early_places) + 1, len(late_places)

    cost = pl.CostEstimate(flops=2 * TILE * 4 * TILE * width * 2, bytes_accessed=4 * 1024 * 1024, transcendentals=0)
    total_shape = jax.ShapeDtypeStruct((TILE, value_width), jnp.float32)
    line_shape = jax.ShapeDtypeStruct((TILE, LANES), jnp.float32)
    attend_params = params((count_early + count_late) * piece_rows * value_width * 2)
    own_specs = [pl.BlockSpec(memory_space=pl.ANY), VMEM]
    own_scratch = [pltpu.VMEM(library_keys.shape, library_keys.dtype), pltpu.SemaphoreType.DMA]
    returned = []
    for mask, visiting in visitors:
        *state, = pl.pallas_call(
            functools.partial(early_kernel, early_places, mask),
            out_shape=(total_shape, line_shape, line_shape),
            in_specs=[SMEM, SMEM] + [VMEM] * (1 + len(early_arrays)) + own_specs,
            out_specs=(VMEM,) * 3,
            scratch_shapes=[pltpu.VMEM((count_early, TILE, TILE), jnp.float32)] + own_scratch,
            compiler_params=attend_params,
            cost_estimate=cost,
        )(block_list, block_count, visiting, *early_arrays, library_keys, values)
        packed = pl.pallas_call(
            functools.partial(late_kernel, late_places, mask),
            out_shape=jax.ShapeDtypeStruct((TILE + EXTRA, value_width), jnp.bfloat16),
            in_specs=[SMEM, SMEM] + [VMEM] * (4 + len(late_arrays)),
            out_specs=VMEM,
            scratch_shapes=[
                pltpu.VMEM((count_late, TILE, TILE), jnp.float32),
                pltpu.VMEM((TILE, value_width), jnp.float32),
                pltpu.VMEM((TILE, TILE), jnp.float32),
            ],
            compiler_params=attend_params,
            cost_estimate=cost,
        )(block_list, block_count, visiting, *state, *late_arrays)
        returned.append(swap(packed, "qry", mask))

    total, stats = pl.pallas_call(
        functools.partial(home_kernel, early_places + late_places),
        out_shape=(total_shape, jax.ShapeDtypeStruct((2, TILE, LANES), jnp.float32)),
        in_specs=[SMEM, SMEM] + [VMEM] * (1 + len(early_arrays) + len(late_arrays)) + own_specs,
        out_specs=(VMEM, VMEM),
        scratch_shapes=[
            pltpu.VMEM((count_early + count_late, TILE, TILE), jnp.float32),
            pltpu.VMEM((TILE, TILE), jnp.float32),
        ]
        + own_scratch,
        compiler_params=attend_params,
        cost_estimate=cost,
    )(block_list, block_count, queries, *early_arrays, *late_arrays, library_keys, values)

    return pl.pallas_call(
        merge_kernel,
        out_shape=jax.ShapeDtypeStruct((TILE, value_width), jnp.bfloat16),
        in_specs=[VMEM] * (2 + len(returned)),
        out_specs=VMEM,
        compiler_params=params(),
    )(total, stats, *returned)


def solution(mesh):
    in_specs = (
        P(("groups", "lib", "qry"), None),
        P(("groups", "lib", "qry"), None),
        P(("groups", "lib", "qry"), None),
        P(("groups", "lib", "qry")),
        P("groups", None),
        P("groups"),
    )
    out_specs = P(("groups", "lib", "qry"), None)
    return jax.shard_map(body, mesh=mesh, in_specs=in_specs, out_specs=out_specs, check_vma=False)
```

```python
import functools
import math

import jax
import jax.numpy as jnp
from jax import lax
from jax.experimental import pallas as pl
from jax.experimental.pallas import tpu as pltpu
from jax.sharding import PartitionSpec as P

TILE = 128
LANES = 128
EXTRA = 16
MASKED_SCORE = -1e30
SMEM = pl.BlockSpec(memory_space=pltpu.SMEM)
VMEM = pl.BlockSpec(memory_space=pltpu.VMEM)


def params(operand_bytes=0):
    return pltpu.CompilerParams(vmem_limit_bytes=operand_bytes * 3 // 2 + 6 * 1024 * 1024)


def swap(value, axis, mask):
    length = lax.axis_size(axis)
    return lax.ppermute(value, axis, [(i, i ^ mask) for i in range(length)])


def tie(*values):
    return lax.optimization_barrier(values)


def split_three(value):
    high = value.astype(jnp.bfloat16)
    rest = value - high.astype(jnp.float32)
    middle = rest.astype(jnp.bfloat16)
    low = (rest - middle.astype(jnp.float32)).astype(jnp.bfloat16)
    return high, middle, low


def pack_kernel(values_ref, scale_ref, packed_ref, row_ref, sems):
    value_width = values_ref.shape[1]
    copies = (
        pltpu.make_async_copy(values_ref, packed_ref.at[pl.ds(0, TILE)], sems.at[0]),
        pltpu.make_async_copy(scale_ref, row_ref, sems.at[1]),
    )
    for copy in copies:
        copy.start()
    packed_ref[TILE:, TILE:] = jnp.zeros((EXTRA, value_width - TILE), jnp.bfloat16)
    for copy in reversed(copies):
        copy.wait()
    row = row_ref[...].astype(jnp.float32)
    packed_ref[TILE:, 0:TILE] = jnp.broadcast_to(row, (EXTRA, TILE)).astype(jnp.bfloat16)


class Piece:
    def __init__(self, place, keys_ref, values_ref, copy=None):
        self.place = place
        self.refs = (keys_ref, values_ref)
        self.copy = copy

    def scores(self, query_ref, inverse_root):
        keys_ref, values_ref = self.refs
        product = lax.dot_general(
            query_ref[...], keys_ref[...], (((1,), (1,)), ((), ())), preferred_element_type=jnp.float32
        )
        scale = values_ref[TILE : TILE + EXTRA, 0:TILE]
        return product * (scale.astype(jnp.float32)[0:1] * inverse_root)

    def values(self):
        return self.refs[1][0:TILE, :]


def read_pieces(places, refs, own=None):
    pieces = [Piece(place, refs[2 * at], refs[2 * at + 1]) for at, place in enumerate(places)]
    refs = refs[2 * len(places) :]
    if own is not None:
        keys_ref, values_ref, *refs, held_ref, sem = refs
        copy = pltpu.make_async_copy(keys_ref, held_ref, sem)
        copy.start()
        pieces.append(Piece((0, 0), held_ref, values_ref, copy))
    return pieces, refs


def attend(pieces, panel_mask, lists_ref, counts_ref, query_ref, score_ref, total_ref, mass_ref, before=None):
    lib_index = lax.axis_index("lib")
    qry_index = lax.axis_index("qry")
    qry_count = lax.axis_size("qry")
    block_total = lax.axis_size("lib") * qry_count
    panel = lib_index * qry_count + lax.bitwise_xor(qry_index, panel_mask)
    first = lists_ref[panel, 0]
    count = counts_ref[panel]
    width = query_ref.shape[1]
    inverse_root = 1.0 / math.sqrt(width)

    def active(lib_mask, qry_mask):
        block = lax.bitwise_xor(lib_index, lib_mask) * qry_count + lax.bitwise_xor(qry_index, qry_mask)
        return lax.rem(block - first + block_total, block_total) < count

    flags = [active(*piece.place) for piece in pieces]
    score_ref[...] = jnp.full(score_ref.shape, MASKED_SCORE, jnp.float32)
    for at, (piece, flag) in enumerate(zip(pieces, flags)):
        if piece.copy is not None:
            piece.copy.wait()

        @pl.when(flag)
        def _(at=at, piece=piece):
            score_ref[at] = piece.scores(query_ref, inverse_root)

    largest = score_ref[0]
    for at in range(1, len(flags)):
        largest = jnp.maximum(largest, score_ref[at])
    row_max = jnp.max(largest, axis=1, keepdims=True)
    if before is None:
        total_ref[...] = jnp.zeros(total_ref.shape, jnp.float32)
        mass_ref[...] = jnp.zeros(mass_ref.shape, jnp.float32)
    else:
        old_total_ref, old_mass_ref, old_max_ref = before
        old_max = old_max_ref[...]
        new_max = jnp.maximum(old_max, row_max)
        shrink = jnp.exp(old_max - new_max)
        row_max = new_max[:, 0:1]
        mass_ref[...] = old_mass_ref[...] * shrink
        for at in range(0, total_ref.shape[1], LANES):
            total_ref[:, at : at + LANES] = old_total_ref[:, at : at + LANES] * shrink
    for at, (piece, flag) in enumerate(zip(pieces, flags)):

        @pl.when(flag)
        def _(at=at, piece=piece):
            weights = jnp.exp(score_ref[at] - row_max)
            mass_ref[...] += weights
            weight_high = weights.astype(jnp.bfloat16)
            weight_low = (weights - weight_high.astype(jnp.float32)).astype(jnp.bfloat16)
            values = piece.values()
            added = jnp.dot(weight_high, values, preferred_element_type=jnp.float32)
            added = added + jnp.dot(weight_low, values, preferred_element_type=jnp.float32)
            total_ref[...] += added

    return row_max


def early_kernel(places, panel_mask, lists_ref, counts_ref, query_ref, *refs):
    pieces, refs = read_pieces(places, refs, own=True)
    total_ref, mass_ref, max_ref, score_ref = refs
    row_max = attend(pieces, panel_mask, lists_ref, counts_ref, query_ref, score_ref, total_ref, mass_ref)
    max_ref[...] = jnp.broadcast_to(row_max, max_ref.shape)


def late_kernel(places, panel_mask, lists_ref, counts_ref, query_ref, *refs):
    before, refs = refs[:3], refs[3:]
    pieces, refs = read_pieces(places, refs)
    packed_ref, score_ref, total_ref, mass_ref = refs
    row_max = attend(pieces, panel_mask, lists_ref, counts_ref, query_ref, score_ref, total_ref, mass_ref, before)
    row_sum = jnp.sum(mass_ref[...], axis=1, keepdims=True)
    value_width = total_ref.shape[1]
    inverse = 1.0 / jnp.where(row_sum > 0.0, row_sum, 1.0)
    packed_ref[0:TILE, :] = (total_ref[...] * inverse).astype(jnp.bfloat16)
    row = lax.broadcasted_iota(jnp.int32, (EXTRA, LANES), 0)
    packed = jnp.zeros((EXTRA, LANES), jnp.float32)
    for first, column in ((0, row_max), (3, row_sum)):
        turned = jnp.transpose(jnp.broadcast_to(column, (TILE, LANES)))[0:EXTRA]
        for at, part in enumerate(split_three(turned)):
            packed = jnp.where(row == first + at, part.astype(jnp.float32), packed)
    packed_ref[TILE:, 0:LANES] = packed.astype(jnp.bfloat16)
    packed_ref[TILE:, LANES:] = jnp.zeros((EXTRA, value_width - LANES), jnp.bfloat16)


def home_kernel(places, lists_ref, counts_ref, query_ref, *refs):
    pieces, refs = read_pieces(places, refs, own=True)
    total_ref, stats_ref, score_ref, mass_ref = refs
    row_max = attend(pieces, 0, lists_ref, counts_ref, query_ref, score_ref, total_ref, mass_ref)
    row_sum = jnp.sum(mass_ref[...], axis=1, keepdims=True)
    stats_ref[0] = jnp.broadcast_to(row_max, (TILE, LANES))
    stats_ref[1] = jnp.broadcast_to(row_sum, (TILE, LANES))


def merge_kernel(total_ref, stats_ref, *refs):
    packed_refs, out_ref = refs[:-1], refs[-1]
    maxima = [stats_ref[0]]
    sums = [stats_ref[1]]
    for packed_ref in packed_refs:
        packed = packed_ref[TILE:, 0:LANES].astype(jnp.float32)
        for first, kept in ((0, maxima), (3, sums)):
            line = packed[first : first + 1] + packed[first + 1 : first + 2] + packed[first + 2 : first + 3]
            kept.append(jnp.transpose(jnp.broadcast_to(line, (TILE, LANES))))
    top = functools.reduce(jnp.maximum, maxima)
    factors = [jnp.exp(row_max - top) for row_max in maxima]
    masses = [factor * row_sum for factor, row_sum in zip(factors, sums)]
    inverse = 1.0 / functools.reduce(jnp.add, masses)
    scales = [factors[0] * inverse] + [mass * inverse for mass in masses[1:]]
    for at in range(0, total_ref.shape[1], LANES):
        merged = total_ref[:, at : at + LANES] * scales[0]
        for packed_ref, scale in zip(packed_refs, scales[1:]):
            merged = merged + packed_ref[0:TILE, at : at + LANES].astype(jnp.float32) * scale
        out_ref[:, at : at + LANES] = merged.astype(jnp.bfloat16)


def gather_library(keys, values, queries, masks):
    steps = [("qry", 1)]
    mask = lax.axis_size("lib") // 2
    while mask > 1:
        steps.append(("lib", mask))
        mask //= 2
    leaving, _ = tie(queries, values)
    visitors = [swap(leaving, "qry", mask) for mask in masks]
    early, late = [], []
    for axis, mask in steps:
        place = (0, mask) if axis == "qry" else (mask, 0)
        near = (place, swap(keys, axis, mask), swap(values, axis, mask))
        relayed = []
        for (lib_mask, qry_mask), far_keys, far_values in early + late:
            far_keys, *_ = tie(far_keys, near[1], values)
            far_values, _ = tie(far_values, near[2])
            place = (lib_mask | mask, qry_mask)
            relayed.append((place, swap(far_keys, axis, mask), swap(far_values, axis, mask)))
        early, late = early + late + [near], relayed
    return early, late, list(zip(masks, visitors))


def cross_cores(pieces, arrivals=()):
    crossed = []
    for (lib_mask, qry_mask), *pair in pieces:
        pair = tie(*pair, *arrivals)[:2]
        crossed.append(((lib_mask | 1, qry_mask), *(swap(array, "lib", 1) for array in pair)))
    return crossed


def places_of(pieces):
    return [piece[0] for piece in pieces]


def arrays_of(pieces):
    return [array for piece in pieces for array in piece[1:]]


def body(queries, library_keys, library_values, key_scale, block_list, block_count):
    qry_count = lax.axis_size("qry")
    width = library_keys.shape[1]
    value_width = library_values.shape[1]

    partner_keys = swap(library_keys, "lib", 1)
    own_values, _ = tie(library_values, partner_keys)
    values = pl.pallas_call(
        pack_kernel,
        out_shape=jax.ShapeDtypeStruct((TILE + EXTRA, value_width), jnp.bfloat16),
        in_specs=[pl.BlockSpec(memory_space=pl.ANY)] * 2,
        out_specs=VMEM,
        scratch_shapes=[pltpu.VMEM((1, TILE), jnp.bfloat16), pltpu.SemaphoreType.DMA((2,))],
        compiler_params=params(),
    )(own_values, key_scale.reshape(1, TILE))

    masks = [2 * at + 1 for at in range(1, qry_count // 2)]
    early, relayed, visitors = gather_library(library_keys, values, queries, masks)
    piece_rows = (width // value_width + 1) * TILE + EXTRA
    cost = pl.CostEstimate(flops=2 * TILE * 4 * TILE * width * 2, bytes_accessed=4 * 1024 * 1024, transcendentals=0)
    total_shape = jax.ShapeDtypeStruct((TILE, value_width), jnp.float32)
    line_shape = jax.ShapeDtypeStruct((TILE, LANES), jnp.float32)
    pieces_total = 2 * (1 + len(early) + len(relayed))
    attend_params = params(pieces_total * piece_rows * value_width * 2)
    own_specs = [pl.BlockSpec(memory_space=pl.ANY), VMEM]
    own_scratch = [pltpu.VMEM(library_keys.shape, library_keys.dtype), pltpu.SemaphoreType.DMA]
    early_arrays = arrays_of(early)
    states = []
    for mask, visiting in visitors:
        state = pl.pallas_call(
            functools.partial(early_kernel, places_of(early), mask),
            out_shape=(total_shape, line_shape, line_shape),
            in_specs=[SMEM, SMEM] + [VMEM] * (1 + len(early_arrays)) + own_specs,
            out_specs=(VMEM,) * 3,
            scratch_shapes=[pltpu.VMEM((len(early) + 1, TILE, TILE), jnp.float32)] + own_scratch,
            compiler_params=attend_params,
            cost_estimate=cost,
        )(block_list, block_count, visiting, *early_arrays, library_keys, values)
        states.append(state)

    late = [((1, 0), partner_keys, swap(values, "lib", 1))] + cross_cores(early) + relayed + cross_cores(relayed, [state[2] for state in states])
    late_arrays = arrays_of(late)
    returned = []
    for (mask, visiting), state in zip(visitors, states):
        packed = pl.pallas_call(
            functools.partial(late_kernel, places_of(late), mask),
            out_shape=jax.ShapeDtypeStruct((TILE + EXTRA, value_width), jnp.bfloat16),
            in_specs=[SMEM, SMEM] + [VMEM] * (4 + len(late_arrays)),
            out_specs=VMEM,
            scratch_shapes=[
                pltpu.VMEM((len(late), TILE, TILE), jnp.float32),
                pltpu.VMEM((TILE, value_width), jnp.float32),
                pltpu.VMEM((TILE, TILE), jnp.float32),
            ],
            compiler_params=attend_params,
            cost_estimate=cost,
        )(block_list, block_count, visiting, *state, *late_arrays)
        returned.append(swap(packed, "qry", mask))

    total, stats = pl.pallas_call(
        functools.partial(home_kernel, places_of(early + late)),
        out_shape=(total_shape, jax.ShapeDtypeStruct((2, TILE, LANES), jnp.float32)),
        in_specs=[SMEM, SMEM] + [VMEM] * (1 + len(early_arrays) + len(late_arrays)) + own_specs,
        out_specs=(VMEM, VMEM),
        scratch_shapes=[
            pltpu.VMEM((pieces_total, TILE, TILE), jnp.float32),
            pltpu.VMEM((TILE, TILE), jnp.float32),
        ]
        + own_scratch,
        compiler_params=attend_params,
        cost_estimate=cost,
    )(block_list, block_count, queries, *early_arrays, *late_arrays, library_keys, values)

    return pl.pallas_call(
        merge_kernel,
        out_shape=jax.ShapeDtypeStruct((TILE, value_width), jnp.bfloat16),
        in_specs=[VMEM] * (2 + len(returned)),
        out_specs=VMEM,
        compiler_params=params(),
    )(total, stats, *returned)


def solution(mesh):
    in_specs = (
        P(("groups", "lib", "qry"), None),
        P(("groups", "lib", "qry"), None),
        P(("groups", "lib", "qry"), None),
        P(("groups", "lib", "qry")),
        P("groups", None),
        P("groups"),
    )
    out_specs = P(("groups", "lib", "qry"), None)
    return jax.shard_map(body, mesh=mesh, in_specs=in_specs, out_specs=out_specs, check_vma=False)
```

```python
import functools
import math

import jax
import jax.numpy as jnp
from jax import lax
from jax.experimental import pallas as pl
from jax.experimental.pallas import tpu as pltpu
from jax.sharding import PartitionSpec as P

TILE = 128
LANES = 128
EXTRA = 16
MASKED_SCORE = -1e30
SMEM = pl.BlockSpec(memory_space=pltpu.SMEM)
VMEM = pl.BlockSpec(memory_space=pltpu.VMEM)


def params(operand_bytes=0):
    return pltpu.CompilerParams(vmem_limit_bytes=operand_bytes * 3 // 2 + 6 * 1024 * 1024)


def swap(value, axis, mask):
    length = lax.axis_size(axis)
    return lax.ppermute(value, axis, [(i, i ^ mask) for i in range(length)])


def tie(*values):
    return lax.optimization_barrier(values)


def split_three(value):
    high = value.astype(jnp.bfloat16)
    rest = value - high.astype(jnp.float32)
    middle = rest.astype(jnp.bfloat16)
    low = (rest - middle.astype(jnp.float32)).astype(jnp.bfloat16)
    return high, middle, low


def pack_kernel(values_ref, scale_ref, packed_ref, row_ref, sems):
    value_width = values_ref.shape[1]
    copies = (
        pltpu.make_async_copy(values_ref, packed_ref.at[pl.ds(0, TILE)], sems.at[0]),
        pltpu.make_async_copy(scale_ref, row_ref, sems.at[1]),
    )
    for copy in copies:
        copy.start()
    packed_ref[TILE:, TILE:] = jnp.zeros((EXTRA, value_width - TILE), jnp.bfloat16)
    for copy in reversed(copies):
        copy.wait()
    row = row_ref[...].astype(jnp.float32)
    packed_ref[TILE:, 0:TILE] = jnp.broadcast_to(row, (EXTRA, TILE)).astype(jnp.bfloat16)


class Piece:
    def __init__(self, place, keys_ref, values_ref, copy=None):
        self.place = place
        self.refs = (keys_ref, values_ref)
        self.copy = copy

    def scores(self, query_ref, inverse_root):
        keys_ref, values_ref = self.refs
        product = lax.dot_general(
            query_ref[...], keys_ref[...], (((1,), (1,)), ((), ())), preferred_element_type=jnp.float32
        )
        scale = values_ref[TILE : TILE + EXTRA, 0:TILE]
        return product * (scale.astype(jnp.float32)[0:1] * inverse_root)

    def values(self):
        return self.refs[1][0:TILE, :]


def read_pieces(places, refs, own=None):
    pieces = [Piece(place, refs[2 * at], refs[2 * at + 1]) for at, place in enumerate(places)]
    refs = refs[2 * len(places) :]
    if own is not None:
        keys_ref, values_ref, *refs, held_ref, sem = refs
        copy = pltpu.make_async_copy(keys_ref, held_ref, sem)
        copy.start()
        pieces.append(Piece((0, 0), held_ref, values_ref, copy))
    return pieces, refs


def attend(pieces, panel_mask, lists_ref, counts_ref, query_ref, score_ref, total_ref, mass_ref, before=None):
    lib_index = lax.axis_index("lib")
    qry_index = lax.axis_index("qry")
    qry_count = lax.axis_size("qry")
    block_total = lax.axis_size("lib") * qry_count
    panel = lib_index * qry_count + lax.bitwise_xor(qry_index, panel_mask)
    first = lists_ref[panel, 0]
    count = counts_ref[panel]
    width = query_ref.shape[1]
    inverse_root = 1.0 / math.sqrt(width)

    def active(lib_mask, qry_mask):
        block = lax.bitwise_xor(lib_index, lib_mask) * qry_count + lax.bitwise_xor(qry_index, qry_mask)
        return lax.rem(block - first + block_total, block_total) < count

    flags = [active(*piece.place) for piece in pieces]
    score_ref[...] = jnp.full(score_ref.shape, MASKED_SCORE, jnp.float32)
    for at, (piece, flag) in enumerate(zip(pieces, flags)):
        if piece.copy is not None:
            piece.copy.wait()

        @pl.when(flag)
        def _(at=at, piece=piece):
            score_ref[at] = piece.scores(query_ref, inverse_root)

    largest = score_ref[0]
    for at in range(1, len(flags)):
        largest = jnp.maximum(largest, score_ref[at])
    row_max = jnp.max(largest, axis=1, keepdims=True)
    if before is None:
        total_ref[...] = jnp.zeros(total_ref.shape, jnp.float32)
        mass_ref[...] = jnp.zeros(mass_ref.shape, jnp.float32)
    else:
        old_total_ref, old_mass_ref, old_max_ref = before
        old_max = old_max_ref[...]
        new_max = jnp.maximum(old_max, row_max)
        shrink = jnp.exp(old_max - new_max)
        row_max = new_max[:, 0:1]
        mass_ref[...] = old_mass_ref[...] * shrink
        for at in range(0, total_ref.shape[1], LANES):
            total_ref[:, at : at + LANES] = old_total_ref[:, at : at + LANES] * shrink
    for at, (piece, flag) in enumerate(zip(pieces, flags)):

        @pl.when(flag)
        def _(at=at, piece=piece):
            weights = jnp.exp(score_ref[at] - row_max)
            mass_ref[...] += weights
            weight_high = weights.astype(jnp.bfloat16)
            weight_low = (weights - weight_high.astype(jnp.float32)).astype(jnp.bfloat16)
            values = piece.values()
            added = jnp.dot(weight_high, values, preferred_element_type=jnp.float32)
            added = added + jnp.dot(weight_low, values, preferred_element_type=jnp.float32)
            total_ref[...] += added

    return row_max


def early_kernel(places, panel_mask, lists_ref, counts_ref, query_ref, *refs):
    pieces, refs = read_pieces(places, refs, own=True)
    total_ref, mass_ref, max_ref, score_ref = refs
    row_max = attend(pieces, panel_mask, lists_ref, counts_ref, query_ref, score_ref, total_ref, mass_ref)
    max_ref[...] = jnp.broadcast_to(row_max, max_ref.shape)


def late_kernel(places, panel_mask, lists_ref, counts_ref, query_ref, *refs):
    before, refs = refs[:3], refs[3:]
    pieces, refs = read_pieces(places, refs)
    packed_ref, score_ref, total_ref, mass_ref = refs
    row_max = attend(pieces, panel_mask, lists_ref, counts_ref, query_ref, score_ref, total_ref, mass_ref, before)
    row_sum = jnp.sum(mass_ref[...], axis=1, keepdims=True)
    value_width = total_ref.shape[1]
    inverse = 1.0 / jnp.where(row_sum > 0.0, row_sum, 1.0)
    packed_ref[0:TILE, :] = (total_ref[...] * inverse).astype(jnp.bfloat16)
    row = lax.broadcasted_iota(jnp.int32, (EXTRA, LANES), 0)
    packed = jnp.zeros((EXTRA, LANES), jnp.float32)
    for first, column in ((0, row_max), (3, row_sum)):
        turned = jnp.transpose(jnp.broadcast_to(column, (TILE, LANES)))[0:EXTRA]
        for at, part in enumerate(split_three(turned)):
            packed = jnp.where(row == first + at, part.astype(jnp.float32), packed)
    packed_ref[TILE:, 0:LANES] = packed.astype(jnp.bfloat16)
    packed_ref[TILE:, LANES:] = jnp.zeros((EXTRA, value_width - LANES), jnp.bfloat16)


def home_kernel(places, lists_ref, counts_ref, query_ref, *refs):
    pieces, refs = read_pieces(places, refs, own=True)
    total_ref, stats_ref, score_ref, mass_ref = refs
    row_max = attend(pieces, 0, lists_ref, counts_ref, query_ref, score_ref, total_ref, mass_ref)
    row_sum = jnp.sum(mass_ref[...], axis=1, keepdims=True)
    stats_ref[0] = jnp.broadcast_to(row_max, (TILE, LANES))
    stats_ref[1] = jnp.broadcast_to(row_sum, (TILE, LANES))


def merge_kernel(total_ref, stats_ref, *refs):
    packed_refs, out_ref = refs[:-1], refs[-1]
    maxima = [stats_ref[0]]
    sums = [stats_ref[1]]
    for packed_ref in packed_refs:
        packed = packed_ref[TILE:, 0:LANES].astype(jnp.float32)
        for first, kept in ((0, maxima), (3, sums)):
            line = packed[first : first + 1] + packed[first + 1 : first + 2] + packed[first + 2 : first + 3]
            kept.append(jnp.transpose(jnp.broadcast_to(line, (TILE, LANES))))
    top = functools.reduce(jnp.maximum, maxima)
    factors = [jnp.exp(row_max - top) for row_max in maxima]
    masses = [factor * row_sum for factor, row_sum in zip(factors, sums)]
    inverse = 1.0 / functools.reduce(jnp.add, masses)
    scales = [factors[0] * inverse] + [mass * inverse for mass in masses[1:]]
    for at in range(0, total_ref.shape[1], LANES):
        merged = total_ref[:, at : at + LANES] * scales[0]
        for packed_ref, scale in zip(packed_refs, scales[1:]):
            merged = merged + packed_ref[0:TILE, at : at + LANES].astype(jnp.float32) * scale
        out_ref[:, at : at + LANES] = merged.astype(jnp.bfloat16)


def gather_library(keys, values, queries, masks):
    steps = [("qry", 1)]
    mask = lax.axis_size("lib") // 2
    while mask > 1:
        steps.append(("lib", mask))
        mask //= 2
    leaving, _ = tie(queries, values)
    visitors = [swap(leaving, "qry", mask) for mask in masks]
    early, late = [], []
    for axis, mask in steps:
        place = (0, mask) if axis == "qry" else (mask, 0)
        near = (place, swap(keys, axis, mask), swap(values, axis, mask))
        relayed = []
        for (lib_mask, qry_mask), far_keys, far_values in early + late:
            far_keys, *_ = tie(far_keys, near[1], values)
            far_values, _ = tie(far_values, near[2])
            place = (lib_mask | mask, qry_mask)
            relayed.append((place, swap(far_keys, axis, mask), swap(far_values, axis, mask)))
        early, late = early + late + [near], relayed
    return early, late, list(zip(masks, visitors))


def cross_cores(pieces, arrivals=()):
    crossed = []
    for (lib_mask, qry_mask), *pair in pieces:
        pair = tie(*pair, *arrivals)[:2]
        crossed.append(((lib_mask | 1, qry_mask), *(swap(array, "lib", 1) for array in pair)))
    return crossed


def places_of(pieces):
    return [piece[0] for piece in pieces]


def arrays_of(pieces):
    return [array for piece in pieces for array in piece[1:]]


def body(queries, library_keys, library_values, key_scale, block_list, block_count):
    qry_count = lax.axis_size("qry")
    width = library_keys.shape[1]
    value_width = library_values.shape[1]

    partner_keys = swap(library_keys, "lib", 1)
    own_values, _ = tie(library_values, partner_keys)
    values = pl.pallas_call(
        pack_kernel,
        out_shape=jax.ShapeDtypeStruct((TILE + EXTRA, value_width), jnp.bfloat16),
        in_specs=[pl.BlockSpec(memory_space=pl.ANY)] * 2,
        out_specs=VMEM,
        scratch_shapes=[pltpu.VMEM((1, TILE), jnp.bfloat16), pltpu.SemaphoreType.DMA((2,))],
        compiler_params=params(),
    )(own_values, key_scale.reshape(1, TILE))

    masks = [2 * at for at in range(1, qry_count // 2)]
    early, relayed, visitors = gather_library(library_keys, values, queries, masks)
    piece_rows = (width // value_width + 1) * TILE + EXTRA
    cost = pl.CostEstimate(flops=2 * TILE * 4 * TILE * width * 2, bytes_accessed=4 * 1024 * 1024, transcendentals=0)
    total_shape = jax.ShapeDtypeStruct((TILE, value_width), jnp.float32)
    line_shape = jax.ShapeDtypeStruct((TILE, LANES), jnp.float32)
    pieces_total = 2 * (1 + len(early) + len(relayed))
    attend_params = params(pieces_total * piece_rows * value_width * 2)
    own_specs = [pl.BlockSpec(memory_space=pl.ANY), VMEM]
    own_scratch = [pltpu.VMEM(library_keys.shape, library_keys.dtype), pltpu.SemaphoreType.DMA]
    early_arrays = arrays_of(early)
    states = []
    for mask, visiting in visitors:
        state = pl.pallas_call(
            functools.partial(early_kernel, places_of(early), mask),
            out_shape=(total_shape, line_shape, line_shape),
            in_specs=[SMEM, SMEM] + [VMEM] * (1 + len(early_arrays)) + own_specs,
            out_specs=(VMEM,) * 3,
            scratch_shapes=[pltpu.VMEM((len(early) + 1, TILE, TILE), jnp.float32)] + own_scratch,
            compiler_params=attend_params,
            cost_estimate=cost,
        )(block_list, block_count, visiting, *early_arrays, library_keys, values)
        states.append(state)

    late = [((1, 0), partner_keys, swap(values, "lib", 1))] + cross_cores(early) + relayed + cross_cores(relayed, [state[2] for state in states])
    late_arrays = arrays_of(late)
    returned = []
    for (mask, visiting), state in zip(visitors, states):
        packed = pl.pallas_call(
            functools.partial(late_kernel, places_of(late), mask),
            out_shape=jax.ShapeDtypeStruct((TILE + EXTRA, value_width), jnp.bfloat16),
            in_specs=[SMEM, SMEM] + [VMEM] * (4 + len(late_arrays)),
            out_specs=VMEM,
            scratch_shapes=[
                pltpu.VMEM((len(late), TILE, TILE), jnp.float32),
                pltpu.VMEM((TILE, value_width), jnp.float32),
                pltpu.VMEM((TILE, TILE), jnp.float32),
            ],
            compiler_params=attend_params,
            cost_estimate=cost,
        )(block_list, block_count, visiting, *state, *late_arrays)
        returned.append(swap(packed, "qry", mask))

    total, stats = pl.pallas_call(
        functools.partial(home_kernel, places_of(early + late)),
        out_shape=(total_shape, jax.ShapeDtypeStruct((2, TILE, LANES), jnp.float32)),
        in_specs=[SMEM, SMEM] + [VMEM] * (1 + len(early_arrays) + len(late_arrays)) + own_specs,
        out_specs=(VMEM, VMEM),
        scratch_shapes=[
            pltpu.VMEM((pieces_total, TILE, TILE), jnp.float32),
            pltpu.VMEM((TILE, TILE), jnp.float32),
        ]
        + own_scratch,
        compiler_params=attend_params,
        cost_estimate=cost,
    )(block_list, block_count, queries, *early_arrays, *late_arrays, library_keys, values)

    return pl.pallas_call(
        merge_kernel,
        out_shape=jax.ShapeDtypeStruct((TILE, value_width), jnp.bfloat16),
        in_specs=[VMEM] * (2 + len(returned)),
        out_specs=VMEM,
        compiler_params=params(),
    )(total, stats, *returned)


def solution(mesh):
    in_specs = (
        P(("groups", "lib", "qry"), None),
        P(("groups", "lib", "qry"), None),
        P(("groups", "lib", "qry"), None),
        P(("groups", "lib", "qry")),
        P("groups", None),
        P("groups"),
    )
    out_specs = P(("groups", "lib", "qry"), None)
    return jax.shard_map(body, mesh=mesh, in_specs=in_specs, out_specs=out_specs, check_vma=False)
```

```python
import functools
import math

import jax
import jax.numpy as jnp
from jax import lax
from jax.experimental import pallas as pl
from jax.experimental.pallas import tpu as pltpu
from jax.sharding import PartitionSpec as P

TILE = 128
LANES = 128
EXTRA = 16
MASKED_SCORE = -1e30
SMEM = pl.BlockSpec(memory_space=pltpu.SMEM)
VMEM = pl.BlockSpec(memory_space=pltpu.VMEM)


def params(operand_bytes=0):
    return pltpu.CompilerParams(vmem_limit_bytes=operand_bytes * 3 // 2 + 6 * 1024 * 1024)


def swap(value, axis, mask):
    length = lax.axis_size(axis)
    return lax.ppermute(value, axis, [(i, i ^ mask) for i in range(length)])


def tie(*values):
    return lax.optimization_barrier(values)


def split_three(value):
    high = value.astype(jnp.bfloat16)
    rest = value - high.astype(jnp.float32)
    middle = rest.astype(jnp.bfloat16)
    low = (rest - middle.astype(jnp.float32)).astype(jnp.bfloat16)
    return high, middle, low


def pack_kernel(values_ref, scale_ref, packed_ref, row_ref, sems):
    value_width = values_ref.shape[1]
    copies = (
        pltpu.make_async_copy(values_ref, packed_ref.at[pl.ds(0, TILE)], sems.at[0]),
        pltpu.make_async_copy(scale_ref, row_ref, sems.at[1]),
    )
    for copy in copies:
        copy.start()
    packed_ref[TILE:, TILE:] = jnp.zeros((EXTRA, value_width - TILE), jnp.bfloat16)
    for copy in reversed(copies):
        copy.wait()
    row = row_ref[...].astype(jnp.float32)
    packed_ref[TILE:, 0:TILE] = jnp.broadcast_to(row, (EXTRA, TILE)).astype(jnp.bfloat16)


class Piece:
    def __init__(self, place, keys_ref, values_ref, copy=None):
        self.place = place
        self.refs = (keys_ref, values_ref)
        self.copy = copy

    def scores(self, query_ref, inverse_root):
        keys_ref, values_ref = self.refs
        product = lax.dot_general(
            query_ref[...], keys_ref[...], (((1,), (1,)), ((), ())), preferred_element_type=jnp.float32
        )
        scale = values_ref[TILE : TILE + EXTRA, 0:TILE]
        return product * (scale.astype(jnp.float32)[0:1] * inverse_root)

    def values(self):
        return self.refs[1][0:TILE, :]


def read_pieces(places, refs, own=None):
    pieces = [Piece(place, refs[2 * at], refs[2 * at + 1]) for at, place in enumerate(places)]
    refs = refs[2 * len(places) :]
    if own is not None:
        keys_ref, values_ref, *refs, held_ref, sem = refs
        copy = pltpu.make_async_copy(keys_ref, held_ref, sem)
        copy.start()
        pieces.append(Piece((0, 0), held_ref, values_ref, copy))
    return pieces, refs


def attend(pieces, panel_mask, lists_ref, counts_ref, query_ref, score_ref, total_ref, mass_ref, before=None):
    lib_index = lax.axis_index("lib")
    qry_index = lax.axis_index("qry")
    qry_count = lax.axis_size("qry")
    block_total = lax.axis_size("lib") * qry_count
    panel = lib_index * qry_count + lax.bitwise_xor(qry_index, panel_mask)
    first = lists_ref[panel, 0]
    count = counts_ref[panel]
    width = query_ref.shape[1]
    inverse_root = 1.0 / math.sqrt(width)

    def active(lib_mask, qry_mask):
        block = lax.bitwise_xor(lib_index, lib_mask) * qry_count + lax.bitwise_xor(qry_index, qry_mask)
        return lax.rem(block - first + block_total, block_total) < count

    flags = [active(*piece.place) for piece in pieces]
    score_ref[...] = jnp.full(score_ref.shape, MASKED_SCORE, jnp.float32)
    for at, (piece, flag) in enumerate(zip(pieces, flags)):
        if piece.copy is not None:
            piece.copy.wait()

        @pl.when(flag)
        def _(at=at, piece=piece):
            score_ref[at] = piece.scores(query_ref, inverse_root)

    largest = score_ref[0]
    for at in range(1, len(flags)):
        largest = jnp.maximum(largest, score_ref[at])
    row_max = jnp.max(largest, axis=1, keepdims=True)
    if before is None:
        total_ref[...] = jnp.zeros(total_ref.shape, jnp.float32)
        mass_ref[...] = jnp.zeros(mass_ref.shape, jnp.float32)
    else:
        old_total_ref, old_mass_ref, old_max_ref = before
        old_max = old_max_ref[...]
        new_max = jnp.maximum(old_max, row_max)
        shrink = jnp.exp(old_max - new_max)
        row_max = new_max[:, 0:1]
        mass_ref[...] = old_mass_ref[...] * shrink
        for at in range(0, total_ref.shape[1], LANES):
            total_ref[:, at : at + LANES] = old_total_ref[:, at : at + LANES] * shrink
    for at, (piece, flag) in enumerate(zip(pieces, flags)):

        @pl.when(flag)
        def _(at=at, piece=piece):
            weights = jnp.exp(score_ref[at] - row_max)
            mass_ref[...] += weights
            weight_high = weights.astype(jnp.bfloat16)
            weight_low = (weights - weight_high.astype(jnp.float32)).astype(jnp.bfloat16)
            values = piece.values()
            added = jnp.dot(weight_high, values, preferred_element_type=jnp.float32)
            added = added + jnp.dot(weight_low, values, preferred_element_type=jnp.float32)
            total_ref[...] += added

    return row_max


def early_kernel(places, panel_mask, lists_ref, counts_ref, query_ref, *refs):
    pieces, refs = read_pieces(places, refs, own=True)
    total_ref, mass_ref, max_ref, score_ref = refs
    row_max = attend(pieces, panel_mask, lists_ref, counts_ref, query_ref, score_ref, total_ref, mass_ref)
    max_ref[...] = jnp.broadcast_to(row_max, max_ref.shape)


def late_kernel(places, panel_mask, lists_ref, counts_ref, query_ref, *refs):
    before, refs = refs[:3], refs[3:]
    pieces, refs = read_pieces(places, refs)
    packed_ref, score_ref, total_ref, mass_ref = refs
    row_max = attend(pieces, panel_mask, lists_ref, counts_ref, query_ref, score_ref, total_ref, mass_ref, before)
    row_sum = jnp.sum(mass_ref[...], axis=1, keepdims=True)
    value_width = total_ref.shape[1]
    inverse = 1.0 / jnp.where(row_sum > 0.0, row_sum, 1.0)
    packed_ref[0:TILE, :] = (total_ref[...] * inverse).astype(jnp.bfloat16)
    row = lax.broadcasted_iota(jnp.int32, (EXTRA, LANES), 0)
    packed = jnp.zeros((EXTRA, LANES), jnp.float32)
    for first, column in ((0, row_max), (3, row_sum)):
        turned = jnp.transpose(jnp.broadcast_to(column, (TILE, LANES)))[0:EXTRA]
        for at, part in enumerate(split_three(turned)):
            packed = jnp.where(row == first + at, part.astype(jnp.float32), packed)
    packed_ref[TILE:, 0:LANES] = packed.astype(jnp.bfloat16)
    packed_ref[TILE:, LANES:] = jnp.zeros((EXTRA, value_width - LANES), jnp.bfloat16)


def home_kernel(places, lists_ref, counts_ref, query_ref, *refs):
    pieces, refs = read_pieces(places, refs, own=True)
    total_ref, stats_ref, score_ref, mass_ref = refs
    row_max = attend(pieces, 0, lists_ref, counts_ref, query_ref, score_ref, total_ref, mass_ref)
    row_sum = jnp.sum(mass_ref[...], axis=1, keepdims=True)
    stats_ref[0] = jnp.broadcast_to(row_max, (TILE, LANES))
    stats_ref[1] = jnp.broadcast_to(row_sum, (TILE, LANES))


def merge_kernel(total_ref, stats_ref, *refs):
    packed_refs, out_ref = refs[:-1], refs[-1]
    maxima = [stats_ref[0]]
    sums = [stats_ref[1]]
    for packed_ref in packed_refs:
        packed = packed_ref[TILE:, 0:LANES].astype(jnp.float32)
        for first, kept in ((0, maxima), (3, sums)):
            line = packed[first : first + 1] + packed[first + 1 : first + 2] + packed[first + 2 : first + 3]
            kept.append(jnp.transpose(jnp.broadcast_to(line, (TILE, LANES))))
    top = functools.reduce(jnp.maximum, maxima)
    factors = [jnp.exp(row_max - top) for row_max in maxima]
    masses = [factor * row_sum for factor, row_sum in zip(factors, sums)]
    inverse = 1.0 / functools.reduce(jnp.add, masses)
    scales = [factors[0] * inverse] + [mass * inverse for mass in masses[1:]]
    for at in range(0, total_ref.shape[1], LANES):
        merged = total_ref[:, at : at + LANES] * scales[0]
        for packed_ref, scale in zip(packed_refs, scales[1:]):
            merged = merged + packed_ref[0:TILE, at : at + LANES].astype(jnp.float32) * scale
        out_ref[:, at : at + LANES] = merged.astype(jnp.bfloat16)


def gather_library(keys, partner_keys, values, queries, masks):
    steps = [("qry", 1)]
    mask = lax.axis_size("lib") // 2
    while mask > 1:
        steps.append(("lib", mask))
        mask //= 2
    leaving, _ = tie(queries, values)
    visitors = [swap(leaving, "qry", mask) for mask in masks]
    early, late = [], []
    for axis, mask in steps:
        place = (0, mask) if axis == "qry" else (mask, 0)
        leaving_keys = tie(keys, partner_keys)[0] if axis == "qry" else keys
        near = (place, swap(leaving_keys, axis, mask), swap(values, axis, mask))
        relayed = []
        for (lib_mask, qry_mask), far_keys, far_values in early + late:
            far_keys, *_ = tie(far_keys, near[1], values)
            far_values, _ = tie(far_values, near[2])
            place = (lib_mask | mask, qry_mask)
            relayed.append((place, swap(far_keys, axis, mask), swap(far_values, axis, mask)))
        early, late = early + late + [near], relayed
    return early, late, list(zip(masks, visitors))


def cross_cores(pieces, arrivals=()):
    crossed = []
    for (lib_mask, qry_mask), *pair in pieces:
        pair = tie(*pair, *arrivals)[:2]
        crossed.append(((lib_mask | 1, qry_mask), *(swap(array, "lib", 1) for array in pair)))
    return crossed


def places_of(pieces):
    return [piece[0] for piece in pieces]


def arrays_of(pieces):
    return [array for piece in pieces for array in piece[1:]]


def body(queries, library_keys, library_values, key_scale, block_list, block_count):
    qry_count = lax.axis_size("qry")
    width = library_keys.shape[1]
    value_width = library_values.shape[1]

    partner_keys = swap(library_keys, "lib", 1)
    own_values, _ = tie(library_values, partner_keys)
    values = pl.pallas_call(
        pack_kernel,
        out_shape=jax.ShapeDtypeStruct((TILE + EXTRA, value_width), jnp.bfloat16),
        in_specs=[pl.BlockSpec(memory_space=pl.ANY)] * 2,
        out_specs=VMEM,
        scratch_shapes=[pltpu.VMEM((1, TILE), jnp.bfloat16), pltpu.SemaphoreType.DMA((2,))],
        compiler_params=params(),
    )(own_values, key_scale.reshape(1, TILE))

    masks = [2 * at + 1 for at in range(1, qry_count // 2)]
    early, relayed, visitors = gather_library(library_keys, partner_keys, values, queries, masks)
    piece_rows = (width // value_width + 1) * TILE + EXTRA
    cost = pl.CostEstimate(flops=2 * TILE * 4 * TILE * width * 2, bytes_accessed=4 * 1024 * 1024, transcendentals=0)
    total_shape = jax.ShapeDtypeStruct((TILE, value_width), jnp.float32)
    line_shape = jax.ShapeDtypeStruct((TILE, LANES), jnp.float32)
    pieces_total = 2 * (1 + len(early) + len(relayed))
    attend_params = params(pieces_total * piece_rows * value_width * 2)
    own_specs = [pl.BlockSpec(memory_space=pl.ANY), VMEM]
    own_scratch = [pltpu.VMEM(library_keys.shape, library_keys.dtype), pltpu.SemaphoreType.DMA]
    near = early + cross_cores(early[:-1])
    near_arrays = arrays_of(near)
    states = []
    for mask, visiting in visitors:
        state = pl.pallas_call(
            functools.partial(early_kernel, places_of(near), mask),
            out_shape=(total_shape, line_shape, line_shape),
            in_specs=[SMEM, SMEM] + [VMEM] * (1 + len(near_arrays)) + own_specs,
            out_specs=(VMEM,) * 3,
            scratch_shapes=[pltpu.VMEM((len(near) + 1, TILE, TILE), jnp.float32)] + own_scratch,
            compiler_params=attend_params,
            cost_estimate=cost,
        )(block_list, block_count, visiting, *near_arrays, library_keys, values)
        states.append(state)

    late = [((1, 0), partner_keys, swap(values, "lib", 1))] + cross_cores(early[-1:]) + relayed
    late += cross_cores(relayed, [state[2] for state in states])
    late_arrays = arrays_of(late)
    returned = []
    for (mask, visiting), state in zip(visitors, states):
        packed = pl.pallas_call(
            functools.partial(late_kernel, places_of(late), mask),
            out_shape=jax.ShapeDtypeStruct((TILE + EXTRA, value_width), jnp.bfloat16),
            in_specs=[SMEM, SMEM] + [VMEM] * (4 + len(late_arrays)),
            out_specs=VMEM,
            scratch_shapes=[
                pltpu.VMEM((len(late), TILE, TILE), jnp.float32),
                pltpu.VMEM((TILE, value_width), jnp.float32),
                pltpu.VMEM((TILE, TILE), jnp.float32),
            ],
            compiler_params=attend_params,
            cost_estimate=cost,
        )(block_list, block_count, visiting, *state, *late_arrays)
        returned.append(swap(packed, "qry", mask))

    total, stats = pl.pallas_call(
        functools.partial(home_kernel, places_of(near + late)),
        out_shape=(total_shape, jax.ShapeDtypeStruct((2, TILE, LANES), jnp.float32)),
        in_specs=[SMEM, SMEM] + [VMEM] * (1 + len(near_arrays) + len(late_arrays)) + own_specs,
        out_specs=(VMEM, VMEM),
        scratch_shapes=[
            pltpu.VMEM((pieces_total, TILE, TILE), jnp.float32),
            pltpu.VMEM((TILE, TILE), jnp.float32),
        ]
        + own_scratch,
        compiler_params=attend_params,
        cost_estimate=cost,
    )(block_list, block_count, queries, *near_arrays, *late_arrays, library_keys, values)

    return pl.pallas_call(
        merge_kernel,
        out_shape=jax.ShapeDtypeStruct((TILE, value_width), jnp.bfloat16),
        in_specs=[VMEM] * (2 + len(returned)),
        out_specs=VMEM,
        compiler_params=params(),
    )(total, stats, *returned)


def solution(mesh):
    in_specs = (
        P(("groups", "lib", "qry"), None),
        P(("groups", "lib", "qry"), None),
        P(("groups", "lib", "qry"), None),
        P(("groups", "lib", "qry")),
        P("groups", None),
        P("groups"),
    )
    out_specs = P(("groups", "lib", "qry"), None)
    return jax.shard_map(body, mesh=mesh, in_specs=in_specs, out_specs=out_specs, check_vma=False)
```

```python
import functools
import math

import jax
import jax.numpy as jnp
from jax import lax
from jax.experimental import pallas as pl
from jax.experimental.pallas import tpu as pltpu
from jax.sharding import PartitionSpec as P

TILE = 128
LANES = 128
EXTRA = 16
MASKED_SCORE = -1e30
SMEM = pl.BlockSpec(memory_space=pltpu.SMEM)
VMEM = pl.BlockSpec(memory_space=pltpu.VMEM)


def params(operand_bytes=0):
    return pltpu.CompilerParams(vmem_limit_bytes=operand_bytes * 3 // 2 + 6 * 1024 * 1024)


def swap(value, axis, mask):
    length = lax.axis_size(axis)
    return lax.ppermute(value, axis, [(i, i ^ mask) for i in range(length)])


def tie(*values):
    return lax.optimization_barrier(values)


def split_three(value):
    high = value.astype(jnp.bfloat16)
    rest = value - high.astype(jnp.float32)
    middle = rest.astype(jnp.bfloat16)
    low = (rest - middle.astype(jnp.float32)).astype(jnp.bfloat16)
    return high, middle, low


def pack_kernel(values_ref, scale_ref, packed_ref, row_ref, sems):
    value_width = values_ref.shape[1]
    copies = (
        pltpu.make_async_copy(values_ref, packed_ref.at[pl.ds(0, TILE)], sems.at[0]),
        pltpu.make_async_copy(scale_ref, row_ref, sems.at[1]),
    )
    for copy in copies:
        copy.start()
    packed_ref[TILE:, TILE:] = jnp.zeros((EXTRA, value_width - TILE), jnp.bfloat16)
    for copy in reversed(copies):
        copy.wait()
    row = row_ref[...].astype(jnp.float32)
    packed_ref[TILE:, 0:TILE] = jnp.broadcast_to(row, (EXTRA, TILE)).astype(jnp.bfloat16)


class Piece:
    def __init__(self, place, keys_ref, values_ref, copy=None):
        self.place = place
        self.refs = (keys_ref, values_ref)
        self.copy = copy

    def scores(self, query_ref, inverse_root):
        keys_ref, values_ref = self.refs
        product = lax.dot_general(
            query_ref[...], keys_ref[...], (((1,), (1,)), ((), ())), preferred_element_type=jnp.float32
        )
        scale = values_ref[TILE : TILE + EXTRA, 0:TILE]
        return product * (scale.astype(jnp.float32)[0:1] * inverse_root)

    def values(self):
        return self.refs[1][0:TILE, :]


def read_pieces(places, refs, own=None):
    pieces = [Piece(place, refs[2 * at], refs[2 * at + 1]) for at, place in enumerate(places)]
    refs = refs[2 * len(places) :]
    if own is not None:
        keys_ref, values_ref, *refs, held_ref, sem = refs
        copy = pltpu.make_async_copy(keys_ref, held_ref, sem)
        copy.start()
        pieces.append(Piece((0, 0), held_ref, values_ref, copy))
    return pieces, refs


def attend(pieces, panel_mask, lists_ref, counts_ref, query_ref, score_ref, total_ref, mass_ref, before=None):
    lib_index = lax.axis_index("lib")
    qry_index = lax.axis_index("qry")
    qry_count = lax.axis_size("qry")
    block_total = lax.axis_size("lib") * qry_count
    panel = lib_index * qry_count + lax.bitwise_xor(qry_index, panel_mask)
    first = lists_ref[panel, 0]
    count = counts_ref[panel]
    width = query_ref.shape[1]
    inverse_root = 1.0 / math.sqrt(width)

    def active(lib_mask, qry_mask):
        block = lax.bitwise_xor(lib_index, lib_mask) * qry_count + lax.bitwise_xor(qry_index, qry_mask)
        return lax.rem(block - first + block_total, block_total) < count

    flags = [active(*piece.place) for piece in pieces]
    score_ref[...] = jnp.full(score_ref.shape, MASKED_SCORE, jnp.float32)
    for at, (piece, flag) in enumerate(zip(pieces, flags)):
        if piece.copy is not None:
            piece.copy.wait()

        @pl.when(flag)
        def _(at=at, piece=piece):
            score_ref[at] = piece.scores(query_ref, inverse_root)

    largest = score_ref[0]
    for at in range(1, len(flags)):
        largest = jnp.maximum(largest, score_ref[at])
    row_max = jnp.max(largest, axis=1, keepdims=True)
    if before is None:
        total_ref[...] = jnp.zeros(total_ref.shape, jnp.float32)
        mass_ref[...] = jnp.zeros(mass_ref.shape, jnp.float32)
    else:
        old_total_ref, old_mass_ref, old_max_ref = before
        old_max = old_max_ref[...]
        new_max = jnp.maximum(old_max, row_max)
        shrink = jnp.exp(old_max - new_max)
        row_max = new_max[:, 0:1]
        mass_ref[...] = old_mass_ref[...] * shrink
        for at in range(0, total_ref.shape[1], LANES):
            total_ref[:, at : at + LANES] = old_total_ref[:, at : at + LANES] * shrink
    for at, (piece, flag) in enumerate(zip(pieces, flags)):

        @pl.when(flag)
        def _(at=at, piece=piece):
            weights = jnp.exp(score_ref[at] - row_max)
            mass_ref[...] += weights
            weight_high = weights.astype(jnp.bfloat16)
            weight_low = (weights - weight_high.astype(jnp.float32)).astype(jnp.bfloat16)
            values = piece.values()
            added = jnp.dot(weight_high, values, preferred_element_type=jnp.float32)
            added = added + jnp.dot(weight_low, values, preferred_element_type=jnp.float32)
            total_ref[...] += added

    return row_max


def early_kernel(places, panel_mask, lists_ref, counts_ref, query_ref, *refs):
    pieces, refs = read_pieces(places, refs, own=True)
    total_ref, mass_ref, max_ref, score_ref = refs
    row_max = attend(pieces, panel_mask, lists_ref, counts_ref, query_ref, score_ref, total_ref, mass_ref)
    max_ref[...] = jnp.broadcast_to(row_max, max_ref.shape)


def late_kernel(places, panel_mask, lists_ref, counts_ref, query_ref, *refs):
    before, refs = refs[:3], refs[3:]
    pieces, refs = read_pieces(places, refs)
    packed_ref, score_ref, total_ref, mass_ref = refs
    row_max = attend(pieces, panel_mask, lists_ref, counts_ref, query_ref, score_ref, total_ref, mass_ref, before)
    row_sum = jnp.sum(mass_ref[...], axis=1, keepdims=True)
    value_width = total_ref.shape[1]
    inverse = 1.0 / jnp.where(row_sum > 0.0, row_sum, 1.0)
    packed_ref[0:TILE, :] = (total_ref[...] * inverse).astype(jnp.bfloat16)
    row = lax.broadcasted_iota(jnp.int32, (EXTRA, LANES), 0)
    packed = jnp.zeros((EXTRA, LANES), jnp.float32)
    for first, column in ((0, row_max), (3, row_sum)):
        turned = jnp.transpose(jnp.broadcast_to(column, (TILE, LANES)))[0:EXTRA]
        for at, part in enumerate(split_three(turned)):
            packed = jnp.where(row == first + at, part.astype(jnp.float32), packed)
    packed_ref[TILE:, 0:LANES] = packed.astype(jnp.bfloat16)
    packed_ref[TILE:, LANES:] = jnp.zeros((EXTRA, value_width - LANES), jnp.bfloat16)


def home_kernel(places, lists_ref, counts_ref, query_ref, *refs):
    pieces, refs = read_pieces(places, refs, own=True)
    total_ref, stats_ref, score_ref, mass_ref = refs
    row_max = attend(pieces, 0, lists_ref, counts_ref, query_ref, score_ref, total_ref, mass_ref)
    row_sum = jnp.sum(mass_ref[...], axis=1, keepdims=True)
    stats_ref[0] = jnp.broadcast_to(row_max, (TILE, LANES))
    stats_ref[1] = jnp.broadcast_to(row_sum, (TILE, LANES))


def merge_kernel(total_ref, stats_ref, *refs):
    packed_refs, out_ref = refs[:-1], refs[-1]
    maxima = [stats_ref[0]]
    sums = [stats_ref[1]]
    for packed_ref in packed_refs:
        packed = packed_ref[TILE:, 0:LANES].astype(jnp.float32)
        for first, kept in ((0, maxima), (3, sums)):
            line = packed[first : first + 1] + packed[first + 1 : first + 2] + packed[first + 2 : first + 3]
            kept.append(jnp.transpose(jnp.broadcast_to(line, (TILE, LANES))))
    top = functools.reduce(jnp.maximum, maxima)
    factors = [jnp.exp(row_max - top) for row_max in maxima]
    masses = [factor * row_sum for factor, row_sum in zip(factors, sums)]
    inverse = 1.0 / functools.reduce(jnp.add, masses)
    scales = [factors[0] * inverse] + [mass * inverse for mass in masses[1:]]
    for at in range(0, total_ref.shape[1], LANES):
        merged = total_ref[:, at : at + LANES] * scales[0]
        for packed_ref, scale in zip(packed_refs, scales[1:]):
            merged = merged + packed_ref[0:TILE, at : at + LANES].astype(jnp.float32) * scale
        out_ref[:, at : at + LANES] = merged.astype(jnp.bfloat16)


def gather_library(keys, partner_keys, values, queries, masks):
    steps = [("qry", 1)]
    mask = lax.axis_size("lib") // 2
    while mask > 1:
        steps.append(("lib", mask))
        mask //= 2
    leaving, _ = tie(queries, values)
    visitors = [swap(leaving, "qry", mask) for mask in masks]
    early, late = [], []
    for axis, mask in steps:
        place = (0, mask) if axis == "qry" else (mask, 0)
        leaving_keys = tie(keys, partner_keys)[0] if axis == "qry" else keys
        near = (place, swap(leaving_keys, axis, mask), swap(values, axis, mask))
        relayed = []
        for (lib_mask, qry_mask), far_keys, far_values in early + late:
            far_keys, *_ = tie(far_keys, near[1], values)
            far_values, _ = tie(far_values, near[2])
            place = (lib_mask | mask, qry_mask)
            relayed.append((place, swap(far_keys, axis, mask), swap(far_values, axis, mask)))
        early, late = early + late + [near], relayed
    return early, late, list(zip(masks, visitors))


def cross_cores(pieces, arrivals=()):
    crossed = []
    for (lib_mask, qry_mask), *pair in pieces:
        pair = tie(*pair, *arrivals)[:2]
        crossed.append(((lib_mask | 1, qry_mask), *(swap(array, "lib", 1) for array in pair)))
    return crossed


def places_of(pieces):
    return [piece[0] for piece in pieces]


def arrays_of(pieces):
    return [array for piece in pieces for array in piece[1:]]


def body(queries, library_keys, library_values, key_scale, block_list, block_count):
    qry_count = lax.axis_size("qry")
    width = library_keys.shape[1]
    value_width = library_values.shape[1]

    partner_keys = swap(library_keys, "lib", 1)
    own_values, _ = tie(library_values, partner_keys)
    values = pl.pallas_call(
        pack_kernel,
        out_shape=jax.ShapeDtypeStruct((TILE + EXTRA, value_width), jnp.bfloat16),
        in_specs=[pl.BlockSpec(memory_space=pl.ANY)] * 2,
        out_specs=VMEM,
        scratch_shapes=[pltpu.VMEM((1, TILE), jnp.bfloat16), pltpu.SemaphoreType.DMA((2,))],
        compiler_params=params(),
    )(own_values, key_scale.reshape(1, TILE))

    masks = [2 * at + 1 for at in range(1, qry_count // 2)]
    early, relayed, visitors = gather_library(library_keys, partner_keys, values, queries, masks)
    piece_rows = (width // value_width + 1) * TILE + EXTRA
    cost = pl.CostEstimate(flops=2 * TILE * 4 * TILE * width * 2, bytes_accessed=4 * 1024 * 1024, transcendentals=0)
    total_shape = jax.ShapeDtypeStruct((TILE, value_width), jnp.float32)
    line_shape = jax.ShapeDtypeStruct((TILE, LANES), jnp.float32)
    pieces_total = 2 * (1 + len(early) + len(relayed))
    attend_params = params(pieces_total * piece_rows * value_width * 2)
    own_specs = [pl.BlockSpec(memory_space=pl.ANY), VMEM]
    own_scratch = [pltpu.VMEM(library_keys.shape, library_keys.dtype), pltpu.SemaphoreType.DMA]
    early_arrays = arrays_of(early)
    states = []
    for mask, visiting in visitors:
        state = pl.pallas_call(
            functools.partial(early_kernel, places_of(early), mask),
            out_shape=(total_shape, line_shape, line_shape),
            in_specs=[SMEM, SMEM] + [VMEM] * (1 + len(early_arrays)) + own_specs,
            out_specs=(VMEM,) * 3,
            scratch_shapes=[pltpu.VMEM((len(early) + 1, TILE, TILE), jnp.float32)] + own_scratch,
            compiler_params=attend_params,
            cost_estimate=cost,
        )(block_list, block_count, visiting, *early_arrays, library_keys, values)
        states.append(state)

    late = [((1, 0), partner_keys, swap(values, "lib", 1))] + cross_cores(early) + relayed + cross_cores(relayed, [state[2] for state in states])
    late_arrays = arrays_of(late)
    returned = []
    for (mask, visiting), state in zip(visitors, states):
        packed = pl.pallas_call(
            functools.partial(late_kernel, places_of(late), mask),
            out_shape=jax.ShapeDtypeStruct((TILE + EXTRA, value_width), jnp.bfloat16),
            in_specs=[SMEM, SMEM] + [VMEM] * (4 + len(late_arrays)),
            out_specs=VMEM,
            scratch_shapes=[
                pltpu.VMEM((len(late), TILE, TILE), jnp.float32),
                pltpu.VMEM((TILE, value_width), jnp.float32),
                pltpu.VMEM((TILE, TILE), jnp.float32),
            ],
            compiler_params=attend_params,
            cost_estimate=cost,
        )(block_list, block_count, visiting, *state, *late_arrays)
        returned.append(swap(packed, "qry", mask))

    total, stats = pl.pallas_call(
        functools.partial(home_kernel, places_of(early + late)),
        out_shape=(total_shape, jax.ShapeDtypeStruct((2, TILE, LANES), jnp.float32)),
        in_specs=[SMEM, SMEM] + [VMEM] * (1 + len(early_arrays) + len(late_arrays)) + own_specs,
        out_specs=(VMEM, VMEM),
        scratch_shapes=[
            pltpu.VMEM((pieces_total, TILE, TILE), jnp.float32),
            pltpu.VMEM((TILE, TILE), jnp.float32),
        ]
        + own_scratch,
        compiler_params=attend_params,
        cost_estimate=cost,
    )(block_list, block_count, queries, *early_arrays, *late_arrays, library_keys, values)

    return pl.pallas_call(
        merge_kernel,
        out_shape=jax.ShapeDtypeStruct((TILE, value_width), jnp.bfloat16),
        in_specs=[VMEM] * (2 + len(returned)),
        out_specs=VMEM,
        compiler_params=params(),
    )(total, stats, *returned)


def solution(mesh):
    in_specs = (
        P(("groups", "lib", "qry"), None),
        P(("groups", "lib", "qry"), None),
        P(("groups", "lib", "qry"), None),
        P(("groups", "lib", "qry")),
        P("groups", None),
        P("groups"),
    )
    out_specs = P(("groups", "lib", "qry"), None)
    return jax.shard_map(body, mesh=mesh, in_specs=in_specs, out_specs=out_specs, check_vma=False)
```

```python
import functools
import math

import jax
import jax.numpy as jnp
from jax import lax
from jax.experimental import pallas as pl
from jax.experimental.pallas import tpu as pltpu
from jax.sharding import PartitionSpec as P

TILE = 128
LANES = 128
EXTRA = 16
MASKED_SCORE = -1e30
SMEM = pl.BlockSpec(memory_space=pltpu.SMEM)
VMEM = pl.BlockSpec(memory_space=pltpu.VMEM)


def params(operand_bytes=0):
    return pltpu.CompilerParams(vmem_limit_bytes=operand_bytes * 3 // 2 + 6 * 1024 * 1024)


def swap(value, axis, mask):
    length = lax.axis_size(axis)
    return lax.ppermute(value, axis, [(i, i ^ mask) for i in range(length)])


def swap_some(value, axis, mask, inner):
    length = lax.axis_size(axis)
    pairs = [(i, i ^ mask) for i in range(length) if (abs(i - (i ^ mask)) * 2 <= mask) == inner]
    return lax.ppermute(value, axis, pairs)


def tie(*values):
    return lax.optimization_barrier(values)


def split_three(value):
    high = value.astype(jnp.bfloat16)
    rest = value - high.astype(jnp.float32)
    middle = rest.astype(jnp.bfloat16)
    low = (rest - middle.astype(jnp.float32)).astype(jnp.bfloat16)
    return high, middle, low


def pack_kernel(values_ref, scale_ref, packed_ref, row_ref, sems):
    value_width = values_ref.shape[1]
    copies = (
        pltpu.make_async_copy(values_ref, packed_ref.at[pl.ds(0, TILE)], sems.at[0]),
        pltpu.make_async_copy(scale_ref, row_ref, sems.at[1]),
    )
    for copy in copies:
        copy.start()
    packed_ref[TILE:, TILE:] = jnp.zeros((EXTRA, value_width - TILE), jnp.bfloat16)
    for copy in reversed(copies):
        copy.wait()
    row = row_ref[...].astype(jnp.float32)
    packed_ref[TILE:, 0:TILE] = jnp.broadcast_to(row, (EXTRA, TILE)).astype(jnp.bfloat16)


class Piece:
    def __init__(self, place, keys_ref, values_ref, copy=None):
        self.place = place
        self.refs = (keys_ref, values_ref)
        self.copy = copy

    def scores(self, query_ref, inverse_root):
        keys_ref, values_ref = self.refs
        product = lax.dot_general(
            query_ref[...], keys_ref[...], (((1,), (1,)), ((), ())), preferred_element_type=jnp.float32
        )
        scale = values_ref[TILE : TILE + EXTRA, 0:TILE]
        return product * (scale.astype(jnp.float32)[0:1] * inverse_root)

    def values(self):
        return self.refs[1][0:TILE, :]


def read_pieces(places, refs, own=None):
    pieces = [Piece(place, refs[2 * at], refs[2 * at + 1]) for at, place in enumerate(places)]
    refs = refs[2 * len(places) :]
    if own is not None:
        keys_ref, values_ref, *refs, held_ref, sem = refs
        copy = pltpu.make_async_copy(keys_ref, held_ref, sem)
        copy.start()
        pieces.append(Piece((0, 0), held_ref, values_ref, copy))
    return pieces, refs


def attend(pieces, panel_mask, lists_ref, counts_ref, query_ref, score_ref, total_ref, mass_ref, before=None):
    lib_index = lax.axis_index("lib")
    qry_index = lax.axis_index("qry")
    qry_count = lax.axis_size("qry")
    block_total = lax.axis_size("lib") * qry_count
    panel = lib_index * qry_count + lax.bitwise_xor(qry_index, panel_mask)
    first = lists_ref[panel, 0]
    count = counts_ref[panel]
    width = query_ref.shape[1]
    inverse_root = 1.0 / math.sqrt(width)

    def active(lib_mask, qry_mask):
        block = lax.bitwise_xor(lib_index, lib_mask) * qry_count + lax.bitwise_xor(qry_index, qry_mask)
        return lax.rem(block - first + block_total, block_total) < count

    flags = [active(*piece.place) for piece in pieces]
    score_ref[...] = jnp.full(score_ref.shape, MASKED_SCORE, jnp.float32)
    for at, (piece, flag) in enumerate(zip(pieces, flags)):
        if piece.copy is not None:
            piece.copy.wait()

        @pl.when(flag)
        def _(at=at, piece=piece):
            score_ref[at] = piece.scores(query_ref, inverse_root)

    largest = score_ref[0]
    for at in range(1, len(flags)):
        largest = jnp.maximum(largest, score_ref[at])
    row_max = jnp.max(largest, axis=1, keepdims=True)
    if before is None:
        total_ref[...] = jnp.zeros(total_ref.shape, jnp.float32)
        mass_ref[...] = jnp.zeros(mass_ref.shape, jnp.float32)
    else:
        old_total_ref, old_mass_ref, old_max_ref = before
        old_max = old_max_ref[...]
        new_max = jnp.maximum(old_max, row_max)
        shrink = jnp.exp(old_max - new_max)
        row_max = new_max[:, 0:1]
        mass_ref[...] = old_mass_ref[...] * shrink
        for at in range(0, total_ref.shape[1], LANES):
            total_ref[:, at : at + LANES] = old_total_ref[:, at : at + LANES] * shrink
    for at, (piece, flag) in enumerate(zip(pieces, flags)):

        @pl.when(flag)
        def _(at=at, piece=piece):
            weights = jnp.exp(score_ref[at] - row_max)
            mass_ref[...] += weights
            weight_high = weights.astype(jnp.bfloat16)
            weight_low = (weights - weight_high.astype(jnp.float32)).astype(jnp.bfloat16)
            values = piece.values()
            added = jnp.dot(weight_high, values, preferred_element_type=jnp.float32)
            added = added + jnp.dot(weight_low, values, preferred_element_type=jnp.float32)
            total_ref[...] += added

    return row_max


def is_inner(mask):
    index = lax.axis_index("qry")
    return jnp.abs(index - lax.bitwise_xor(index, mask)) * 2 <= mask


def early_kernel(places, panel_mask, lists_ref, counts_ref, inner_ref, outer_ref, *refs):
    pieces, refs = read_pieces(places, refs, own=True)
    query_ref, total_ref, mass_ref, max_ref, score_ref = refs
    inner = is_inner(panel_mask)

    @pl.when(inner)
    def _():
        query_ref[...] = inner_ref[...]

    @pl.when(jnp.logical_not(inner))
    def _():
        query_ref[...] = outer_ref[...]

    row_max = attend(pieces, panel_mask, lists_ref, counts_ref, query_ref, score_ref, total_ref, mass_ref)
    max_ref[...] = jnp.broadcast_to(row_max, max_ref.shape)


def late_kernel(places, panel_mask, lists_ref, counts_ref, query_ref, *refs):
    before, refs = refs[:3], refs[3:]
    pieces, refs = read_pieces(places, refs)
    packed_ref, score_ref, total_ref, mass_ref = refs
    row_max = attend(pieces, panel_mask, lists_ref, counts_ref, query_ref, score_ref, total_ref, mass_ref, before)
    row_sum = jnp.sum(mass_ref[...], axis=1, keepdims=True)
    value_width = total_ref.shape[1]
    inverse = 1.0 / jnp.where(row_sum > 0.0, row_sum, 1.0)
    packed_ref[0:TILE, :] = (total_ref[...] * inverse).astype(jnp.bfloat16)
    row = lax.broadcasted_iota(jnp.int32, (EXTRA, LANES), 0)
    packed = jnp.zeros((EXTRA, LANES), jnp.float32)
    for first, column in ((0, row_max), (3, row_sum)):
        turned = jnp.transpose(jnp.broadcast_to(column, (TILE, LANES)))[0:EXTRA]
        for at, part in enumerate(split_three(turned)):
            packed = jnp.where(row == first + at, part.astype(jnp.float32), packed)
    packed_ref[TILE:, 0:LANES] = packed.astype(jnp.bfloat16)
    packed_ref[TILE:, LANES:] = jnp.zeros((EXTRA, value_width - LANES), jnp.bfloat16)


def home_kernel(places, lists_ref, counts_ref, query_ref, *refs):
    pieces, refs = read_pieces(places, refs, own=True)
    total_ref, stats_ref, score_ref, mass_ref = refs
    row_max = attend(pieces, 0, lists_ref, counts_ref, query_ref, score_ref, total_ref, mass_ref)
    row_sum = jnp.sum(mass_ref[...], axis=1, keepdims=True)
    stats_ref[0] = jnp.broadcast_to(row_max, (TILE, LANES))
    stats_ref[1] = jnp.broadcast_to(row_sum, (TILE, LANES))


def merge_kernel(total_ref, stats_ref, *refs):
    packed_refs, out_ref = refs[:-1], refs[-1]
    maxima = [stats_ref[0]]
    sums = [stats_ref[1]]
    for packed_ref in packed_refs:
        packed = packed_ref[TILE:, 0:LANES].astype(jnp.float32)
        for first, kept in ((0, maxima), (3, sums)):
            line = packed[first : first + 1] + packed[first + 1 : first + 2] + packed[first + 2 : first + 3]
            kept.append(jnp.transpose(jnp.broadcast_to(line, (TILE, LANES))))
    top = functools.reduce(jnp.maximum, maxima)
    factors = [jnp.exp(row_max - top) for row_max in maxima]
    masses = [factor * row_sum for factor, row_sum in zip(factors, sums)]
    inverse = 1.0 / functools.reduce(jnp.add, masses)
    scales = [factors[0] * inverse] + [mass * inverse for mass in masses[1:]]
    for at in range(0, total_ref.shape[1], LANES):
        merged = total_ref[:, at : at + LANES] * scales[0]
        for packed_ref, scale in zip(packed_refs, scales[1:]):
            merged = merged + packed_ref[0:TILE, at : at + LANES].astype(jnp.float32) * scale
        out_ref[:, at : at + LANES] = merged.astype(jnp.bfloat16)


def gather_library(keys, values, queries, masks):
    steps = [("qry", 1)]
    mask = lax.axis_size("lib") // 2
    while mask > 1:
        steps.append(("lib", mask))
        mask //= 2
    leaving, _ = tie(queries, values)
    inner = [swap_some(leaving, "qry", mask, True) for mask in masks]
    early, late = [], []
    for axis, mask in steps:
        place = (0, mask) if axis == "qry" else (mask, 0)
        near = (place, swap(keys, axis, mask), swap(values, axis, mask))
        relayed = []
        for (lib_mask, qry_mask), far_keys, far_values in early + late:
            far_keys, *_ = tie(far_keys, near[1], values)
            far_values, _ = tie(far_values, near[2])
            place = (lib_mask | mask, qry_mask)
            relayed.append((place, swap(far_keys, axis, mask), swap(far_values, axis, mask)))
        early, late = early + late + [near], relayed
    leaving, _ = tie(queries, early[0][1])
    outer = [swap_some(leaving, "qry", mask, False) for mask in masks]
    return early, late, list(zip(masks, inner, outer))


def cross_cores(pieces, arrivals=()):
    crossed = []
    for (lib_mask, qry_mask), *pair in pieces:
        pair = tie(*pair, *arrivals)[:2]
        crossed.append(((lib_mask | 1, qry_mask), *(swap(array, "lib", 1) for array in pair)))
    return crossed


def places_of(pieces):
    return [piece[0] for piece in pieces]


def arrays_of(pieces):
    return [array for piece in pieces for array in piece[1:]]


def body(queries, library_keys, library_values, key_scale, block_list, block_count):
    qry_count = lax.axis_size("qry")
    width = library_keys.shape[1]
    value_width = library_values.shape[1]

    partner_keys = swap(library_keys, "lib", 1)
    own_values, _ = tie(library_values, partner_keys)
    values = pl.pallas_call(
        pack_kernel,
        out_shape=jax.ShapeDtypeStruct((TILE + EXTRA, value_width), jnp.bfloat16),
        in_specs=[pl.BlockSpec(memory_space=pl.ANY)] * 2,
        out_specs=VMEM,
        scratch_shapes=[pltpu.VMEM((1, TILE), jnp.bfloat16), pltpu.SemaphoreType.DMA((2,))],
        compiler_params=params(),
    )(own_values, key_scale.reshape(1, TILE))

    masks = [2 * at + 1 for at in range(1, qry_count // 2)]
    early, relayed, visitors = gather_library(library_keys, values, queries, masks)
    piece_rows = (width // value_width + 1) * TILE + EXTRA
    cost = pl.CostEstimate(flops=2 * TILE * 4 * TILE * width * 2, bytes_accessed=4 * 1024 * 1024, transcendentals=0)
    total_shape = jax.ShapeDtypeStruct((TILE, value_width), jnp.float32)
    line_shape = jax.ShapeDtypeStruct((TILE, LANES), jnp.float32)
    pieces_total = 2 * (1 + len(early) + len(relayed))
    attend_params = params(pieces_total * piece_rows * value_width * 2)
    own_specs = [pl.BlockSpec(memory_space=pl.ANY), VMEM]
    own_scratch = [pltpu.VMEM(library_keys.shape, library_keys.dtype), pltpu.SemaphoreType.DMA]
    early_arrays = arrays_of(early)
    states = []
    for mask, inner, outer in visitors:
        state = pl.pallas_call(
            functools.partial(early_kernel, places_of(early), mask),
            out_shape=(jax.ShapeDtypeStruct(queries.shape, queries.dtype), total_shape, line_shape, line_shape),
            in_specs=[SMEM, SMEM] + [VMEM] * (2 + len(early_arrays)) + own_specs,
            out_specs=(VMEM,) * 4,
            scratch_shapes=[pltpu.VMEM((len(early) + 1, TILE, TILE), jnp.float32)] + own_scratch,
            compiler_params=attend_params,
            cost_estimate=cost,
        )(block_list, block_count, inner, outer, *early_arrays, library_keys, values)
        states.append(state)

    late = [((1, 0), partner_keys, swap(values, "lib", 1))] + cross_cores(early) + relayed + cross_cores(relayed, [state[3] for state in states])
    late_arrays = arrays_of(late)
    returned = []
    for (mask, *_), state in zip(visitors, states):
        packed = pl.pallas_call(
            functools.partial(late_kernel, places_of(late), mask),
            out_shape=jax.ShapeDtypeStruct((TILE + EXTRA, value_width), jnp.bfloat16),
            in_specs=[SMEM, SMEM] + [VMEM] * (4 + len(late_arrays)),
            out_specs=VMEM,
            scratch_shapes=[
                pltpu.VMEM((len(late), TILE, TILE), jnp.float32),
                pltpu.VMEM((TILE, value_width), jnp.float32),
                pltpu.VMEM((TILE, TILE), jnp.float32),
            ],
            compiler_params=attend_params,
            cost_estimate=cost,
        )(block_list, block_count, *state, *late_arrays)
        returned.append(swap(packed, "qry", mask))

    total, stats = pl.pallas_call(
        functools.partial(home_kernel, places_of(early + late)),
        out_shape=(total_shape, jax.ShapeDtypeStruct((2, TILE, LANES), jnp.float32)),
        in_specs=[SMEM, SMEM] + [VMEM] * (1 + len(early_arrays) + len(late_arrays)) + own_specs,
        out_specs=(VMEM, VMEM),
        scratch_shapes=[
            pltpu.VMEM((pieces_total, TILE, TILE), jnp.float32),
            pltpu.VMEM((TILE, TILE), jnp.float32),
        ]
        + own_scratch,
        compiler_params=attend_params,
        cost_estimate=cost,
    )(block_list, block_count, queries, *early_arrays, *late_arrays, library_keys, values)

    return pl.pallas_call(
        merge_kernel,
        out_shape=jax.ShapeDtypeStruct((TILE, value_width), jnp.bfloat16),
        in_specs=[VMEM] * (2 + len(returned)),
        out_specs=VMEM,
        compiler_params=params(),
    )(total, stats, *returned)


def solution(mesh):
    in_specs = (
        P(("groups", "lib", "qry"), None),
        P(("groups", "lib", "qry"), None),
        P(("groups", "lib", "qry"), None),
        P(("groups", "lib", "qry")),
        P("groups", None),
        P("groups"),
    )
    out_specs = P(("groups", "lib", "qry"), None)
    return jax.shard_map(body, mesh=mesh, in_specs=in_specs, out_specs=out_specs, check_vma=False)
```

```python
import functools
import math

import jax
import jax.numpy as jnp
from jax import lax
from jax.experimental import pallas as pl
from jax.experimental.pallas import tpu as pltpu
from jax.sharding import PartitionSpec as P

TILE = 128
LANES = 128
EXTRA = 16
MASKED_SCORE = -1e30
SMEM = pl.BlockSpec(memory_space=pltpu.SMEM)
VMEM = pl.BlockSpec(memory_space=pltpu.VMEM)


def params(operand_bytes=0):
    return pltpu.CompilerParams(vmem_limit_bytes=operand_bytes * 3 // 2 + 6 * 1024 * 1024)


def swap(value, axis, mask):
    length = lax.axis_size(axis)
    return lax.ppermute(value, axis, [(i, i ^ mask) for i in range(length)])


def tie(*values):
    return lax.optimization_barrier(values)


def split_three(value):
    high = value.astype(jnp.bfloat16)
    rest = value - high.astype(jnp.float32)
    middle = rest.astype(jnp.bfloat16)
    low = (rest - middle.astype(jnp.float32)).astype(jnp.bfloat16)
    return high, middle, low


def pack_kernel(values_ref, scale_ref, packed_ref, row_ref, sems):
    value_width = values_ref.shape[1]
    copies = (
        pltpu.make_async_copy(values_ref, packed_ref.at[pl.ds(0, TILE)], sems.at[0]),
        pltpu.make_async_copy(scale_ref, row_ref, sems.at[1]),
    )
    for copy in copies:
        copy.start()
    packed_ref[TILE:, TILE:] = jnp.zeros((EXTRA, value_width - TILE), jnp.bfloat16)
    for copy in reversed(copies):
        copy.wait()
    row = row_ref[...].astype(jnp.float32)
    packed_ref[TILE:, 0:TILE] = jnp.broadcast_to(row, (EXTRA, TILE)).astype(jnp.bfloat16)


class Piece:
    def __init__(self, place, keys_ref, values_ref, copy=None):
        self.place = place
        self.refs = (keys_ref, values_ref)
        self.copy = copy

    def scores(self, query_ref, inverse_root):
        keys_ref, values_ref = self.refs
        product = lax.dot_general(
            query_ref[...], keys_ref[...], (((1,), (1,)), ((), ())), preferred_element_type=jnp.float32
        )
        scale = values_ref[TILE : TILE + EXTRA, 0:TILE]
        return product * (scale.astype(jnp.float32)[0:1] * inverse_root)

    def values(self):
        return self.refs[1][0:TILE, :]


def read_pieces(places, refs, own=None):
    pieces = [Piece(place, refs[2 * at], refs[2 * at + 1]) for at, place in enumerate(places)]
    refs = refs[2 * len(places) :]
    if own is not None:
        keys_ref, values_ref, *refs, held_ref, sem = refs
        copy = pltpu.make_async_copy(keys_ref, held_ref, sem)
        copy.start()
        pieces.append(Piece((0, 0), held_ref, values_ref, copy))
    return pieces, refs


def attend(pieces, panel_mask, lists_ref, counts_ref, query_ref, score_ref, total_ref, mass_ref, before=None):
    lib_index = lax.axis_index("lib")
    qry_index = lax.axis_index("qry")
    qry_count = lax.axis_size("qry")
    block_total = lax.axis_size("lib") * qry_count
    panel = lib_index * qry_count + lax.bitwise_xor(qry_index, panel_mask)
    first = lists_ref[panel, 0]
    count = counts_ref[panel]
    width = query_ref.shape[1]
    inverse_root = 1.0 / math.sqrt(width)

    def active(lib_mask, qry_mask):
        block = lax.bitwise_xor(lib_index, lib_mask) * qry_count + lax.bitwise_xor(qry_index, qry_mask)
        return lax.rem(block - first + block_total, block_total) < count

    flags = [active(*piece.place) for piece in pieces]
    score_ref[...] = jnp.full(score_ref.shape, MASKED_SCORE, jnp.float32)
    for at, (piece, flag) in enumerate(zip(pieces, flags)):
        if piece.copy is not None:
            piece.copy.wait()

        @pl.when(flag)
        def _(at=at, piece=piece):
            score_ref[at] = piece.scores(query_ref, inverse_root)

    largest = score_ref[0]
    for at in range(1, len(flags)):
        largest = jnp.maximum(largest, score_ref[at])
    row_max = jnp.max(largest, axis=1, keepdims=True)
    if before is None:
        total_ref[...] = jnp.zeros(total_ref.shape, jnp.float32)
        mass_ref[...] = jnp.zeros(mass_ref.shape, jnp.float32)
    else:
        old_total_ref, old_mass_ref, old_max_ref = before
        old_max = old_max_ref[...]
        new_max = jnp.maximum(old_max, row_max)
        shrink = jnp.exp(old_max - new_max)
        row_max = new_max[:, 0:1]
        mass_ref[...] = old_mass_ref[...] * shrink
        for at in range(0, total_ref.shape[1], LANES):
            total_ref[:, at : at + LANES] = old_total_ref[:, at : at + LANES] * shrink
    for at, (piece, flag) in enumerate(zip(pieces, flags)):

        @pl.when(flag)
        def _(at=at, piece=piece):
            weights = jnp.exp(score_ref[at] - row_max)
            mass_ref[...] += weights
            weight_high = weights.astype(jnp.bfloat16)
            weight_low = (weights - weight_high.astype(jnp.float32)).astype(jnp.bfloat16)
            values = piece.values()
            added = jnp.dot(weight_high, values, preferred_element_type=jnp.float32)
            added = added + jnp.dot(weight_low, values, preferred_element_type=jnp.float32)
            total_ref[...] += added

    return row_max


def early_kernel(places, panel_mask, lists_ref, counts_ref, query_ref, *refs):
    pieces, refs = read_pieces(places, refs, own=True)
    total_ref, mass_ref, max_ref, score_ref = refs
    row_max = attend(pieces, panel_mask, lists_ref, counts_ref, query_ref, score_ref, total_ref, mass_ref)
    max_ref[...] = jnp.broadcast_to(row_max, max_ref.shape)


def late_kernel(places, panel_mask, lists_ref, counts_ref, query_ref, *refs):
    before, refs = refs[:3], refs[3:]
    pieces, refs = read_pieces(places, refs)
    packed_ref, score_ref, total_ref, mass_ref = refs
    row_max = attend(pieces, panel_mask, lists_ref, counts_ref, query_ref, score_ref, total_ref, mass_ref, before)
    row_sum = jnp.sum(mass_ref[...], axis=1, keepdims=True)
    value_width = total_ref.shape[1]
    inverse = 1.0 / jnp.where(row_sum > 0.0, row_sum, 1.0)
    packed_ref[0:TILE, :] = (total_ref[...] * inverse).astype(jnp.bfloat16)
    row = lax.broadcasted_iota(jnp.int32, (EXTRA, LANES), 0)
    packed = jnp.zeros((EXTRA, LANES), jnp.float32)
    for first, column in ((0, row_max), (3, row_sum)):
        turned = jnp.transpose(jnp.broadcast_to(column, (TILE, LANES)))[0:EXTRA]
        for at, part in enumerate(split_three(turned)):
            packed = jnp.where(row == first + at, part.astype(jnp.float32), packed)
    packed_ref[TILE:, 0:LANES] = packed.astype(jnp.bfloat16)
    packed_ref[TILE:, LANES:] = jnp.zeros((EXTRA, value_width - LANES), jnp.bfloat16)


def home_kernel(places, lists_ref, counts_ref, query_ref, *refs):
    pieces, refs = read_pieces(places, refs, own=True)
    total_ref, stats_ref, score_ref, mass_ref = refs
    row_max = attend(pieces, 0, lists_ref, counts_ref, query_ref, score_ref, total_ref, mass_ref)
    row_sum = jnp.sum(mass_ref[...], axis=1, keepdims=True)
    stats_ref[0] = jnp.broadcast_to(row_max, (TILE, LANES))
    stats_ref[1] = jnp.broadcast_to(row_sum, (TILE, LANES))


def merge_kernel(total_ref, stats_ref, *refs):
    packed_refs, out_ref = refs[:-1], refs[-1]
    maxima = [stats_ref[0]]
    sums = [stats_ref[1]]
    for packed_ref in packed_refs:
        packed = packed_ref[TILE:, 0:LANES].astype(jnp.float32)
        for first, kept in ((0, maxima), (3, sums)):
            line = packed[first : first + 1] + packed[first + 1 : first + 2] + packed[first + 2 : first + 3]
            kept.append(jnp.transpose(jnp.broadcast_to(line, (TILE, LANES))))
    top = functools.reduce(jnp.maximum, maxima)
    factors = [jnp.exp(row_max - top) for row_max in maxima]
    masses = [factor * row_sum for factor, row_sum in zip(factors, sums)]
    inverse = 1.0 / functools.reduce(jnp.add, masses)
    scales = [factors[0] * inverse] + [mass * inverse for mass in masses[1:]]
    for at in range(0, total_ref.shape[1], LANES):
        merged = total_ref[:, at : at + LANES] * scales[0]
        for packed_ref, scale in zip(packed_refs, scales[1:]):
            merged = merged + packed_ref[0:TILE, at : at + LANES].astype(jnp.float32) * scale
        out_ref[:, at : at + LANES] = merged.astype(jnp.bfloat16)


def gather_library(keys, values, queries, masks):
    steps = [("qry", 1)]
    mask = lax.axis_size("lib") // 2
    while mask > 1:
        steps.append(("lib", mask))
        mask //= 2
    partner_values = swap(values, "lib", 1)
    leaving, _ = tie(queries, partner_values)
    visitors = [swap(leaving, "qry", mask) for mask in masks]
    early, late = [], []
    for axis, mask in steps:
        place = (0, mask) if axis == "qry" else (mask, 0)
        near = (place, swap(keys, axis, mask), swap(values, axis, mask))
        relayed = []
        for (lib_mask, qry_mask), far_keys, far_values in early + late:
            far_keys, *_ = tie(far_keys, near[1], values)
            far_values, _ = tie(far_values, near[2])
            place = (lib_mask | mask, qry_mask)
            relayed.append((place, swap(far_keys, axis, mask), swap(far_values, axis, mask)))
        early, late = early + late + [near], relayed
    return early, late, partner_values, list(zip(masks, visitors))


def cross_cores(pieces, arrivals=()):
    crossed = []
    for (lib_mask, qry_mask), *pair in pieces:
        pair = tie(*pair, *arrivals)[:2]
        crossed.append(((lib_mask | 1, qry_mask), *(swap(array, "lib", 1) for array in pair)))
    return crossed


def places_of(pieces):
    return [piece[0] for piece in pieces]


def arrays_of(pieces):
    return [array for piece in pieces for array in piece[1:]]


def body(queries, library_keys, library_values, key_scale, block_list, block_count):
    qry_count = lax.axis_size("qry")
    width = library_keys.shape[1]
    value_width = library_values.shape[1]

    partner_keys = swap(library_keys, "lib", 1)
    own_values, _ = tie(library_values, partner_keys)
    values = pl.pallas_call(
        pack_kernel,
        out_shape=jax.ShapeDtypeStruct((TILE + EXTRA, value_width), jnp.bfloat16),
        in_specs=[pl.BlockSpec(memory_space=pl.ANY)] * 2,
        out_specs=VMEM,
        scratch_shapes=[pltpu.VMEM((1, TILE), jnp.bfloat16), pltpu.SemaphoreType.DMA((2,))],
        compiler_params=params(),
    )(own_values, key_scale.reshape(1, TILE))

    masks = [2 * at + 1 for at in range(1, qry_count // 2)]
    early, relayed, partner_values, visitors = gather_library(library_keys, values, queries, masks)
    piece_rows = (width // value_width + 1) * TILE + EXTRA
    cost = pl.CostEstimate(flops=2 * TILE * 4 * TILE * width * 2, bytes_accessed=4 * 1024 * 1024, transcendentals=0)
    total_shape = jax.ShapeDtypeStruct((TILE, value_width), jnp.float32)
    line_shape = jax.ShapeDtypeStruct((TILE, LANES), jnp.float32)
    pieces_total = 2 * (1 + len(early) + len(relayed))
    attend_params = params(pieces_total * piece_rows * value_width * 2)
    own_specs = [pl.BlockSpec(memory_space=pl.ANY), VMEM]
    own_scratch = [pltpu.VMEM(library_keys.shape, library_keys.dtype), pltpu.SemaphoreType.DMA]
    early_arrays = arrays_of(early)
    states = []
    for mask, visiting in visitors:
        state = pl.pallas_call(
            functools.partial(early_kernel, places_of(early), mask),
            out_shape=(total_shape, line_shape, line_shape),
            in_specs=[SMEM, SMEM] + [VMEM] * (1 + len(early_arrays)) + own_specs,
            out_specs=(VMEM,) * 3,
            scratch_shapes=[pltpu.VMEM((len(early) + 1, TILE, TILE), jnp.float32)] + own_scratch,
            compiler_params=attend_params,
            cost_estimate=cost,
        )(block_list, block_count, visiting, *early_arrays, library_keys, values)
        states.append(state)

    late = [((1, 0), partner_keys, partner_values)] + cross_cores(early) + relayed + cross_cores(relayed, [state[2] for state in states])
    late_arrays = arrays_of(late)
    returned = []
    for (mask, visiting), state in zip(visitors, states):
        packed = pl.pallas_call(
            functools.partial(late_kernel, places_of(late), mask),
            out_shape=jax.ShapeDtypeStruct((TILE + EXTRA, value_width), jnp.bfloat16),
            in_specs=[SMEM, SMEM] + [VMEM] * (4 + len(late_arrays)),
            out_specs=VMEM,
            scratch_shapes=[
                pltpu.VMEM((len(late), TILE, TILE), jnp.float32),
                pltpu.VMEM((TILE, value_width), jnp.float32),
                pltpu.VMEM((TILE, TILE), jnp.float32),
            ],
            compiler_params=attend_params,
            cost_estimate=cost,
        )(block_list, block_count, visiting, *state, *late_arrays)
        returned.append(swap(packed, "qry", mask))

    total, stats = pl.pallas_call(
        functools.partial(home_kernel, places_of(early + late)),
        out_shape=(total_shape, jax.ShapeDtypeStruct((2, TILE, LANES), jnp.float32)),
        in_specs=[SMEM, SMEM] + [VMEM] * (1 + len(early_arrays) + len(late_arrays)) + own_specs,
        out_specs=(VMEM, VMEM),
        scratch_shapes=[
            pltpu.VMEM((pieces_total, TILE, TILE), jnp.float32),
            pltpu.VMEM((TILE, TILE), jnp.float32),
        ]
        + own_scratch,
        compiler_params=attend_params,
        cost_estimate=cost,
    )(block_list, block_count, queries, *early_arrays, *late_arrays, library_keys, values)

    return pl.pallas_call(
        merge_kernel,
        out_shape=jax.ShapeDtypeStruct((TILE, value_width), jnp.bfloat16),
        in_specs=[VMEM] * (2 + len(returned)),
        out_specs=VMEM,
        compiler_params=params(),
    )(total, stats, *returned)


def solution(mesh):
    in_specs = (
        P(("groups", "lib", "qry"), None),
        P(("groups", "lib", "qry"), None),
        P(("groups", "lib", "qry"), None),
        P(("groups", "lib", "qry")),
        P("groups", None),
        P("groups"),
    )
    out_specs = P(("groups", "lib", "qry"), None)
    return jax.shard_map(body, mesh=mesh, in_specs=in_specs, out_specs=out_specs, check_vma=False)
```

```python
import functools
import math

import jax
import jax.numpy as jnp
from jax import lax
from jax.experimental import pallas as pl
from jax.experimental.pallas import tpu as pltpu
from jax.sharding import PartitionSpec as P

TILE = 128
LANES = 128
EXTRA = 16
SUBLANES = 8
MASKED_SCORE = -1e30
SMEM = pl.BlockSpec(memory_space=pltpu.SMEM)
VMEM = pl.BlockSpec(memory_space=pltpu.VMEM)


def params(operand_bytes=0):
    return pltpu.CompilerParams(vmem_limit_bytes=operand_bytes * 3 // 2 + 6 * 1024 * 1024)


def swap(value, axis, mask):
    length = lax.axis_size(axis)
    return lax.ppermute(value, axis, [(i, i ^ mask) for i in range(length)])


def tie(*values):
    return lax.optimization_barrier(values)


def pack_kernel(values_ref, scale_ref, packed_ref, row_ref, sems):
    value_width = values_ref.shape[1]
    copies = (
        pltpu.make_async_copy(values_ref, packed_ref.at[pl.ds(0, TILE)], sems.at[0]),
        pltpu.make_async_copy(scale_ref, row_ref, sems.at[1]),
    )
    for copy in copies:
        copy.start()
    packed_ref[TILE:, TILE:] = jnp.zeros((EXTRA, value_width - TILE), jnp.bfloat16)
    for copy in reversed(copies):
        copy.wait()
    row = row_ref[...].astype(jnp.float32)
    packed_ref[TILE:, 0:TILE] = jnp.broadcast_to(row, (EXTRA, TILE)).astype(jnp.bfloat16)


class Piece:
    def __init__(self, place, keys_ref, values_ref, copy=None):
        self.place = place
        self.refs = (keys_ref, values_ref)
        self.copy = copy

    def scores(self, query_ref, inverse_root):
        keys_ref, values_ref = self.refs
        product = lax.dot_general(
            query_ref[...], keys_ref[...], (((1,), (1,)), ((), ())), preferred_element_type=jnp.float32
        )
        scale = values_ref[TILE : TILE + EXTRA, 0:TILE]
        return product * (scale.astype(jnp.float32)[0:1] * inverse_root)

    def values(self):
        return self.refs[1][0:TILE, :]


def read_pieces(places, refs, own=None):
    pieces = [Piece(place, refs[2 * at], refs[2 * at + 1]) for at, place in enumerate(places)]
    refs = refs[2 * len(places) :]
    if own is not None:
        keys_ref, values_ref, *refs, held_ref, sem = refs
        copy = pltpu.make_async_copy(keys_ref, held_ref, sem)
        copy.start()
        pieces.append(Piece((0, 0), held_ref, values_ref, copy))
    return pieces, refs


def attend(pieces, panel_mask, lists_ref, counts_ref, query_ref, score_ref, total_ref, mass_ref, before=None):
    lib_index = lax.axis_index("lib")
    qry_index = lax.axis_index("qry")
    qry_count = lax.axis_size("qry")
    block_total = lax.axis_size("lib") * qry_count
    panel = lib_index * qry_count + lax.bitwise_xor(qry_index, panel_mask)
    first = lists_ref[panel, 0]
    count = counts_ref[panel]
    width = query_ref.shape[1]
    inverse_root = 1.0 / math.sqrt(width)

    def active(lib_mask, qry_mask):
        block = lax.bitwise_xor(lib_index, lib_mask) * qry_count + lax.bitwise_xor(qry_index, qry_mask)
        return lax.rem(block - first + block_total, block_total) < count

    flags = [active(*piece.place) for piece in pieces]
    score_ref[...] = jnp.full(score_ref.shape, MASKED_SCORE, jnp.float32)
    for at, (piece, flag) in enumerate(zip(pieces, flags)):
        if piece.copy is not None:
            piece.copy.wait()

        @pl.when(flag)
        def _(at=at, piece=piece):
            score_ref[at] = piece.scores(query_ref, inverse_root)

    largest = score_ref[0]
    for at in range(1, len(flags)):
        largest = jnp.maximum(largest, score_ref[at])
    row_max = jnp.max(largest, axis=1, keepdims=True)
    if before is None:
        total_ref[...] = jnp.zeros(total_ref.shape, jnp.float32)
        mass_ref[...] = jnp.zeros(mass_ref.shape, jnp.float32)
    else:
        old_total_ref, old_mass_ref, old_max_ref = before
        old_max = old_max_ref[...]
        new_max = jnp.maximum(old_max, row_max)
        shrink = jnp.exp(old_max - new_max)
        row_max = new_max[:, 0:1]
        mass_ref[...] = old_mass_ref[...] * shrink
        for at in range(0, total_ref.shape[1], LANES):
            total_ref[:, at : at + LANES] = old_total_ref[:, at : at + LANES] * shrink
    for at, (piece, flag) in enumerate(zip(pieces, flags)):

        @pl.when(flag)
        def _(at=at, piece=piece):
            weights = jnp.exp(score_ref[at] - row_max)
            mass_ref[...] += weights
            weight_high = weights.astype(jnp.bfloat16)
            weight_low = (weights - weight_high.astype(jnp.float32)).astype(jnp.bfloat16)
            values = piece.values()
            stacked = jnp.concatenate([weight_high, weight_low], axis=0)
            added = jnp.dot(stacked, values, preferred_element_type=jnp.float32)
            total_ref[...] += added[0:TILE] + added[TILE:]

    return row_max


def early_kernel(places, panel_mask, lists_ref, counts_ref, query_ref, *refs):
    pieces, refs = read_pieces(places, refs, own=True)
    total_ref, mass_ref, max_ref, score_ref = refs
    row_max = attend(pieces, panel_mask, lists_ref, counts_ref, query_ref, score_ref, total_ref, mass_ref)
    max_ref[...] = jnp.broadcast_to(row_max, max_ref.shape)


def late_kernel(places, panel_mask, lists_ref, counts_ref, query_ref, *refs):
    before, refs = refs[:3], refs[3:]
    pieces, refs = read_pieces(places, refs)
    partial_ref, lines_ref, score_ref, total_ref, mass_ref = refs
    row_max = attend(pieces, panel_mask, lists_ref, counts_ref, query_ref, score_ref, total_ref, mass_ref, before)
    row_sum = jnp.sum(mass_ref[...], axis=1, keepdims=True)
    inverse = 1.0 / jnp.where(row_sum > 0.0, row_sum, 1.0)
    partial_ref[...] = (total_ref[...] * inverse).astype(jnp.bfloat16)
    lane = lax.broadcasted_iota(jnp.int32, (TILE, LANES), 1)
    lines_ref[...] = jnp.transpose(jnp.where(lane == 0, row_max, row_sum))[0:SUBLANES]


def home_kernel(places, lists_ref, counts_ref, query_ref, *refs):
    pieces, refs = read_pieces(places, refs, own=True)
    total_ref, stats_ref, score_ref, mass_ref = refs
    row_max = attend(pieces, 0, lists_ref, counts_ref, query_ref, score_ref, total_ref, mass_ref)
    row_sum = jnp.sum(mass_ref[...], axis=1, keepdims=True)
    stats_ref[0] = jnp.broadcast_to(row_max, (TILE, LANES))
    stats_ref[1] = jnp.broadcast_to(row_sum, (TILE, LANES))


def merge_kernel(total_ref, stats_ref, *refs):
    returned, out_ref = refs[:-1], refs[-1]
    partial_refs, lines_refs = returned[0::2], returned[1::2]
    maxima = [stats_ref[0]]
    sums = [stats_ref[1]]
    for lines_ref in lines_refs:
        turned = jnp.transpose(jnp.concatenate([lines_ref[...]] * (TILE // SUBLANES), axis=0))
        maxima.append(jnp.broadcast_to(turned[:, 0:1], (TILE, LANES)))
        sums.append(jnp.broadcast_to(turned[:, 1:2], (TILE, LANES)))
    top = functools.reduce(jnp.maximum, maxima)
    factors = [jnp.exp(row_max - top) for row_max in maxima]
    masses = [factor * row_sum for factor, row_sum in zip(factors, sums)]
    inverse = 1.0 / functools.reduce(jnp.add, masses)
    shares = [factors[0] * inverse] + [mass * inverse for mass in masses[1:]]
    for at in range(0, total_ref.shape[1], LANES):
        merged = total_ref[:, at : at + LANES] * shares[0]
        for partial_ref, share in zip(partial_refs, shares[1:]):
            merged = merged + partial_ref[:, at : at + LANES].astype(jnp.float32) * share
        out_ref[:, at : at + LANES] = merged.astype(jnp.bfloat16)


def gather_library(keys, values, queries, masks):
    steps = [("qry", 1)]
    mask = lax.axis_size("lib") // 2
    while mask > 1:
        steps.append(("lib", mask))
        mask //= 2
    partner_values = swap(values, "lib", 1)
    leaving, _ = tie(queries, partner_values)
    visitors = [swap(leaving, "qry", mask) for mask in masks]
    early, late = [], []
    for axis, mask in steps:
        place = (0, mask) if axis == "qry" else (mask, 0)
        near = (place, swap(keys, axis, mask), swap(values, axis, mask))
        relayed = []
        for (lib_mask, qry_mask), far_keys, far_values in early + late:
            far_keys, *_ = tie(far_keys, near[1], values)
            far_values, _ = tie(far_values, near[2])
            place = (lib_mask | mask, qry_mask)
            relayed.append((place, swap(far_keys, axis, mask), swap(far_values, axis, mask)))
        early, late = early + late + [near], relayed
    return early, late, partner_values, list(zip(masks, visitors))


def cross_cores(pieces, arrivals=()):
    crossed = []
    for (lib_mask, qry_mask), *pair in pieces:
        pair = tie(*pair, *arrivals)[:2]
        crossed.append(((lib_mask | 1, qry_mask), *(swap(array, "lib", 1) for array in pair)))
    return crossed


def places_of(pieces):
    return [piece[0] for piece in pieces]


def arrays_of(pieces):
    return [array for piece in pieces for array in piece[1:]]


def body(queries, library_keys, library_values, key_scale, block_list, block_count):
    qry_count = lax.axis_size("qry")
    width = library_keys.shape[1]
    value_width = library_values.shape[1]

    partner_keys = swap(library_keys, "lib", 1)
    own_values, _ = tie(library_values, partner_keys)
    values = pl.pallas_call(
        pack_kernel,
        out_shape=jax.ShapeDtypeStruct((TILE + EXTRA, value_width), jnp.bfloat16),
        in_specs=[pl.BlockSpec(memory_space=pl.ANY)] * 2,
        out_specs=VMEM,
        scratch_shapes=[pltpu.VMEM((1, TILE), jnp.bfloat16), pltpu.SemaphoreType.DMA((2,))],
        compiler_params=params(),
    )(own_values, key_scale.reshape(1, TILE))

    masks = [2 * at + 1 for at in range(1, qry_count // 2)]
    early, relayed, partner_values, visitors = gather_library(library_keys, values, queries, masks)
    piece_rows = (width // value_width + 1) * TILE + EXTRA
    cost = pl.CostEstimate(flops=2 * TILE * 4 * TILE * width * 2, bytes_accessed=4 * 1024 * 1024, transcendentals=0)
    total_shape = jax.ShapeDtypeStruct((TILE, value_width), jnp.float32)
    line_shape = jax.ShapeDtypeStruct((TILE, LANES), jnp.float32)
    pieces_total = 2 * (1 + len(early) + len(relayed))
    attend_params = params(pieces_total * piece_rows * value_width * 2)
    own_specs = [pl.BlockSpec(memory_space=pl.ANY), VMEM]
    own_scratch = [pltpu.VMEM(library_keys.shape, library_keys.dtype), pltpu.SemaphoreType.DMA]
    early = early + [((1, 0), partner_keys, partner_values)]
    early_arrays = arrays_of(early)
    states = []
    for mask, visiting in visitors:
        state = pl.pallas_call(
            functools.partial(early_kernel, places_of(early), mask),
            out_shape=(total_shape, line_shape, line_shape),
            in_specs=[SMEM, SMEM] + [VMEM] * (1 + len(early_arrays)) + own_specs,
            out_specs=(VMEM,) * 3,
            scratch_shapes=[pltpu.VMEM((len(early) + 1, TILE, TILE), jnp.float32)] + own_scratch,
            compiler_params=attend_params,
            cost_estimate=cost,
        )(block_list, block_count, visiting, *early_arrays, library_keys, values)
        states.append(state)

    late = cross_cores(early[:-1]) + relayed + cross_cores(relayed, [state[2] for state in states])
    late_arrays = arrays_of(late)
    returned = []
    for (mask, visiting), state in zip(visitors, states):
        partial, lines = pl.pallas_call(
            functools.partial(late_kernel, places_of(late), mask),
            out_shape=(
                jax.ShapeDtypeStruct((TILE, value_width), jnp.bfloat16),
                jax.ShapeDtypeStruct((SUBLANES, LANES), jnp.float32),
            ),
            in_specs=[SMEM, SMEM] + [VMEM] * (4 + len(late_arrays)),
            out_specs=(VMEM, VMEM),
            scratch_shapes=[
                pltpu.VMEM((len(late), TILE, TILE), jnp.float32),
                pltpu.VMEM((TILE, value_width), jnp.float32),
                pltpu.VMEM((TILE, TILE), jnp.float32),
            ],
            compiler_params=attend_params,
            cost_estimate=cost,
        )(block_list, block_count, visiting, *state, *late_arrays)
        returned += [swap(partial, "qry", mask), swap(lines, "qry", mask)]

    total, stats = pl.pallas_call(
        functools.partial(home_kernel, places_of(early + late)),
        out_shape=(total_shape, jax.ShapeDtypeStruct((2, TILE, LANES), jnp.float32)),
        in_specs=[SMEM, SMEM] + [VMEM] * (1 + len(early_arrays) + len(late_arrays)) + own_specs,
        out_specs=(VMEM, VMEM),
        scratch_shapes=[
            pltpu.VMEM((pieces_total, TILE, TILE), jnp.float32),
            pltpu.VMEM((TILE, TILE), jnp.float32),
        ]
        + own_scratch,
        compiler_params=attend_params,
        cost_estimate=cost,
    )(block_list, block_count, queries, *early_arrays, *late_arrays, library_keys, values)

    return pl.pallas_call(
        merge_kernel,
        out_shape=jax.ShapeDtypeStruct((TILE, value_width), jnp.bfloat16),
        in_specs=[VMEM] * (2 + len(returned)),
        out_specs=VMEM,
        compiler_params=params(),
    )(total, stats, *returned)


def solution(mesh):
    in_specs = (
        P(("groups", "lib", "qry"), None),
        P(("groups", "lib", "qry"), None),
        P(("groups", "lib", "qry"), None),
        P(("groups", "lib", "qry")),
        P("groups", None),
        P("groups"),
    )
    out_specs = P(("groups", "lib", "qry"), None)
    return jax.shard_map(body, mesh=mesh, in_specs=in_specs, out_specs=out_specs, check_vma=False)
```

```python
import functools
import math

import jax
import jax.numpy as jnp
from jax import lax
from jax.experimental import pallas as pl
from jax.experimental.pallas import tpu as pltpu
from jax.sharding import PartitionSpec as P

TILE = 128
LANES = 128
EXTRA = 16
MASKED_SCORE = -1e30
VMEM = pl.BlockSpec(memory_space=pltpu.VMEM)


def params(operand_bytes=0):
    return pltpu.CompilerParams(vmem_limit_bytes=operand_bytes * 3 // 2 + 6 * 1024 * 1024)


def swap(value, axis, mask):
    length = lax.axis_size(axis)
    return lax.ppermute(value, axis, [(i, i ^ mask) for i in range(length)])


def tie(*values):
    return lax.optimization_barrier(values)


def split_three(value):
    high = value.astype(jnp.bfloat16)
    rest = value - high.astype(jnp.float32)
    middle = rest.astype(jnp.bfloat16)
    low = (rest - middle.astype(jnp.float32)).astype(jnp.bfloat16)
    return high, middle, low


def pack_kernel(values_ref, scale_ref, packed_ref, row_ref, sems):
    value_width = values_ref.shape[1]
    copies = (
        pltpu.make_async_copy(values_ref, packed_ref.at[pl.ds(0, TILE)], sems.at[0]),
        pltpu.make_async_copy(scale_ref, row_ref, sems.at[1]),
    )
    for copy in copies:
        copy.start()
    packed_ref[TILE:, TILE:] = jnp.zeros((EXTRA, value_width - TILE), jnp.bfloat16)
    for copy in reversed(copies):
        copy.wait()
    row = row_ref[...].astype(jnp.float32)
    packed_ref[TILE:, 0:TILE] = jnp.broadcast_to(row, (EXTRA, TILE)).astype(jnp.bfloat16)


class Piece:
    def __init__(self, place, keys_ref, values_ref, copy=None):
        self.place = place
        self.refs = (keys_ref, values_ref)
        self.copy = copy

    def scores(self, query_ref, inverse_root):
        keys_ref, values_ref = self.refs
        product = lax.dot_general(
            query_ref[...], keys_ref[...], (((1,), (1,)), ((), ())), preferred_element_type=jnp.float32
        )
        scale = values_ref[TILE : TILE + EXTRA, 0:TILE]
        return product * (scale.astype(jnp.float32)[0:1] * inverse_root)

    def values(self):
        return self.refs[1][0:TILE, :]


def read_pieces(places, refs, own=None):
    pieces = [Piece(place, refs[2 * at], refs[2 * at + 1]) for at, place in enumerate(places)]
    refs = refs[2 * len(places) :]
    if own is not None:
        keys_ref, values_ref, *refs, held_ref, sem = refs
        copy = pltpu.make_async_copy(keys_ref, held_ref, sem)
        copy.start()
        pieces.append(Piece((0, 0), held_ref, values_ref, copy))
    return pieces, refs


def pick(ref, row, column):
    rows = lax.broadcasted_iota(jnp.int32, ref.shape, 0)
    columns = lax.broadcasted_iota(jnp.int32, ref.shape, 1)
    chosen = jnp.where((rows == row) & (columns == column), ref[...], 0)
    return jnp.sum(chosen.astype(jnp.float32)).astype(jnp.int32)


def attend(pieces, panel_mask, lists_ref, counts_ref, query_ref, score_ref, total_ref, mass_ref, before=None):
    lib_index = lax.axis_index("lib")
    qry_index = lax.axis_index("qry")
    qry_count = lax.axis_size("qry")
    block_total = lax.axis_size("lib") * qry_count
    panel = lib_index * qry_count + lax.bitwise_xor(qry_index, panel_mask)
    first = pick(lists_ref, 0, panel)
    count = pick(counts_ref, 0, panel)
    width = query_ref.shape[1]
    inverse_root = 1.0 / math.sqrt(width)

    def active(lib_mask, qry_mask):
        block = lax.bitwise_xor(lib_index, lib_mask) * qry_count + lax.bitwise_xor(qry_index, qry_mask)
        return lax.rem(block - first + block_total, block_total) < count

    flags = [active(*piece.place) for piece in pieces]
    score_ref[...] = jnp.full(score_ref.shape, MASKED_SCORE, jnp.float32)
    for at, (piece, flag) in enumerate(zip(pieces, flags)):
        if piece.copy is not None:
            piece.copy.wait()

        @pl.when(flag)
        def _(at=at, piece=piece):
            score_ref[at] = piece.scores(query_ref, inverse_root)

    largest = score_ref[0]
    for at in range(1, len(flags)):
        largest = jnp.maximum(largest, score_ref[at])
    row_max = jnp.max(largest, axis=1, keepdims=True)
    if before is None:
        total_ref[...] = jnp.zeros(total_ref.shape, jnp.float32)
        mass_ref[...] = jnp.zeros(mass_ref.shape, jnp.float32)
    else:
        old_total_ref, old_mass_ref, old_max_ref = before
        old_max = old_max_ref[...]
        new_max = jnp.maximum(old_max, row_max)
        shrink = jnp.exp(old_max - new_max)
        row_max = new_max[:, 0:1]
        mass_ref[...] = old_mass_ref[...] * shrink
        for at in range(0, total_ref.shape[1], LANES):
            total_ref[:, at : at + LANES] = old_total_ref[:, at : at + LANES] * shrink
    for at, (piece, flag) in enumerate(zip(pieces, flags)):

        @pl.when(flag)
        def _(at=at, piece=piece):
            weights = jnp.exp(score_ref[at] - row_max)
            mass_ref[...] += weights
            weight_high = weights.astype(jnp.bfloat16)
            weight_low = (weights - weight_high.astype(jnp.float32)).astype(jnp.bfloat16)
            values = piece.values()
            added = jnp.dot(weight_high, values, preferred_element_type=jnp.float32)
            added = added + jnp.dot(weight_low, values, preferred_element_type=jnp.float32)
            total_ref[...] += added

    return row_max


def early_kernel(places, panel_mask, lists_ref, counts_ref, query_ref, *refs):
    pieces, refs = read_pieces(places, refs, own=True)
    total_ref, mass_ref, max_ref, score_ref = refs
    row_max = attend(pieces, panel_mask, lists_ref, counts_ref, query_ref, score_ref, total_ref, mass_ref)
    max_ref[...] = jnp.broadcast_to(row_max, max_ref.shape)


def late_kernel(places, panel_mask, lists_ref, counts_ref, query_ref, *refs):
    before, refs = refs[:3], refs[3:]
    pieces, refs = read_pieces(places, refs)
    packed_ref, score_ref, total_ref, mass_ref = refs
    row_max = attend(pieces, panel_mask, lists_ref, counts_ref, query_ref, score_ref, total_ref, mass_ref, before)
    row_sum = jnp.sum(mass_ref[...], axis=1, keepdims=True)
    value_width = total_ref.shape[1]
    inverse = 1.0 / jnp.where(row_sum > 0.0, row_sum, 1.0)
    packed_ref[0:TILE, :] = (total_ref[...] * inverse).astype(jnp.bfloat16)
    row = lax.broadcasted_iota(jnp.int32, (EXTRA, LANES), 0)
    packed = jnp.zeros((EXTRA, LANES), jnp.float32)
    for first, column in ((0, row_max), (3, row_sum)):
        turned = jnp.transpose(jnp.broadcast_to(column, (TILE, LANES)))[0:EXTRA]
        for at, part in enumerate(split_three(turned)):
            packed = jnp.where(row == first + at, part.astype(jnp.float32), packed)
    packed_ref[TILE:, 0:LANES] = packed.astype(jnp.bfloat16)
    packed_ref[TILE:, LANES:] = jnp.zeros((EXTRA, value_width - LANES), jnp.bfloat16)


def home_kernel(places, lists_ref, counts_ref, query_ref, *refs):
    pieces, refs = read_pieces(places, refs, own=True)
    total_ref, stats_ref, score_ref, mass_ref = refs
    row_max = attend(pieces, 0, lists_ref, counts_ref, query_ref, score_ref, total_ref, mass_ref)
    row_sum = jnp.sum(mass_ref[...], axis=1, keepdims=True)
    stats_ref[0] = jnp.broadcast_to(row_max, (TILE, LANES))
    stats_ref[1] = jnp.broadcast_to(row_sum, (TILE, LANES))


def merge_kernel(total_ref, stats_ref, *refs):
    packed_refs, out_ref = refs[:-1], refs[-1]
    maxima = [stats_ref[0]]
    sums = [stats_ref[1]]
    for packed_ref in packed_refs:
        packed = packed_ref[TILE:, 0:LANES].astype(jnp.float32)
        for first, kept in ((0, maxima), (3, sums)):
            line = packed[first : first + 1] + packed[first + 1 : first + 2] + packed[first + 2 : first + 3]
            kept.append(jnp.transpose(jnp.broadcast_to(line, (TILE, LANES))))
    top = functools.reduce(jnp.maximum, maxima)
    factors = [jnp.exp(row_max - top) for row_max in maxima]
    masses = [factor * row_sum for factor, row_sum in zip(factors, sums)]
    inverse = 1.0 / functools.reduce(jnp.add, masses)
    scales = [factors[0] * inverse] + [mass * inverse for mass in masses[1:]]
    for at in range(0, total_ref.shape[1], LANES):
        merged = total_ref[:, at : at + LANES] * scales[0]
        for packed_ref, scale in zip(packed_refs, scales[1:]):
            merged = merged + packed_ref[0:TILE, at : at + LANES].astype(jnp.float32) * scale
        out_ref[:, at : at + LANES] = merged.astype(jnp.bfloat16)


def gather_library(keys, values, queries, masks):
    steps = [("qry", 1)]
    mask = lax.axis_size("lib") // 2
    while mask > 1:
        steps.append(("lib", mask))
        mask //= 2
    partner_values = swap(values, "lib", 1)
    leaving, _ = tie(queries, partner_values)
    visitors = [swap(leaving, "qry", mask) for mask in masks]
    early, late = [], []
    for axis, mask in steps:
        place = (0, mask) if axis == "qry" else (mask, 0)
        near = (place, swap(keys, axis, mask), swap(values, axis, mask))
        relayed = []
        for (lib_mask, qry_mask), far_keys, far_values in early + late:
            far_keys, *_ = tie(far_keys, near[1], values)
            far_values, _ = tie(far_values, near[2])
            place = (lib_mask | mask, qry_mask)
            relayed.append((place, swap(far_keys, axis, mask), swap(far_values, axis, mask)))
        early, late = early + late + [near], relayed
    return early, late, partner_values, list(zip(masks, visitors))


def cross_cores(pieces, arrivals=()):
    crossed = []
    for (lib_mask, qry_mask), *pair in pieces:
        pair = tie(*pair, *arrivals)[:2]
        crossed.append(((lib_mask | 1, qry_mask), *(swap(array, "lib", 1) for array in pair)))
    return crossed


def places_of(pieces):
    return [piece[0] for piece in pieces]


def arrays_of(pieces):
    return [array for piece in pieces for array in piece[1:]]


def body(queries, library_keys, library_values, key_scale, block_list, block_count):
    qry_count = lax.axis_size("qry")
    width = library_keys.shape[1]
    value_width = library_values.shape[1]

    partner_keys = swap(library_keys, "lib", 1)
    own_values, _ = tie(library_values, partner_keys)
    values = pl.pallas_call(
        pack_kernel,
        out_shape=jax.ShapeDtypeStruct((TILE + EXTRA, value_width), jnp.bfloat16),
        in_specs=[pl.BlockSpec(memory_space=pl.ANY)] * 2,
        out_specs=VMEM,
        scratch_shapes=[pltpu.VMEM((1, TILE), jnp.bfloat16), pltpu.SemaphoreType.DMA((2,))],
        compiler_params=params(),
    )(own_values, key_scale.reshape(1, TILE))

    window_lists = block_list.T
    window_counts = block_count.reshape(1, -1)
    masks = [2 * at + 1 for at in range(1, qry_count // 2)]
    early, relayed, partner_values, visitors = gather_library(library_keys, values, queries, masks)
    piece_rows = (width // value_width + 1) * TILE + EXTRA
    cost = pl.CostEstimate(flops=2 * TILE * 4 * TILE * width * 2, bytes_accessed=4 * 1024 * 1024, transcendentals=0)
    total_shape = jax.ShapeDtypeStruct((TILE, value_width), jnp.float32)
    line_shape = jax.ShapeDtypeStruct((TILE, LANES), jnp.float32)
    pieces_total = 2 * (1 + len(early) + len(relayed))
    attend_params = params(pieces_total * piece_rows * value_width * 2)
    own_specs = [pl.BlockSpec(memory_space=pl.ANY), VMEM]
    own_scratch = [pltpu.VMEM(library_keys.shape, library_keys.dtype), pltpu.SemaphoreType.DMA]
    early_arrays = arrays_of(early)
    states = []
    for mask, visiting in visitors:
        state = pl.pallas_call(
            functools.partial(early_kernel, places_of(early), mask),
            out_shape=(total_shape, line_shape, line_shape),
            in_specs=[VMEM, VMEM] + [VMEM] * (1 + len(early_arrays)) + own_specs,
            out_specs=(VMEM,) * 3,
            scratch_shapes=[pltpu.VMEM((len(early) + 1, TILE, TILE), jnp.float32)] + own_scratch,
            compiler_params=attend_params,
            cost_estimate=cost,
        )(window_lists, window_counts, visiting, *early_arrays, library_keys, values)
        states.append(state)

    late = [((1, 0), partner_keys, partner_values)] + cross_cores(early) + relayed + cross_cores(relayed, [state[2] for state in states])
    late_arrays = arrays_of(late)
    returned = []
    for (mask, visiting), state in zip(visitors, states):
        packed = pl.pallas_call(
            functools.partial(late_kernel, places_of(late), mask),
            out_shape=jax.ShapeDtypeStruct((TILE + EXTRA, value_width), jnp.bfloat16),
            in_specs=[VMEM, VMEM] + [VMEM] * (4 + len(late_arrays)),
            out_specs=VMEM,
            scratch_shapes=[
                pltpu.VMEM((len(late), TILE, TILE), jnp.float32),
                pltpu.VMEM((TILE, value_width), jnp.float32),
                pltpu.VMEM((TILE, TILE), jnp.float32),
            ],
            compiler_params=attend_params,
            cost_estimate=cost,
        )(window_lists, window_counts, visiting, *state, *late_arrays)
        returned.append(swap(packed, "qry", mask))

    total, stats = pl.pallas_call(
        functools.partial(home_kernel, places_of(early + late)),
        out_shape=(total_shape, jax.ShapeDtypeStruct((2, TILE, LANES), jnp.float32)),
        in_specs=[VMEM, VMEM] + [VMEM] * (1 + len(early_arrays) + len(late_arrays)) + own_specs,
        out_specs=(VMEM, VMEM),
        scratch_shapes=[
            pltpu.VMEM((pieces_total, TILE, TILE), jnp.float32),
            pltpu.VMEM((TILE, TILE), jnp.float32),
        ]
        + own_scratch,
        compiler_params=attend_params,
        cost_estimate=cost,
    )(window_lists, window_counts, queries, *early_arrays, *late_arrays, library_keys, values)

    return pl.pallas_call(
        merge_kernel,
        out_shape=jax.ShapeDtypeStruct((TILE, value_width), jnp.bfloat16),
        in_specs=[VMEM] * (2 + len(returned)),
        out_specs=VMEM,
        compiler_params=params(),
    )(total, stats, *returned)


def solution(mesh):
    in_specs = (
        P(("groups", "lib", "qry"), None),
        P(("groups", "lib", "qry"), None),
        P(("groups", "lib", "qry"), None),
        P(("groups", "lib", "qry")),
        P("groups", None),
        P("groups"),
    )
    out_specs = P(("groups", "lib", "qry"), None)
    return jax.shard_map(body, mesh=mesh, in_specs=in_specs, out_specs=out_specs, check_vma=False)
```

```python
import functools
import math

import jax
import jax.numpy as jnp
from jax import lax
from jax.experimental import pallas as pl
from jax.experimental.pallas import tpu as pltpu
from jax.sharding import PartitionSpec as P

TILE = 128
LANES = 128
EXTRA = 16
MASKED_SCORE = -1e30
VMEM = pl.BlockSpec(memory_space=pltpu.VMEM)


def params(operand_bytes=0):
    return pltpu.CompilerParams(vmem_limit_bytes=operand_bytes * 3 // 2 + 6 * 1024 * 1024)


def swap(value, axis, mask):
    length = lax.axis_size(axis)
    return lax.ppermute(value, axis, [(i, i ^ mask) for i in range(length)])


def tie(*values):
    return lax.optimization_barrier(values)


def split_three(value):
    high = value.astype(jnp.bfloat16)
    rest = value - high.astype(jnp.float32)
    middle = rest.astype(jnp.bfloat16)
    low = (rest - middle.astype(jnp.float32)).astype(jnp.bfloat16)
    return high, middle, low


def pack_kernel(values_ref, scale_ref, packed_ref, row_ref, sems):
    value_width = values_ref.shape[1]
    copies = (
        pltpu.make_async_copy(values_ref, packed_ref.at[pl.ds(0, TILE)], sems.at[0]),
        pltpu.make_async_copy(scale_ref, row_ref, sems.at[1]),
    )
    for copy in copies:
        copy.start()
    packed_ref[TILE:, TILE:] = jnp.zeros((EXTRA, value_width - TILE), jnp.bfloat16)
    for copy in reversed(copies):
        copy.wait()
    row = row_ref[...].astype(jnp.float32)
    packed_ref[TILE:, 0:TILE] = jnp.broadcast_to(row, (EXTRA, TILE)).astype(jnp.bfloat16)


class Piece:
    def __init__(self, place, keys_ref, values_ref, row=0, copy=None):
        self.place = place
        self.keys_ref = keys_ref
        self.values_ref = values_ref
        self.row = row
        self.copy = copy

    def scores(self, query_ref, inverse_root):
        product = lax.dot_general(
            query_ref[...], self.keys_ref[...], (((1,), (1,)), ((), ())), preferred_element_type=jnp.float32
        )
        scale = self.values_ref[self.row + TILE : self.row + TILE + EXTRA, 0:TILE]
        return product * (scale.astype(jnp.float32)[0:1] * inverse_root)

    def values(self):
        return self.values_ref[self.row : self.row + TILE, :]


def read_pieces(places, refs, bundled=(), own=None):
    pieces = [Piece(place, refs[2 * at], refs[2 * at + 1]) for at, place in enumerate(places)]
    refs = refs[2 * len(places) :]
    if bundled:
        values_ref = refs[len(bundled)]
        pieces += [
            Piece(place, refs[at], values_ref, at * (TILE + EXTRA)) for at, place in enumerate(bundled)
        ]
        refs = refs[len(bundled) + 1 :]
    if own is not None:
        keys_ref, values_ref, *refs, held_ref, sem = refs
        copy = pltpu.make_async_copy(keys_ref, held_ref, sem)
        copy.start()
        pieces.append(Piece((0, 0), held_ref, values_ref, copy=copy))
    return pieces, refs


def bundle_kernel(*refs):
    *refs, bundle_ref = refs
    row = 0
    for ref in refs:
        bundle_ref[row : row + ref.shape[0], :] = ref[...]
        row += ref.shape[0]


def pick(ref, row, column):
    rows = lax.broadcasted_iota(jnp.int32, ref.shape, 0)
    columns = lax.broadcasted_iota(jnp.int32, ref.shape, 1)
    chosen = jnp.where((rows == row) & (columns == column), ref[...], 0)
    return jnp.sum(chosen.astype(jnp.float32)).astype(jnp.int32)


def attend(pieces, panel_mask, lists_ref, counts_ref, query_ref, score_ref, total_ref, mass_ref, before=None):
    lib_index = lax.axis_index("lib")
    qry_index = lax.axis_index("qry")
    qry_count = lax.axis_size("qry")
    block_total = lax.axis_size("lib") * qry_count
    panel = lib_index * qry_count + lax.bitwise_xor(qry_index, panel_mask)
    first = pick(lists_ref, 0, panel)
    count = pick(counts_ref, 0, panel)
    width = query_ref.shape[1]
    inverse_root = 1.0 / math.sqrt(width)

    def active(lib_mask, qry_mask):
        block = lax.bitwise_xor(lib_index, lib_mask) * qry_count + lax.bitwise_xor(qry_index, qry_mask)
        return lax.rem(block - first + block_total, block_total) < count

    flags = [active(*piece.place) for piece in pieces]
    score_ref[...] = jnp.full(score_ref.shape, MASKED_SCORE, jnp.float32)
    for at, (piece, flag) in enumerate(zip(pieces, flags)):
        if piece.copy is not None:
            piece.copy.wait()

        @pl.when(flag)
        def _(at=at, piece=piece):
            score_ref[at] = piece.scores(query_ref, inverse_root)

    largest = score_ref[0]
    for at in range(1, len(flags)):
        largest = jnp.maximum(largest, score_ref[at])
    row_max = jnp.max(largest, axis=1, keepdims=True)
    if before is None:
        total_ref[...] = jnp.zeros(total_ref.shape, jnp.float32)
        mass_ref[...] = jnp.zeros(mass_ref.shape, jnp.float32)
    else:
        old_total_ref, old_mass_ref, old_max_ref = before
        old_max = old_max_ref[...]
        new_max = jnp.maximum(old_max, row_max)
        shrink = jnp.exp(old_max - new_max)
        row_max = new_max[:, 0:1]
        mass_ref[...] = old_mass_ref[...] * shrink
        for at in range(0, total_ref.shape[1], LANES):
            total_ref[:, at : at + LANES] = old_total_ref[:, at : at + LANES] * shrink
    for at, (piece, flag) in enumerate(zip(pieces, flags)):

        @pl.when(flag)
        def _(at=at, piece=piece):
            weights = jnp.exp(score_ref[at] - row_max)
            mass_ref[...] += weights
            weight_high = weights.astype(jnp.bfloat16)
            weight_low = (weights - weight_high.astype(jnp.float32)).astype(jnp.bfloat16)
            values = piece.values()
            added = jnp.dot(weight_high, values, preferred_element_type=jnp.float32)
            added = added + jnp.dot(weight_low, values, preferred_element_type=jnp.float32)
            total_ref[...] += added

    return row_max


def early_kernel(places, panel_mask, lists_ref, counts_ref, query_ref, *refs):
    pieces, refs = read_pieces(places, refs, own=True)
    total_ref, mass_ref, max_ref, score_ref = refs
    row_max = attend(pieces, panel_mask, lists_ref, counts_ref, query_ref, score_ref, total_ref, mass_ref)
    max_ref[...] = jnp.broadcast_to(row_max, max_ref.shape)


def late_kernel(places, bundled, panel_mask, lists_ref, counts_ref, query_ref, *refs):
    before, refs = refs[:3], refs[3:]
    pieces, refs = read_pieces(places, refs, bundled)
    packed_ref, score_ref, total_ref, mass_ref = refs
    row_max = attend(pieces, panel_mask, lists_ref, counts_ref, query_ref, score_ref, total_ref, mass_ref, before)
    row_sum = jnp.sum(mass_ref[...], axis=1, keepdims=True)
    value_width = total_ref.shape[1]
    inverse = 1.0 / jnp.where(row_sum > 0.0, row_sum, 1.0)
    packed_ref[0:TILE, :] = (total_ref[...] * inverse).astype(jnp.bfloat16)
    row = lax.broadcasted_iota(jnp.int32, (EXTRA, LANES), 0)
    packed = jnp.zeros((EXTRA, LANES), jnp.float32)
    for first, column in ((0, row_max), (3, row_sum)):
        turned = jnp.transpose(jnp.broadcast_to(column, (TILE, LANES)))[0:EXTRA]
        for at, part in enumerate(split_three(turned)):
            packed = jnp.where(row == first + at, part.astype(jnp.float32), packed)
    packed_ref[TILE:, 0:LANES] = packed.astype(jnp.bfloat16)
    packed_ref[TILE:, LANES:] = jnp.zeros((EXTRA, value_width - LANES), jnp.bfloat16)


def home_kernel(places, bundled, lists_ref, counts_ref, query_ref, *refs):
    pieces, refs = read_pieces(places, refs, bundled, own=True)
    total_ref, stats_ref, score_ref, mass_ref = refs
    row_max = attend(pieces, 0, lists_ref, counts_ref, query_ref, score_ref, total_ref, mass_ref)
    row_sum = jnp.sum(mass_ref[...], axis=1, keepdims=True)
    stats_ref[0] = jnp.broadcast_to(row_max, (TILE, LANES))
    stats_ref[1] = jnp.broadcast_to(row_sum, (TILE, LANES))


def merge_kernel(total_ref, stats_ref, *refs):
    packed_refs, out_ref = refs[:-1], refs[-1]
    maxima = [stats_ref[0]]
    sums = [stats_ref[1]]
    for packed_ref in packed_refs:
        packed = packed_ref[TILE:, 0:LANES].astype(jnp.float32)
        for first, kept in ((0, maxima), (3, sums)):
            line = packed[first : first + 1] + packed[first + 1 : first + 2] + packed[first + 2 : first + 3]
            kept.append(jnp.transpose(jnp.broadcast_to(line, (TILE, LANES))))
    top = functools.reduce(jnp.maximum, maxima)
    factors = [jnp.exp(row_max - top) for row_max in maxima]
    masses = [factor * row_sum for factor, row_sum in zip(factors, sums)]
    inverse = 1.0 / functools.reduce(jnp.add, masses)
    scales = [factors[0] * inverse] + [mass * inverse for mass in masses[1:]]
    for at in range(0, total_ref.shape[1], LANES):
        merged = total_ref[:, at : at + LANES] * scales[0]
        for packed_ref, scale in zip(packed_refs, scales[1:]):
            merged = merged + packed_ref[0:TILE, at : at + LANES].astype(jnp.float32) * scale
        out_ref[:, at : at + LANES] = merged.astype(jnp.bfloat16)


def gather_library(keys, values, queries, masks):
    steps = [("qry", 1)]
    mask = lax.axis_size("lib") // 2
    while mask > 1:
        steps.append(("lib", mask))
        mask //= 2
    partner_values = swap(values, "lib", 1)
    leaving, _ = tie(queries, partner_values)
    visitors = [swap(leaving, "qry", mask) for mask in masks]
    early, late = [], []
    for axis, mask in steps:
        place = (0, mask) if axis == "qry" else (mask, 0)
        near = (place, swap(keys, axis, mask), swap(values, axis, mask))
        relayed = []
        for (lib_mask, qry_mask), far_keys, far_values in early + late:
            far_keys, *_ = tie(far_keys, near[1], values)
            far_values, _ = tie(far_values, near[2])
            place = (lib_mask | mask, qry_mask)
            relayed.append((place, swap(far_keys, axis, mask), swap(far_values, axis, mask)))
        early, late = early + late + [near], relayed
    return early, late, partner_values, list(zip(masks, visitors))


def cross_cores(pieces, arrivals=()):
    crossed = []
    for (lib_mask, qry_mask), *pair in pieces:
        pair = tie(*pair, *arrivals)[:2]
        crossed.append(((lib_mask | 1, qry_mask), *(swap(array, "lib", 1) for array in pair)))
    return crossed


def places_of(pieces):
    return [piece[0] for piece in pieces]


def arrays_of(pieces):
    return [array for piece in pieces for array in piece[1:]]


def body(queries, library_keys, library_values, key_scale, block_list, block_count):
    qry_count = lax.axis_size("qry")
    width = library_keys.shape[1]
    value_width = library_values.shape[1]

    partner_keys = swap(library_keys, "lib", 1)
    own_values, _ = tie(library_values, partner_keys)
    values = pl.pallas_call(
        pack_kernel,
        out_shape=jax.ShapeDtypeStruct((TILE + EXTRA, value_width), jnp.bfloat16),
        in_specs=[pl.BlockSpec(memory_space=pl.ANY)] * 2,
        out_specs=VMEM,
        scratch_shapes=[pltpu.VMEM((1, TILE), jnp.bfloat16), pltpu.SemaphoreType.DMA((2,))],
        compiler_params=params(),
    )(own_values, key_scale.reshape(1, TILE))

    window_lists = block_list.T
    window_counts = block_count.reshape(1, -1)
    masks = [2 * at + 1 for at in range(1, qry_count // 2)]
    early, relayed, partner_values, visitors = gather_library(library_keys, values, queries, masks)
    piece_rows = (width // value_width + 1) * TILE + EXTRA
    cost = pl.CostEstimate(flops=2 * TILE * 4 * TILE * width * 2, bytes_accessed=4 * 1024 * 1024, transcendentals=0)
    total_shape = jax.ShapeDtypeStruct((TILE, value_width), jnp.float32)
    line_shape = jax.ShapeDtypeStruct((TILE, LANES), jnp.float32)
    pieces_total = 2 * (1 + len(early) + len(relayed))
    attend_params = params(pieces_total * piece_rows * value_width * 2)
    own_specs = [pl.BlockSpec(memory_space=pl.ANY), VMEM]
    own_scratch = [pltpu.VMEM(library_keys.shape, library_keys.dtype), pltpu.SemaphoreType.DMA]
    early_arrays = arrays_of(early)
    states = []
    for mask, visiting in visitors:
        state = pl.pallas_call(
            functools.partial(early_kernel, places_of(early), mask),
            out_shape=(total_shape, line_shape, line_shape),
            in_specs=[VMEM, VMEM] + [VMEM] * (1 + len(early_arrays)) + own_specs,
            out_specs=(VMEM,) * 3,
            scratch_shapes=[pltpu.VMEM((len(early) + 1, TILE, TILE), jnp.float32)] + own_scratch,
            compiler_params=attend_params,
            cost_estimate=cost,
        )(window_lists, window_counts, visiting, *early_arrays, library_keys, values)
        states.append(state)

    bundled = [(lib_mask | 1, qry_mask) for lib_mask, qry_mask in places_of(early)]
    early_values = [piece[2] for piece in early]
    bundle = pl.pallas_call(
        bundle_kernel,
        out_shape=jax.ShapeDtypeStruct((len(early) * (TILE + EXTRA), value_width), jnp.bfloat16),
        in_specs=[VMEM] * len(early),
        out_specs=VMEM,
        compiler_params=params(),
    )(*early_values)
    bundled_arrays = [swap(piece[1], "lib", 1) for piece in early] + [swap(bundle, "lib", 1)]
    late = [((1, 0), partner_keys, partner_values)] + relayed
    late += cross_cores(relayed, [state[2] for state in states])
    late_arrays = arrays_of(late) + bundled_arrays
    returned = []
    for (mask, visiting), state in zip(visitors, states):
        packed = pl.pallas_call(
            functools.partial(late_kernel, places_of(late), bundled, mask),
            out_shape=jax.ShapeDtypeStruct((TILE + EXTRA, value_width), jnp.bfloat16),
            in_specs=[VMEM, VMEM] + [VMEM] * (4 + len(late_arrays)),
            out_specs=VMEM,
            scratch_shapes=[
                pltpu.VMEM((len(late) + len(bundled), TILE, TILE), jnp.float32),
                pltpu.VMEM((TILE, value_width), jnp.float32),
                pltpu.VMEM((TILE, TILE), jnp.float32),
            ],
            compiler_params=attend_params,
            cost_estimate=cost,
        )(window_lists, window_counts, visiting, *state, *late_arrays)
        returned.append(swap(packed, "qry", mask))

    total, stats = pl.pallas_call(
        functools.partial(home_kernel, places_of(early + late), bundled),
        out_shape=(total_shape, jax.ShapeDtypeStruct((2, TILE, LANES), jnp.float32)),
        in_specs=[VMEM, VMEM] + [VMEM] * (1 + len(early_arrays) + len(late_arrays)) + own_specs,
        out_specs=(VMEM, VMEM),
        scratch_shapes=[
            pltpu.VMEM((pieces_total, TILE, TILE), jnp.float32),
            pltpu.VMEM((TILE, TILE), jnp.float32),
        ]
        + own_scratch,
        compiler_params=attend_params,
        cost_estimate=cost,
    )(window_lists, window_counts, queries, *early_arrays, *late_arrays, library_keys, values)

    return pl.pallas_call(
        merge_kernel,
        out_shape=jax.ShapeDtypeStruct((TILE, value_width), jnp.bfloat16),
        in_specs=[VMEM] * (2 + len(returned)),
        out_specs=VMEM,
        compiler_params=params(),
    )(total, stats, *returned)


def solution(mesh):
    in_specs = (
        P(("groups", "lib", "qry"), None),
        P(("groups", "lib", "qry"), None),
        P(("groups", "lib", "qry"), None),
        P(("groups", "lib", "qry")),
        P("groups", None),
        P("groups"),
    )
    out_specs = P(("groups", "lib", "qry"), None)
    return jax.shard_map(body, mesh=mesh, in_specs=in_specs, out_specs=out_specs, check_vma=False)
```

```python
import functools
import math

import jax
import jax.numpy as jnp
from jax import lax
from jax.experimental import pallas as pl
from jax.experimental.pallas import tpu as pltpu
from jax.sharding import PartitionSpec as P

TILE = 128
LANES = 128
EXTRA = 16
SUBLANES = 8
MASKED_SCORE = -1e30
VMEM = pl.BlockSpec(memory_space=pltpu.VMEM)


def params(operand_bytes=0):
    return pltpu.CompilerParams(vmem_limit_bytes=operand_bytes * 3 // 2 + 6 * 1024 * 1024)


def swap(value, axis, mask):
    length = lax.axis_size(axis)
    return lax.ppermute(value, axis, [(i, i ^ mask) for i in range(length)])


def tie(*values):
    return lax.optimization_barrier(values)


def pack_kernel(values_ref, scale_ref, packed_ref, row_ref, sems):
    value_width = values_ref.shape[1]
    copies = (
        pltpu.make_async_copy(values_ref, packed_ref.at[pl.ds(0, TILE)], sems.at[0]),
        pltpu.make_async_copy(scale_ref, row_ref, sems.at[1]),
    )
    for copy in copies:
        copy.start()
    packed_ref[TILE:, TILE:] = jnp.zeros((EXTRA, value_width - TILE), jnp.bfloat16)
    for copy in reversed(copies):
        copy.wait()
    row = row_ref[...].astype(jnp.float32)
    packed_ref[TILE:, 0:TILE] = jnp.broadcast_to(row, (EXTRA, TILE)).astype(jnp.bfloat16)


class Piece:
    def __init__(self, place, keys_ref, values_ref, row=0, copy=None):
        self.place = place
        self.keys_ref = keys_ref
        self.values_ref = values_ref
        self.row = row
        self.copy = copy

    def scores(self, query_ref, inverse_root):
        product = lax.dot_general(
            query_ref[...], self.keys_ref[...], (((1,), (1,)), ((), ())), preferred_element_type=jnp.float32
        )
        scale = self.values_ref[self.row + TILE : self.row + TILE + EXTRA, 0:TILE]
        return product * (scale.astype(jnp.float32)[0:1] * inverse_root)

    def values(self):
        return self.values_ref[self.row : self.row + TILE, :]


def read_pieces(places, refs, bundled=(), own=None):
    pieces = [Piece(place, refs[2 * at], refs[2 * at + 1]) for at, place in enumerate(places)]
    refs = refs[2 * len(places) :]
    if bundled:
        values_ref = refs[len(bundled)]
        pieces += [
            Piece(place, refs[at], values_ref, at * (TILE + EXTRA)) for at, place in enumerate(bundled)
        ]
        refs = refs[len(bundled) + 1 :]
    if own is not None:
        keys_ref, values_ref, *refs, held_ref, sem = refs
        copy = pltpu.make_async_copy(keys_ref, held_ref, sem)
        copy.start()
        pieces.append(Piece((0, 0), held_ref, values_ref, copy=copy))
    return pieces, refs


def bundle_kernel(*refs):
    *refs, bundle_ref = refs
    row = 0
    for ref in refs:
        bundle_ref[row : row + ref.shape[0], :] = ref[...]
        row += ref.shape[0]


def pick(ref, row, column):
    rows = lax.broadcasted_iota(jnp.int32, ref.shape, 0)
    columns = lax.broadcasted_iota(jnp.int32, ref.shape, 1)
    chosen = jnp.where((rows == row) & (columns == column), ref[...], 0)
    return jnp.sum(chosen.astype(jnp.float32)).astype(jnp.int32)


def attend(pieces, panel_mask, lists_ref, counts_ref, query_ref, score_ref, total_ref, mass_ref, before=None):
    lib_index = lax.axis_index("lib")
    qry_index = lax.axis_index("qry")
    qry_count = lax.axis_size("qry")
    block_total = lax.axis_size("lib") * qry_count
    panel = lib_index * qry_count + lax.bitwise_xor(qry_index, panel_mask)
    first = pick(lists_ref, 0, panel)
    count = pick(counts_ref, 0, panel)
    width = query_ref.shape[1]
    inverse_root = 1.0 / math.sqrt(width)

    def active(lib_mask, qry_mask):
        block = lax.bitwise_xor(lib_index, lib_mask) * qry_count + lax.bitwise_xor(qry_index, qry_mask)
        return lax.rem(block - first + block_total, block_total) < count

    flags = [active(*piece.place) for piece in pieces]
    score_ref[...] = jnp.full(score_ref.shape, MASKED_SCORE, jnp.float32)
    for at, (piece, flag) in enumerate(zip(pieces, flags)):
        if piece.copy is not None:
            piece.copy.wait()

        @pl.when(flag)
        def _(at=at, piece=piece):
            score_ref[at] = piece.scores(query_ref, inverse_root)

    largest = score_ref[0]
    for at in range(1, len(flags)):
        largest = jnp.maximum(largest, score_ref[at])
    row_max = jnp.max(largest, axis=1, keepdims=True)
    if before is None:
        total_ref[...] = jnp.zeros(total_ref.shape, jnp.float32)
        mass_ref[...] = jnp.zeros(mass_ref.shape, jnp.float32)
    else:
        old_total_ref, old_mass_ref, old_max_ref = before
        old_max = old_max_ref[...]
        new_max = jnp.maximum(old_max, row_max)
        shrink = jnp.exp(old_max - new_max)
        row_max = new_max[:, 0:1]
        mass_ref[...] = old_mass_ref[...] * shrink
        for at in range(0, total_ref.shape[1], LANES):
            total_ref[:, at : at + LANES] = old_total_ref[:, at : at + LANES] * shrink
    for at, (piece, flag) in enumerate(zip(pieces, flags)):

        @pl.when(flag)
        def _(at=at, piece=piece):
            weights = jnp.exp(score_ref[at] - row_max)
            mass_ref[...] += weights
            weight_high = weights.astype(jnp.bfloat16)
            weight_low = (weights - weight_high.astype(jnp.float32)).astype(jnp.bfloat16)
            values = piece.values()
            added = jnp.dot(weight_high, values, preferred_element_type=jnp.float32)
            added = added + jnp.dot(weight_low, values, preferred_element_type=jnp.float32)
            total_ref[...] += added

    return row_max


def early_kernel(places, panel_mask, lists_ref, counts_ref, query_ref, *refs):
    pieces, refs = read_pieces(places, refs, own=True)
    total_ref, mass_ref, max_ref, score_ref = refs
    row_max = attend(pieces, panel_mask, lists_ref, counts_ref, query_ref, score_ref, total_ref, mass_ref)
    max_ref[...] = jnp.broadcast_to(row_max, max_ref.shape)


def late_kernel(places, bundled, panel_mask, lists_ref, counts_ref, query_ref, *refs):
    before, refs = refs[:3], refs[3:]
    pieces, refs = read_pieces(places, refs, bundled)
    partial_ref, lines_ref, score_ref, total_ref, mass_ref = refs
    row_max = attend(pieces, panel_mask, lists_ref, counts_ref, query_ref, score_ref, total_ref, mass_ref, before)
    row_sum = jnp.sum(mass_ref[...], axis=1, keepdims=True)
    inverse = 1.0 / jnp.where(row_sum > 0.0, row_sum, 1.0)
    partial_ref[...] = (total_ref[...] * inverse).astype(jnp.bfloat16)
    lane = lax.broadcasted_iota(jnp.int32, (TILE, LANES), 1)
    lines_ref[...] = jnp.transpose(jnp.where(lane == 0, row_max, row_sum))[0:SUBLANES]


def home_kernel(places, bundled, lists_ref, counts_ref, query_ref, *refs):
    pieces, refs = read_pieces(places, refs, bundled, own=True)
    total_ref, stats_ref, score_ref, mass_ref = refs
    row_max = attend(pieces, 0, lists_ref, counts_ref, query_ref, score_ref, total_ref, mass_ref)
    row_sum = jnp.sum(mass_ref[...], axis=1, keepdims=True)
    stats_ref[0] = jnp.broadcast_to(row_max, (TILE, LANES))
    stats_ref[1] = jnp.broadcast_to(row_sum, (TILE, LANES))


def merge_kernel(total_ref, stats_ref, *refs):
    returned, out_ref = refs[:-1], refs[-1]
    partial_refs, lines_refs = returned[0::2], returned[1::2]
    maxima = [stats_ref[0]]
    sums = [stats_ref[1]]
    for lines_ref in lines_refs:
        turned = jnp.transpose(jnp.concatenate([lines_ref[...]] * (TILE // SUBLANES), axis=0))
        maxima.append(jnp.broadcast_to(turned[:, 0:1], (TILE, LANES)))
        sums.append(jnp.broadcast_to(turned[:, 1:2], (TILE, LANES)))
    top = functools.reduce(jnp.maximum, maxima)
    factors = [jnp.exp(row_max - top) for row_max in maxima]
    masses = [factor * row_sum for factor, row_sum in zip(factors, sums)]
    inverse = 1.0 / functools.reduce(jnp.add, masses)
    shares = [factors[0] * inverse] + [mass * inverse for mass in masses[1:]]
    for at in range(0, total_ref.shape[1], LANES):
        merged = total_ref[:, at : at + LANES] * shares[0]
        for partial_ref, share in zip(partial_refs, shares[1:]):
            merged = merged + partial_ref[:, at : at + LANES].astype(jnp.float32) * share
        out_ref[:, at : at + LANES] = merged.astype(jnp.bfloat16)


def gather_library(keys, values, queries, masks):
    steps = [("qry", 1)]
    mask = lax.axis_size("lib") // 2
    while mask > 1:
        steps.append(("lib", mask))
        mask //= 2
    partner_values = swap(values, "lib", 1)
    leaving, _ = tie(queries, partner_values)
    visitors = [swap(leaving, "qry", mask) for mask in masks]
    early, late = [], []
    for axis, mask in steps:
        place = (0, mask) if axis == "qry" else (mask, 0)
        near = (place, swap(keys, axis, mask), swap(values, axis, mask))
        relayed = []
        for (lib_mask, qry_mask), far_keys, far_values in early + late:
            far_keys, *_ = tie(far_keys, near[1], values)
            far_values, _ = tie(far_values, near[2])
            place = (lib_mask | mask, qry_mask)
            relayed.append((place, swap(far_keys, axis, mask), swap(far_values, axis, mask)))
        early, late = early + late + [near], relayed
    return early, late, partner_values, list(zip(masks, visitors))


def cross_cores(pieces, arrivals=()):
    crossed = []
    for (lib_mask, qry_mask), *pair in pieces:
        pair = tie(*pair, *arrivals)[:2]
        crossed.append(((lib_mask | 1, qry_mask), *(swap(array, "lib", 1) for array in pair)))
    return crossed


def places_of(pieces):
    return [piece[0] for piece in pieces]


def arrays_of(pieces):
    return [array for piece in pieces for array in piece[1:]]


def body(queries, library_keys, library_values, key_scale, block_list, block_count):
    qry_count = lax.axis_size("qry")
    width = library_keys.shape[1]
    value_width = library_values.shape[1]

    partner_keys = swap(library_keys, "lib", 1)
    own_values, _ = tie(library_values, partner_keys)
    values = pl.pallas_call(
        pack_kernel,
        out_shape=jax.ShapeDtypeStruct((TILE + EXTRA, value_width), jnp.bfloat16),
        in_specs=[pl.BlockSpec(memory_space=pl.ANY)] * 2,
        out_specs=VMEM,
        scratch_shapes=[pltpu.VMEM((1, TILE), jnp.bfloat16), pltpu.SemaphoreType.DMA((2,))],
        compiler_params=params(),
    )(own_values, key_scale.reshape(1, TILE))

    window_lists = block_list.T
    window_counts = block_count.reshape(1, -1)
    masks = [2 * at + 1 for at in range(1, qry_count // 2)]
    early, relayed, partner_values, visitors = gather_library(library_keys, values, queries, masks)
    piece_rows = (width // value_width + 1) * TILE + EXTRA
    cost = pl.CostEstimate(flops=2 * TILE * 4 * TILE * width * 2, bytes_accessed=4 * 1024 * 1024, transcendentals=0)
    total_shape = jax.ShapeDtypeStruct((TILE, value_width), jnp.float32)
    line_shape = jax.ShapeDtypeStruct((TILE, LANES), jnp.float32)
    pieces_total = 2 * (1 + len(early) + len(relayed))
    attend_params = params(pieces_total * piece_rows * value_width * 2)
    own_specs = [pl.BlockSpec(memory_space=pl.ANY), VMEM]
    own_scratch = [pltpu.VMEM(library_keys.shape, library_keys.dtype), pltpu.SemaphoreType.DMA]
    early_arrays = arrays_of(early)
    states = []
    for mask, visiting in visitors:
        state = pl.pallas_call(
            functools.partial(early_kernel, places_of(early), mask),
            out_shape=(total_shape, line_shape, line_shape),
            in_specs=[VMEM, VMEM] + [VMEM] * (1 + len(early_arrays)) + own_specs,
            out_specs=(VMEM,) * 3,
            scratch_shapes=[pltpu.VMEM((len(early) + 1, TILE, TILE), jnp.float32)] + own_scratch,
            compiler_params=attend_params,
            cost_estimate=cost,
        )(window_lists, window_counts, visiting, *early_arrays, library_keys, values)
        states.append(state)

    bundled = [(lib_mask | 1, qry_mask) for lib_mask, qry_mask in places_of(early)]
    early_values = [piece[2] for piece in early]
    bundle = pl.pallas_call(
        bundle_kernel,
        out_shape=jax.ShapeDtypeStruct((len(early) * (TILE + EXTRA), value_width), jnp.bfloat16),
        in_specs=[VMEM] * len(early),
        out_specs=VMEM,
        compiler_params=params(),
    )(*early_values)
    bundled_arrays = [swap(piece[1], "lib", 1) for piece in early] + [swap(bundle, "lib", 1)]
    late = [((1, 0), partner_keys, partner_values)] + relayed
    late += cross_cores(relayed, [state[2] for state in states])
    late_arrays = arrays_of(late) + bundled_arrays
    returned = []
    for (mask, visiting), state in zip(visitors, states):
        partial, lines = pl.pallas_call(
            functools.partial(late_kernel, places_of(late), bundled, mask),
            out_shape=(
                jax.ShapeDtypeStruct((TILE, value_width), jnp.bfloat16),
                jax.ShapeDtypeStruct((SUBLANES, LANES), jnp.float32),
            ),
            in_specs=[VMEM, VMEM] + [VMEM] * (4 + len(late_arrays)),
            out_specs=(VMEM, VMEM),
            scratch_shapes=[
                pltpu.VMEM((len(late) + len(bundled), TILE, TILE), jnp.float32),
                pltpu.VMEM((TILE, value_width), jnp.float32),
                pltpu.VMEM((TILE, TILE), jnp.float32),
            ],
            compiler_params=attend_params,
            cost_estimate=cost,
        )(window_lists, window_counts, visiting, *state, *late_arrays)
        returned += [swap(partial, "qry", mask), swap(lines, "qry", mask)]

    total, stats = pl.pallas_call(
        functools.partial(home_kernel, places_of(early + late), bundled),
        out_shape=(total_shape, jax.ShapeDtypeStruct((2, TILE, LANES), jnp.float32)),
        in_specs=[VMEM, VMEM] + [VMEM] * (1 + len(early_arrays) + len(late_arrays)) + own_specs,
        out_specs=(VMEM, VMEM),
        scratch_shapes=[
            pltpu.VMEM((pieces_total, TILE, TILE), jnp.float32),
            pltpu.VMEM((TILE, TILE), jnp.float32),
        ]
        + own_scratch,
        compiler_params=attend_params,
        cost_estimate=cost,
    )(window_lists, window_counts, queries, *early_arrays, *late_arrays, library_keys, values)

    return pl.pallas_call(
        merge_kernel,
        out_shape=jax.ShapeDtypeStruct((TILE, value_width), jnp.bfloat16),
        in_specs=[VMEM] * (2 + len(returned)),
        out_specs=VMEM,
        compiler_params=params(),
    )(total, stats, *returned)


def solution(mesh):
    in_specs = (
        P(("groups", "lib", "qry"), None),
        P(("groups", "lib", "qry"), None),
        P(("groups", "lib", "qry"), None),
        P(("groups", "lib", "qry")),
        P("groups", None),
        P("groups"),
    )
    out_specs = P(("groups", "lib", "qry"), None)
    return jax.shard_map(body, mesh=mesh, in_specs=in_specs, out_specs=out_specs, check_vma=False)
```

```python
import functools
import math

import jax
import jax.numpy as jnp
from jax import lax
from jax.experimental import pallas as pl
from jax.experimental.pallas import tpu as pltpu
from jax.sharding import PartitionSpec as P

TILE = 128
LANES = 128
EXTRA = 16
LINES = 8
MASKED_SCORE = -1e30
VMEM = pl.BlockSpec(memory_space=pltpu.VMEM)


def params(operand_bytes=0):
    return pltpu.CompilerParams(vmem_limit_bytes=operand_bytes * 3 // 2 + 6 * 1024 * 1024)


def swap(value, axis, mask):
    length = lax.axis_size(axis)
    return lax.ppermute(value, axis, [(i, i ^ mask) for i in range(length)])


def tie(*values):
    return lax.optimization_barrier(values)


def split_three(value):
    high = value.astype(jnp.bfloat16)
    rest = value - high.astype(jnp.float32)
    middle = rest.astype(jnp.bfloat16)
    low = (rest - middle.astype(jnp.float32)).astype(jnp.bfloat16)
    return high, middle, low


def pack_kernel(values_ref, scale_ref, packed_ref, row_ref, sems):
    value_width = values_ref.shape[1]
    copies = (
        pltpu.make_async_copy(values_ref, packed_ref.at[pl.ds(0, TILE)], sems.at[0]),
        pltpu.make_async_copy(scale_ref, row_ref, sems.at[1]),
    )
    for copy in copies:
        copy.start()
    packed_ref[TILE:, TILE:] = jnp.zeros((EXTRA, value_width - TILE), jnp.bfloat16)
    for copy in reversed(copies):
        copy.wait()
    row = row_ref[...].astype(jnp.float32)
    packed_ref[TILE:, 0:TILE] = jnp.broadcast_to(row, (EXTRA, TILE)).astype(jnp.bfloat16)


class Piece:
    def __init__(self, place, keys_ref, values_ref, row=0, copy=None):
        self.place = place
        self.keys_ref = keys_ref
        self.values_ref = values_ref
        self.row = row
        self.copy = copy

    def scores(self, query_ref, inverse_root):
        product = lax.dot_general(
            query_ref[...], self.keys_ref[...], (((1,), (1,)), ((), ())), preferred_element_type=jnp.float32
        )
        scale = self.values_ref[self.row + TILE : self.row + TILE + EXTRA, 0:TILE]
        return product * (scale.astype(jnp.float32)[0:1] * inverse_root)

    def values(self):
        return self.values_ref[self.row : self.row + TILE, :]


def read_pieces(places, refs, bundled=(), own=None):
    pieces = [Piece(place, refs[2 * at], refs[2 * at + 1]) for at, place in enumerate(places)]
    refs = refs[2 * len(places) :]
    if bundled:
        values_ref = refs[len(bundled)]
        pieces += [
            Piece(place, refs[at], values_ref, at * (TILE + EXTRA)) for at, place in enumerate(bundled)
        ]
        refs = refs[len(bundled) + 1 :]
    if own is not None:
        keys_ref, values_ref, *refs, held_ref, sem = refs
        copy = pltpu.make_async_copy(keys_ref, held_ref, sem)
        copy.start()
        pieces.append(Piece((0, 0), held_ref, values_ref, copy=copy))
    return pieces, refs


def bundle_kernel(*refs):
    *refs, bundle_ref = refs
    row = 0
    for ref in refs:
        bundle_ref[row : row + ref.shape[0], :] = ref[...]
        row += ref.shape[0]


def pick(ref, row, column):
    rows = lax.broadcasted_iota(jnp.int32, ref.shape, 0)
    columns = lax.broadcasted_iota(jnp.int32, ref.shape, 1)
    chosen = jnp.where((rows == row) & (columns == column), ref[...], 0)
    return jnp.sum(chosen.astype(jnp.float32)).astype(jnp.int32)


def attend(pieces, panel_mask, lists_ref, counts_ref, query_ref, score_ref, total_ref, mass_ref, before=None):
    lib_index = lax.axis_index("lib")
    qry_index = lax.axis_index("qry")
    qry_count = lax.axis_size("qry")
    block_total = lax.axis_size("lib") * qry_count
    panel = lib_index * qry_count + lax.bitwise_xor(qry_index, panel_mask)
    first = pick(lists_ref, 0, panel)
    count = pick(counts_ref, 0, panel)
    width = query_ref.shape[1]
    inverse_root = 1.0 / math.sqrt(width)

    def active(lib_mask, qry_mask):
        block = lax.bitwise_xor(lib_index, lib_mask) * qry_count + lax.bitwise_xor(qry_index, qry_mask)
        return lax.rem(block - first + block_total, block_total) < count

    flags = [active(*piece.place) for piece in pieces]
    score_ref[...] = jnp.full(score_ref.shape, MASKED_SCORE, jnp.float32)
    for at, (piece, flag) in enumerate(zip(pieces, flags)):
        if piece.copy is not None:
            piece.copy.wait()

        @pl.when(flag)
        def _(at=at, piece=piece):
            score_ref[at] = piece.scores(query_ref, inverse_root)

    largest = score_ref[0]
    for at in range(1, len(flags)):
        largest = jnp.maximum(largest, score_ref[at])
    row_max = jnp.max(largest, axis=1, keepdims=True)
    if before is None:
        total_ref[...] = jnp.zeros(total_ref.shape, jnp.float32)
        mass_ref[...] = jnp.zeros(mass_ref.shape, jnp.float32)
    else:
        old_total_ref, old_mass_ref, old_max_ref = before
        old_max = old_max_ref[...]
        new_max = jnp.maximum(old_max, row_max)
        shrink = jnp.exp(old_max - new_max)
        row_max = new_max[:, 0:1]
        mass_ref[...] = old_mass_ref[...] * shrink
        for at in range(0, total_ref.shape[1], LANES):
            total_ref[:, at : at + LANES] = old_total_ref[:, at : at + LANES] * shrink
    for at, (piece, flag) in enumerate(zip(pieces, flags)):

        @pl.when(flag)
        def _(at=at, piece=piece):
            weights = jnp.exp(score_ref[at] - row_max)
            mass_ref[...] += weights
            weight_high = weights.astype(jnp.bfloat16)
            weight_low = (weights - weight_high.astype(jnp.float32)).astype(jnp.bfloat16)
            values = piece.values()
            added = jnp.dot(weight_high, values, preferred_element_type=jnp.float32)
            added = added + jnp.dot(weight_low, values, preferred_element_type=jnp.float32)
            total_ref[...] += added

    return row_max


def early_kernel(places, panel_mask, lists_ref, counts_ref, query_ref, *refs):
    pieces, refs = read_pieces(places, refs, own=True)
    total_ref, mass_ref, max_ref, score_ref = refs
    row_max = attend(pieces, panel_mask, lists_ref, counts_ref, query_ref, score_ref, total_ref, mass_ref)
    max_ref[...] = jnp.broadcast_to(row_max, max_ref.shape)


def late_kernel(places, bundled, panel_mask, lists_ref, counts_ref, query_ref, *refs):
    before, refs = refs[:3], refs[3:]
    pieces, refs = read_pieces(places, refs, bundled)
    packed_ref, score_ref, total_ref, mass_ref = refs
    row_max = attend(pieces, panel_mask, lists_ref, counts_ref, query_ref, score_ref, total_ref, mass_ref, before)
    row_sum = jnp.sum(mass_ref[...], axis=1, keepdims=True)
    value_width = total_ref.shape[1]
    inverse = 1.0 / jnp.where(row_sum > 0.0, row_sum, 1.0)
    packed_ref[0:TILE, :] = (total_ref[...] * inverse).astype(jnp.bfloat16)
    row = lax.broadcasted_iota(jnp.int32, (LINES, LANES), 0)
    packed = jnp.zeros((LINES, LANES), jnp.float32)
    for first, column in ((0, row_max), (3, row_sum)):
        turned = jnp.transpose(jnp.broadcast_to(column, (TILE, LANES)))[0:LINES]
        for at, part in enumerate(split_three(turned)):
            packed = jnp.where(row == first + at, part.astype(jnp.float32), packed)
    packed_ref[TILE:, 0:LANES] = packed.astype(jnp.bfloat16)
    packed_ref[TILE:, LANES:] = jnp.zeros((LINES, value_width - LANES), jnp.bfloat16)


def home_kernel(places, bundled, lists_ref, counts_ref, query_ref, *refs):
    pieces, refs = read_pieces(places, refs, bundled, own=True)
    total_ref, stats_ref, score_ref, mass_ref = refs
    row_max = attend(pieces, 0, lists_ref, counts_ref, query_ref, score_ref, total_ref, mass_ref)
    row_sum = jnp.sum(mass_ref[...], axis=1, keepdims=True)
    stats_ref[0] = jnp.broadcast_to(row_max, (TILE, LANES))
    stats_ref[1] = jnp.broadcast_to(row_sum, (TILE, LANES))


def merge_kernel(total_ref, stats_ref, *refs):
    packed_refs, out_ref = refs[:-1], refs[-1]
    maxima = [stats_ref[0]]
    sums = [stats_ref[1]]
    for packed_ref in packed_refs:
        packed = packed_ref[TILE:, 0:LANES].astype(jnp.float32)
        for first, kept in ((0, maxima), (3, sums)):
            line = packed[first : first + 1] + packed[first + 1 : first + 2] + packed[first + 2 : first + 3]
            kept.append(jnp.transpose(jnp.broadcast_to(line, (TILE, LANES))))
    top = functools.reduce(jnp.maximum, maxima)
    factors = [jnp.exp(row_max - top) for row_max in maxima]
    masses = [factor * row_sum for factor, row_sum in zip(factors, sums)]
    inverse = 1.0 / functools.reduce(jnp.add, masses)
    scales = [factors[0] * inverse] + [mass * inverse for mass in masses[1:]]
    for at in range(0, total_ref.shape[1], LANES):
        merged = total_ref[:, at : at + LANES] * scales[0]
        for packed_ref, scale in zip(packed_refs, scales[1:]):
            merged = merged + packed_ref[0:TILE, at : at + LANES].astype(jnp.float32) * scale
        out_ref[:, at : at + LANES] = merged.astype(jnp.bfloat16)


def gather_library(keys, values, queries, masks):
    steps = [("qry", 1)]
    mask = lax.axis_size("lib") // 2
    while mask > 1:
        steps.append(("lib", mask))
        mask //= 2
    partner_values = swap(values, "lib", 1)
    leaving, _ = tie(queries, partner_values)
    visitors = [swap(leaving, "qry", mask) for mask in masks]
    early, late = [], []
    for axis, mask in steps:
        place = (0, mask) if axis == "qry" else (mask, 0)
        near = (place, swap(keys, axis, mask), swap(values, axis, mask))
        relayed = []
        for (lib_mask, qry_mask), far_keys, far_values in early + late:
            far_keys, *_ = tie(far_keys, near[1], values)
            far_values, _ = tie(far_values, near[2])
            place = (lib_mask | mask, qry_mask)
            relayed.append((place, swap(far_keys, axis, mask), swap(far_values, axis, mask)))
        early, late = early + late + [near], relayed
    return early, late, partner_values, list(zip(masks, visitors))


def cross_cores(pieces, arrivals=()):
    crossed = []
    for (lib_mask, qry_mask), *pair in pieces:
        pair = tie(*pair, *arrivals)[:2]
        crossed.append(((lib_mask | 1, qry_mask), *(swap(array, "lib", 1) for array in pair)))
    return crossed


def places_of(pieces):
    return [piece[0] for piece in pieces]


def arrays_of(pieces):
    return [array for piece in pieces for array in piece[1:]]


def body(queries, library_keys, library_values, key_scale, block_list, block_count):
    qry_count = lax.axis_size("qry")
    width = library_keys.shape[1]
    value_width = library_values.shape[1]

    partner_keys = swap(library_keys, "lib", 1)
    own_values, _ = tie(library_values, partner_keys)
    values = pl.pallas_call(
        pack_kernel,
        out_shape=jax.ShapeDtypeStruct((TILE + EXTRA, value_width), jnp.bfloat16),
        in_specs=[pl.BlockSpec(memory_space=pl.ANY)] * 2,
        out_specs=VMEM,
        scratch_shapes=[pltpu.VMEM((1, TILE), jnp.bfloat16), pltpu.SemaphoreType.DMA((2,))],
        compiler_params=params(),
    )(own_values, key_scale.reshape(1, TILE))

    window_lists = block_list.T
    window_counts = block_count.reshape(1, -1)
    masks = [2 * at + 1 for at in range(1, qry_count // 2)]
    early, relayed, partner_values, visitors = gather_library(library_keys, values, queries, masks)
    piece_rows = (width // value_width + 1) * TILE + EXTRA
    cost = pl.CostEstimate(flops=2 * TILE * 4 * TILE * width * 2, bytes_accessed=4 * 1024 * 1024, transcendentals=0)
    total_shape = jax.ShapeDtypeStruct((TILE, value_width), jnp.float32)
    line_shape = jax.ShapeDtypeStruct((TILE, LANES), jnp.float32)
    pieces_total = 2 * (1 + len(early) + len(relayed))
    attend_params = params(pieces_total * piece_rows * value_width * 2)
    own_specs = [pl.BlockSpec(memory_space=pl.ANY), VMEM]
    own_scratch = [pltpu.VMEM(library_keys.shape, library_keys.dtype), pltpu.SemaphoreType.DMA]
    early_arrays = arrays_of(early)
    states = []
    for mask, visiting in visitors:
        state = pl.pallas_call(
            functools.partial(early_kernel, places_of(early), mask),
            out_shape=(total_shape, line_shape, line_shape),
            in_specs=[VMEM, VMEM] + [VMEM] * (1 + len(early_arrays)) + own_specs,
            out_specs=(VMEM,) * 3,
            scratch_shapes=[pltpu.VMEM((len(early) + 1, TILE, TILE), jnp.float32)] + own_scratch,
            compiler_params=attend_params,
            cost_estimate=cost,
        )(window_lists, window_counts, visiting, *early_arrays, library_keys, values)
        states.append(state)

    bundled = [(lib_mask | 1, qry_mask) for lib_mask, qry_mask in places_of(early)]
    early_values = [piece[2] for piece in early]
    bundle = pl.pallas_call(
        bundle_kernel,
        out_shape=jax.ShapeDtypeStruct((len(early) * (TILE + EXTRA), value_width), jnp.bfloat16),
        in_specs=[VMEM] * len(early),
        out_specs=VMEM,
        compiler_params=params(),
    )(*early_values)
    bundled_arrays = [swap(piece[1], "lib", 1) for piece in early] + [swap(bundle, "lib", 1)]
    late = [((1, 0), partner_keys, partner_values)] + relayed
    late += cross_cores(relayed, [state[2] for state in states])
    late_arrays = arrays_of(late) + bundled_arrays
    returned = []
    for (mask, visiting), state in zip(visitors, states):
        packed = pl.pallas_call(
            functools.partial(late_kernel, places_of(late), bundled, mask),
            out_shape=jax.ShapeDtypeStruct((TILE + LINES, value_width), jnp.bfloat16),
            in_specs=[VMEM, VMEM] + [VMEM] * (4 + len(late_arrays)),
            out_specs=VMEM,
            scratch_shapes=[
                pltpu.VMEM((len(late) + len(bundled), TILE, TILE), jnp.float32),
                pltpu.VMEM((TILE, value_width), jnp.float32),
                pltpu.VMEM((TILE, TILE), jnp.float32),
            ],
            compiler_params=attend_params,
            cost_estimate=cost,
        )(window_lists, window_counts, visiting, *state, *late_arrays)
        returned.append(swap(packed, "qry", mask))

    total, stats = pl.pallas_call(
        functools.partial(home_kernel, places_of(early + late), bundled),
        out_shape=(total_shape, jax.ShapeDtypeStruct((2, TILE, LANES), jnp.float32)),
        in_specs=[VMEM, VMEM] + [VMEM] * (1 + len(early_arrays) + len(late_arrays)) + own_specs,
        out_specs=(VMEM, VMEM),
        scratch_shapes=[
            pltpu.VMEM((pieces_total, TILE, TILE), jnp.float32),
            pltpu.VMEM((TILE, TILE), jnp.float32),
        ]
        + own_scratch,
        compiler_params=attend_params,
        cost_estimate=cost,
    )(window_lists, window_counts, queries, *early_arrays, *late_arrays, library_keys, values)

    return pl.pallas_call(
        merge_kernel,
        out_shape=jax.ShapeDtypeStruct((TILE, value_width), jnp.bfloat16),
        in_specs=[VMEM] * (2 + len(returned)),
        out_specs=VMEM,
        compiler_params=params(),
    )(total, stats, *returned)


def solution(mesh):
    in_specs = (
        P(("groups", "lib", "qry"), None),
        P(("groups", "lib", "qry"), None),
        P(("groups", "lib", "qry"), None),
        P(("groups", "lib", "qry")),
        P("groups", None),
        P("groups"),
    )
    out_specs = P(("groups", "lib", "qry"), None)
    return jax.shard_map(body, mesh=mesh, in_specs=in_specs, out_specs=out_specs, check_vma=False)
```

```python
import functools
import math

import jax
import jax.numpy as jnp
from jax import lax
from jax.experimental import pallas as pl
from jax.experimental.pallas import tpu as pltpu
from jax.sharding import PartitionSpec as P

TILE = 128
LANES = 128
EXTRA = 16
MASKED_SCORE = -1e30
VMEM = pl.BlockSpec(memory_space=pltpu.VMEM)


def params(operand_bytes=0):
    return pltpu.CompilerParams(vmem_limit_bytes=operand_bytes * 3 // 2 + 6 * 1024 * 1024)


def swap(value, axis, mask):
    length = lax.axis_size(axis)
    return lax.ppermute(value, axis, [(i, i ^ mask) for i in range(length)])


def tie(*values):
    return lax.optimization_barrier(values)


def split_three(value):
    high = value.astype(jnp.bfloat16)
    rest = value - high.astype(jnp.float32)
    middle = rest.astype(jnp.bfloat16)
    low = (rest - middle.astype(jnp.float32)).astype(jnp.bfloat16)
    return high, middle, low


def pack_kernel(values_ref, scale_ref, packed_ref, row_ref, sems):
    value_width = values_ref.shape[1]
    copies = (
        pltpu.make_async_copy(values_ref, packed_ref.at[pl.ds(0, TILE)], sems.at[0]),
        pltpu.make_async_copy(scale_ref, row_ref, sems.at[1]),
    )
    for copy in copies:
        copy.start()
    packed_ref[TILE:, TILE:] = jnp.zeros((EXTRA, value_width - TILE), jnp.bfloat16)
    for copy in reversed(copies):
        copy.wait()
    row = row_ref[...].astype(jnp.float32)
    packed_ref[TILE:, 0:TILE] = jnp.broadcast_to(row, (EXTRA, TILE)).astype(jnp.bfloat16)


class Piece:
    def __init__(self, place, keys_ref, values_ref, row=0, copy=None):
        self.place = place
        self.keys_ref = keys_ref
        self.values_ref = values_ref
        self.row = row
        self.copy = copy

    def scores(self, query_ref, inverse_root):
        product = lax.dot_general(
            query_ref[...], self.keys_ref[...], (((1,), (1,)), ((), ())), preferred_element_type=jnp.float32
        )
        scale = self.values_ref[self.row + TILE : self.row + TILE + EXTRA, 0:TILE]
        return product * (scale.astype(jnp.float32)[0:1] * inverse_root)

    def turned_scores(self, turned_ref, inverse_root):
        product = jnp.transpose(jnp.dot(self.keys_ref[...], turned_ref[...], preferred_element_type=jnp.float32))
        scale = self.values_ref[self.row + TILE : self.row + TILE + EXTRA, 0:TILE]
        return product * (scale.astype(jnp.float32)[0:1] * inverse_root)

    def values(self):
        return self.values_ref[self.row : self.row + TILE, :]


def read_pieces(places, refs, bundled=(), own=None):
    pieces = [Piece(place, refs[2 * at], refs[2 * at + 1]) for at, place in enumerate(places)]
    refs = refs[2 * len(places) :]
    if bundled:
        values_ref = refs[len(bundled)]
        pieces += [
            Piece(place, refs[at], values_ref, at * (TILE + EXTRA)) for at, place in enumerate(bundled)
        ]
        refs = refs[len(bundled) + 1 :]
    if own is not None:
        keys_ref, values_ref, *refs, held_ref, sem = refs
        copy = pltpu.make_async_copy(keys_ref, held_ref, sem)
        copy.start()
        pieces.append(Piece((0, 0), held_ref, values_ref, copy=copy))
    return pieces, refs


def bundle_kernel(*refs):
    *refs, bundle_ref = refs
    row = 0
    for ref in refs:
        bundle_ref[row : row + ref.shape[0], :] = ref[...]
        row += ref.shape[0]


def pick(ref, row, column):
    rows = lax.broadcasted_iota(jnp.int32, ref.shape, 0)
    columns = lax.broadcasted_iota(jnp.int32, ref.shape, 1)
    chosen = jnp.where((rows == row) & (columns == column), ref[...], 0)
    return jnp.sum(chosen.astype(jnp.float32)).astype(jnp.int32)


def attend(pieces, panel_mask, lists_ref, counts_ref, query_ref, score_ref, total_ref, mass_ref, before=None):
    lib_index = lax.axis_index("lib")
    qry_index = lax.axis_index("qry")
    qry_count = lax.axis_size("qry")
    block_total = lax.axis_size("lib") * qry_count
    panel = lib_index * qry_count + lax.bitwise_xor(qry_index, panel_mask)
    first = pick(lists_ref, 0, panel)
    count = pick(counts_ref, 0, panel)
    inverse_root = 1.0 / math.sqrt(pieces[0].keys_ref.shape[1])

    def active(lib_mask, qry_mask):
        block = lax.bitwise_xor(lib_index, lib_mask) * qry_count + lax.bitwise_xor(qry_index, qry_mask)
        return lax.rem(block - first + block_total, block_total) < count

    flags = [active(*piece.place) for piece in pieces]
    score_ref[...] = jnp.full(score_ref.shape, MASKED_SCORE, jnp.float32)
    for at, (piece, flag) in enumerate(zip(pieces, flags)):
        if piece.copy is not None:
            piece.copy.wait()

        @pl.when(flag)
        def _(at=at, piece=piece):
            scores = piece.scores if before is None else piece.turned_scores
            score_ref[at] = scores(query_ref, inverse_root)

    largest = score_ref[0]
    for at in range(1, len(flags)):
        largest = jnp.maximum(largest, score_ref[at])
    row_max = jnp.max(largest, axis=1, keepdims=True)
    if before is None:
        total_ref[...] = jnp.zeros(total_ref.shape, jnp.float32)
        mass_ref[...] = jnp.zeros(mass_ref.shape, jnp.float32)
    else:
        old_total_ref, old_mass_ref, old_max_ref = before
        old_max = old_max_ref[...]
        new_max = jnp.maximum(old_max, row_max)
        shrink = jnp.exp(old_max - new_max)
        row_max = new_max[:, 0:1]
        mass_ref[...] = old_mass_ref[...] * shrink
        for at in range(0, total_ref.shape[1], LANES):
            total_ref[:, at : at + LANES] = old_total_ref[:, at : at + LANES] * shrink
    for at, (piece, flag) in enumerate(zip(pieces, flags)):

        @pl.when(flag)
        def _(at=at, piece=piece):
            weights = jnp.exp(score_ref[at] - row_max)
            mass_ref[...] += weights
            weight_high = weights.astype(jnp.bfloat16)
            weight_low = (weights - weight_high.astype(jnp.float32)).astype(jnp.bfloat16)
            values = piece.values()
            added = jnp.dot(weight_high, values, preferred_element_type=jnp.float32)
            added = added + jnp.dot(weight_low, values, preferred_element_type=jnp.float32)
            total_ref[...] += added

    return row_max


def early_kernel(places, panel_mask, lists_ref, counts_ref, query_ref, *refs):
    pieces, refs = read_pieces(places, refs, own=True)
    turned_ref, total_ref, mass_ref, max_ref, score_ref = refs
    row_max = attend(pieces, panel_mask, lists_ref, counts_ref, query_ref, score_ref, total_ref, mass_ref)
    max_ref[...] = jnp.broadcast_to(row_max, max_ref.shape)
    turned_ref[...] = jnp.transpose(query_ref[...])


def late_kernel(places, bundled, panel_mask, lists_ref, counts_ref, turned_ref, *refs):
    before, refs = refs[:3], refs[3:]
    pieces, refs = read_pieces(places, refs, bundled)
    packed_ref, score_ref, total_ref, mass_ref = refs
    row_max = attend(pieces, panel_mask, lists_ref, counts_ref, turned_ref, score_ref, total_ref, mass_ref, before)
    row_sum = jnp.sum(mass_ref[...], axis=1, keepdims=True)
    value_width = total_ref.shape[1]
    inverse = 1.0 / jnp.where(row_sum > 0.0, row_sum, 1.0)
    packed_ref[0:TILE, :] = (total_ref[...] * inverse).astype(jnp.bfloat16)
    row = lax.broadcasted_iota(jnp.int32, (EXTRA, LANES), 0)
    packed = jnp.zeros((EXTRA, LANES), jnp.float32)
    for first, column in ((0, row_max), (3, row_sum)):
        turned = jnp.transpose(jnp.broadcast_to(column, (TILE, LANES)))[0:EXTRA]
        for at, part in enumerate(split_three(turned)):
            packed = jnp.where(row == first + at, part.astype(jnp.float32), packed)
    packed_ref[TILE:, 0:LANES] = packed.astype(jnp.bfloat16)
    packed_ref[TILE:, LANES:] = jnp.zeros((EXTRA, value_width - LANES), jnp.bfloat16)


def home_kernel(places, bundled, lists_ref, counts_ref, query_ref, *refs):
    pieces, refs = read_pieces(places, refs, bundled, own=True)
    total_ref, stats_ref, score_ref, mass_ref = refs
    row_max = attend(pieces, 0, lists_ref, counts_ref, query_ref, score_ref, total_ref, mass_ref)
    row_sum = jnp.sum(mass_ref[...], axis=1, keepdims=True)
    stats_ref[0] = jnp.broadcast_to(row_max, (TILE, LANES))
    stats_ref[1] = jnp.broadcast_to(row_sum, (TILE, LANES))


def merge_kernel(total_ref, stats_ref, *refs):
    packed_refs, out_ref = refs[:-1], refs[-1]
    maxima = [stats_ref[0]]
    sums = [stats_ref[1]]
    for packed_ref in packed_refs:
        packed = packed_ref[TILE:, 0:LANES].astype(jnp.float32)
        for first, kept in ((0, maxima), (3, sums)):
            line = packed[first : first + 1] + packed[first + 1 : first + 2] + packed[first + 2 : first + 3]
            kept.append(jnp.transpose(jnp.broadcast_to(line, (TILE, LANES))))
    top = functools.reduce(jnp.maximum, maxima)
    factors = [jnp.exp(row_max - top) for row_max in maxima]
    masses = [factor * row_sum for factor, row_sum in zip(factors, sums)]
    inverse = 1.0 / functools.reduce(jnp.add, masses)
    scales = [factors[0] * inverse] + [mass * inverse for mass in masses[1:]]
    for at in range(0, total_ref.shape[1], LANES):
        merged = total_ref[:, at : at + LANES] * scales[0]
        for packed_ref, scale in zip(packed_refs, scales[1:]):
            merged = merged + packed_ref[0:TILE, at : at + LANES].astype(jnp.float32) * scale
        out_ref[:, at : at + LANES] = merged.astype(jnp.bfloat16)


def gather_library(keys, values, queries, masks):
    steps = [("qry", 1)]
    mask = lax.axis_size("lib") // 2
    while mask > 1:
        steps.append(("lib", mask))
        mask //= 2
    partner_values = swap(values, "lib", 1)
    leaving, _ = tie(queries, partner_values)
    visitors = [swap(leaving, "qry", mask) for mask in masks]
    early, late = [], []
    for axis, mask in steps:
        place = (0, mask) if axis == "qry" else (mask, 0)
        near = (place, swap(keys, axis, mask), swap(values, axis, mask))
        relayed = []
        for (lib_mask, qry_mask), far_keys, far_values in early + late:
            far_keys, *_ = tie(far_keys, near[1], values)
            far_values, _ = tie(far_values, near[2])
            place = (lib_mask | mask, qry_mask)
            relayed.append((place, swap(far_keys, axis, mask), swap(far_values, axis, mask)))
        early, late = early + late + [near], relayed
    return early, late, partner_values, list(zip(masks, visitors))


def cross_cores(pieces, arrivals=()):
    crossed = []
    for (lib_mask, qry_mask), *pair in pieces:
        pair = tie(*pair, *arrivals)[:2]
        crossed.append(((lib_mask | 1, qry_mask), *(swap(array, "lib", 1) for array in pair)))
    return crossed


def places_of(pieces):
    return [piece[0] for piece in pieces]


def arrays_of(pieces):
    return [array for piece in pieces for array in piece[1:]]


def body(queries, library_keys, library_values, key_scale, block_list, block_count):
    qry_count = lax.axis_size("qry")
    width = library_keys.shape[1]
    value_width = library_values.shape[1]

    partner_keys = swap(library_keys, "lib", 1)
    own_values, _ = tie(library_values, partner_keys)
    values = pl.pallas_call(
        pack_kernel,
        out_shape=jax.ShapeDtypeStruct((TILE + EXTRA, value_width), jnp.bfloat16),
        in_specs=[pl.BlockSpec(memory_space=pl.ANY)] * 2,
        out_specs=VMEM,
        scratch_shapes=[pltpu.VMEM((1, TILE), jnp.bfloat16), pltpu.SemaphoreType.DMA((2,))],
        compiler_params=params(),
    )(own_values, key_scale.reshape(1, TILE))

    window_lists = block_list.T
    window_counts = block_count.reshape(1, -1)
    masks = [2 * at + 1 for at in range(1, qry_count // 2)]
    early, relayed, partner_values, visitors = gather_library(library_keys, values, queries, masks)
    piece_rows = (width // value_width + 1) * TILE + EXTRA
    cost = pl.CostEstimate(flops=2 * TILE * 4 * TILE * width * 2, bytes_accessed=4 * 1024 * 1024, transcendentals=0)
    total_shape = jax.ShapeDtypeStruct((TILE, value_width), jnp.float32)
    line_shape = jax.ShapeDtypeStruct((TILE, LANES), jnp.float32)
    pieces_total = 2 * (1 + len(early) + len(relayed))
    attend_params = params(pieces_total * piece_rows * value_width * 2)
    own_specs = [pl.BlockSpec(memory_space=pl.ANY), VMEM]
    own_scratch = [pltpu.VMEM(library_keys.shape, library_keys.dtype), pltpu.SemaphoreType.DMA]
    early_arrays = arrays_of(early)
    states = []
    for mask, visiting in visitors:
        state = pl.pallas_call(
            functools.partial(early_kernel, places_of(early), mask),
            out_shape=(jax.ShapeDtypeStruct(queries.shape[::-1], queries.dtype), total_shape, line_shape, line_shape),
            in_specs=[VMEM, VMEM] + [VMEM] * (1 + len(early_arrays)) + own_specs,
            out_specs=(VMEM,) * 4,
            scratch_shapes=[pltpu.VMEM((len(early) + 1, TILE, TILE), jnp.float32)] + own_scratch,
            compiler_params=attend_params,
            cost_estimate=cost,
        )(window_lists, window_counts, visiting, *early_arrays, library_keys, values)
        states.append(state)

    bundled = [(lib_mask | 1, qry_mask) for lib_mask, qry_mask in places_of(early)]
    early_values = [piece[2] for piece in early]
    bundle = pl.pallas_call(
        bundle_kernel,
        out_shape=jax.ShapeDtypeStruct((len(early) * (TILE + EXTRA), value_width), jnp.bfloat16),
        in_specs=[VMEM] * len(early),
        out_specs=VMEM,
        compiler_params=params(),
    )(*early_values)
    bundled_arrays = [swap(piece[1], "lib", 1) for piece in early] + [swap(bundle, "lib", 1)]
    late = [((1, 0), partner_keys, partner_values)] + relayed
    late += cross_cores(relayed, [state[3] for state in states])
    late_arrays = arrays_of(late) + bundled_arrays
    returned = []
    for (mask, _), state in zip(visitors, states):
        packed = pl.pallas_call(
            functools.partial(late_kernel, places_of(late), bundled, mask),
            out_shape=jax.ShapeDtypeStruct((TILE + EXTRA, value_width), jnp.bfloat16),
            in_specs=[VMEM, VMEM] + [VMEM] * (4 + len(late_arrays)),
            out_specs=VMEM,
            scratch_shapes=[
                pltpu.VMEM((len(late) + len(bundled), TILE, TILE), jnp.float32),
                pltpu.VMEM((TILE, value_width), jnp.float32),
                pltpu.VMEM((TILE, TILE), jnp.float32),
            ],
            compiler_params=attend_params,
            cost_estimate=cost,
        )(window_lists, window_counts, *state, *late_arrays)
        returned.append(swap(packed, "qry", mask))

    total, stats = pl.pallas_call(
        functools.partial(home_kernel, places_of(early + late), bundled),
        out_shape=(total_shape, jax.ShapeDtypeStruct((2, TILE, LANES), jnp.float32)),
        in_specs=[VMEM, VMEM] + [VMEM] * (1 + len(early_arrays) + len(late_arrays)) + own_specs,
        out_specs=(VMEM, VMEM),
        scratch_shapes=[
            pltpu.VMEM((pieces_total, TILE, TILE), jnp.float32),
            pltpu.VMEM((TILE, TILE), jnp.float32),
        ]
        + own_scratch,
        compiler_params=attend_params,
        cost_estimate=cost,
    )(window_lists, window_counts, queries, *early_arrays, *late_arrays, library_keys, values)

    return pl.pallas_call(
        merge_kernel,
        out_shape=jax.ShapeDtypeStruct((TILE, value_width), jnp.bfloat16),
        in_specs=[VMEM] * (2 + len(returned)),
        out_specs=VMEM,
        compiler_params=params(),
    )(total, stats, *returned)


def solution(mesh):
    in_specs = (
        P(("groups", "lib", "qry"), None),
        P(("groups", "lib", "qry"), None),
        P(("groups", "lib", "qry"), None),
        P(("groups", "lib", "qry")),
        P("groups", None),
        P("groups"),
    )
    out_specs = P(("groups", "lib", "qry"), None)
    return jax.shard_map(body, mesh=mesh, in_specs=in_specs, out_specs=out_specs, check_vma=False)
```

```python
import functools
import math

import jax
import jax.numpy as jnp
from jax import lax
from jax.experimental import pallas as pl
from jax.experimental.pallas import tpu as pltpu
from jax.sharding import PartitionSpec as P

TILE = 128
LANES = 128
EXTRA = 16
MASKED_SCORE = -1e30
VMEM = pl.BlockSpec(memory_space=pltpu.VMEM)


def params(operand_bytes=0):
    return pltpu.CompilerParams(vmem_limit_bytes=operand_bytes * 3 // 2 + 6 * 1024 * 1024)


def swap(value, axis, mask):
    length = lax.axis_size(axis)
    return lax.ppermute(value, axis, [(i, i ^ mask) for i in range(length)])


def tie(*values):
    return lax.optimization_barrier(values)


def split_three(value):
    high = value.astype(jnp.bfloat16)
    rest = value - high.astype(jnp.float32)
    middle = rest.astype(jnp.bfloat16)
    low = (rest - middle.astype(jnp.float32)).astype(jnp.bfloat16)
    return high, middle, low


def pack_kernel(values_ref, scale_ref, packed_ref, row_ref, sems):
    value_width = values_ref.shape[1]
    copies = (
        pltpu.make_async_copy(values_ref, packed_ref.at[pl.ds(0, TILE)], sems.at[0]),
        pltpu.make_async_copy(scale_ref, row_ref, sems.at[1]),
    )
    for copy in copies:
        copy.start()
    packed_ref[TILE:, TILE:] = jnp.zeros((EXTRA, value_width - TILE), jnp.bfloat16)
    for copy in reversed(copies):
        copy.wait()
    row = row_ref[...].astype(jnp.float32)
    packed_ref[TILE:, 0:TILE] = jnp.broadcast_to(row, (EXTRA, TILE)).astype(jnp.bfloat16)


class Piece:
    def __init__(self, place, keys_ref, values_ref, row=0, copy=None):
        self.place = place
        self.keys_ref = keys_ref
        self.values_ref = values_ref
        self.row = row
        self.copy = copy

    def scores(self, query_ref, inverse_root):
        product = lax.dot_general(
            query_ref[...], self.keys_ref[...], (((1,), (1,)), ((), ())), preferred_element_type=jnp.float32
        )
        scale = self.values_ref[self.row + TILE : self.row + TILE + EXTRA, 0:TILE]
        return product * (scale.astype(jnp.float32)[0:1] * inverse_root)

    def turned_scores(self, turned_ref, inverse_root):
        product = jnp.transpose(jnp.dot(self.keys_ref[...], turned_ref[...], preferred_element_type=jnp.float32))
        scale = self.values_ref[self.row + TILE : self.row + TILE + EXTRA, 0:TILE]
        return product * (scale.astype(jnp.float32)[0:1] * inverse_root)

    def values(self):
        return self.values_ref[self.row : self.row + TILE, :]


def read_pieces(places, refs, bundled=(), own=None):
    pieces = [Piece(place, refs[2 * at], refs[2 * at + 1]) for at, place in enumerate(places)]
    refs = refs[2 * len(places) :]
    if bundled:
        values_ref = refs[len(bundled)]
        pieces += [
            Piece(place, refs[at], values_ref, at * (TILE + EXTRA)) for at, place in enumerate(bundled)
        ]
        refs = refs[len(bundled) + 1 :]
    if own is not None:
        keys_ref, values_ref, *refs, held_ref, sem = refs
        copy = pltpu.make_async_copy(keys_ref, held_ref, sem)
        copy.start()
        pieces.append(Piece((0, 0), held_ref, values_ref, copy=copy))
    return pieces, refs


def bundle_kernel(*refs):
    *refs, bundle_ref = refs
    row = 0
    for ref in refs:
        bundle_ref[row : row + ref.shape[0], :] = ref[...]
        row += ref.shape[0]


def pick(ref, row, column):
    rows = lax.broadcasted_iota(jnp.int32, ref.shape, 0)
    columns = lax.broadcasted_iota(jnp.int32, ref.shape, 1)
    chosen = jnp.where((rows == row) & (columns == column), ref[...], 0)
    return jnp.sum(chosen.astype(jnp.float32)).astype(jnp.int32)


def attend(pieces, panel_mask, lists_ref, counts_ref, query_ref, score_ref, total_ref, mass_ref, before=None):
    lib_index = lax.axis_index("lib")
    qry_index = lax.axis_index("qry")
    qry_count = lax.axis_size("qry")
    block_total = lax.axis_size("lib") * qry_count
    panel = lib_index * qry_count + lax.bitwise_xor(qry_index, panel_mask)
    first = pick(lists_ref, 0, panel)
    count = pick(counts_ref, 0, panel)
    inverse_root = 1.0 / math.sqrt(pieces[0].keys_ref.shape[1])

    def active(lib_mask, qry_mask):
        block = lax.bitwise_xor(lib_index, lib_mask) * qry_count + lax.bitwise_xor(qry_index, qry_mask)
        return lax.rem(block - first + block_total, block_total) < count

    flags = [active(*piece.place) for piece in pieces]
    score_ref[...] = jnp.full(score_ref.shape, MASKED_SCORE, jnp.float32)
    for at, (piece, flag) in enumerate(zip(pieces, flags)):
        if piece.copy is not None:
            piece.copy.wait()

        @pl.when(flag)
        def _(at=at, piece=piece):
            scores = piece.scores if before is None else piece.turned_scores
            score_ref[at] = scores(query_ref, inverse_root)

    largest = score_ref[0]
    for at in range(1, len(flags)):
        largest = jnp.maximum(largest, score_ref[at])
    row_max = jnp.max(largest, axis=1, keepdims=True)
    if before is None:
        total_ref[...] = jnp.zeros(total_ref.shape, jnp.float32)
        mass_ref[...] = jnp.zeros(mass_ref.shape, jnp.float32)
    else:
        old_total_ref, old_mass_ref, old_max_ref = before
        old_max = old_max_ref[...]
        new_max = jnp.maximum(old_max, row_max)
        shrink = jnp.exp(old_max - new_max)
        row_max = new_max[:, 0:1]
        mass_ref[...] = old_mass_ref[...] * shrink
        for at in range(0, total_ref.shape[1], LANES):
            total_ref[:, at : at + LANES] = old_total_ref[:, at : at + LANES] * shrink
    for at, (piece, flag) in enumerate(zip(pieces, flags)):

        @pl.when(flag)
        def _(at=at, piece=piece):
            weights = jnp.exp(score_ref[at] - row_max)
            mass_ref[...] += weights
            weight_high = weights.astype(jnp.bfloat16)
            weight_low = (weights - weight_high.astype(jnp.float32)).astype(jnp.bfloat16)
            values = piece.values()
            added = jnp.dot(weight_high, values, preferred_element_type=jnp.float32)
            added = added + jnp.dot(weight_low, values, preferred_element_type=jnp.float32)
            total_ref[...] += added

    return row_max


def early_kernel(places, panel_mask, lists_ref, counts_ref, query_ref, *refs):
    pieces, refs = read_pieces(places, refs, own=True)
    turned_ref, total_ref, mass_ref, max_ref, score_ref = refs
    row_max = attend(pieces, panel_mask, lists_ref, counts_ref, query_ref, score_ref, total_ref, mass_ref)
    max_ref[...] = jnp.broadcast_to(row_max, max_ref.shape)
    turned_ref[...] = jnp.transpose(query_ref[...])


def late_kernel(places, bundled, panel_mask, lists_ref, counts_ref, turned_ref, *refs):
    before, refs = refs[:3], refs[3:]
    pieces, refs = read_pieces(places, refs, bundled)
    packed_ref, score_ref, total_ref, mass_ref = refs
    row_max = attend(pieces, panel_mask, lists_ref, counts_ref, turned_ref, score_ref, total_ref, mass_ref, before)
    row_sum = jnp.sum(mass_ref[...], axis=1, keepdims=True)
    value_width = total_ref.shape[1]
    inverse = 1.0 / jnp.where(row_sum > 0.0, row_sum, 1.0)
    packed_ref[0:TILE, :] = (total_ref[...] * inverse).astype(jnp.bfloat16)
    row = lax.broadcasted_iota(jnp.int32, (EXTRA, LANES), 0)
    packed = jnp.zeros((EXTRA, LANES), jnp.float32)
    for first, column in ((0, row_max), (3, row_sum)):
        turned = jnp.transpose(jnp.broadcast_to(column, (TILE, LANES)))[0:EXTRA]
        for at, part in enumerate(split_three(turned)):
            packed = jnp.where(row == first + at, part.astype(jnp.float32), packed)
    packed_ref[TILE:, 0:LANES] = packed.astype(jnp.bfloat16)
    packed_ref[TILE:, LANES:] = jnp.zeros((EXTRA, value_width - LANES), jnp.bfloat16)


def home_kernel(places, bundled, lists_ref, counts_ref, query_ref, *refs):
    pieces, refs = read_pieces(places, refs, bundled, own=True)
    total_ref, stats_ref, score_ref, mass_ref = refs
    row_max = attend(pieces, 0, lists_ref, counts_ref, query_ref, score_ref, total_ref, mass_ref)
    row_sum = jnp.sum(mass_ref[...], axis=1, keepdims=True)
    stats_ref[0] = jnp.broadcast_to(row_max, (TILE, LANES))
    stats_ref[1] = jnp.broadcast_to(row_sum, (TILE, LANES))


def merge_kernel(total_ref, stats_ref, *refs):
    *packed_refs, out_ref, held_ref, sems = refs
    maxima = [stats_ref[0]]
    sums = [stats_ref[1]]
    for packed_ref in packed_refs:
        packed = packed_ref[TILE:, 0:LANES].astype(jnp.float32)
        for first, kept in ((0, maxima), (3, sums)):
            line = packed[first : first + 1] + packed[first + 1 : first + 2] + packed[first + 2 : first + 3]
            kept.append(jnp.transpose(jnp.broadcast_to(line, (TILE, LANES))))
    top = functools.reduce(jnp.maximum, maxima)
    factors = [jnp.exp(row_max - top) for row_max in maxima]
    masses = [factor * row_sum for factor, row_sum in zip(factors, sums)]
    inverse = 1.0 / functools.reduce(jnp.add, masses)
    scales = [factors[0] * inverse] + [mass * inverse for mass in masses[1:]]
    rows = TILE // sems.shape[0]
    copies = []
    for group in range(sems.shape[0]):
        low, high = group * rows, (group + 1) * rows
        for at in range(0, total_ref.shape[1], LANES):
            merged = total_ref[low:high, at : at + LANES] * scales[0][low:high]
            for packed_ref, scale in zip(packed_refs, scales[1:]):
                merged = merged + packed_ref[low:high, at : at + LANES].astype(jnp.float32) * scale[low:high]
            held_ref[low:high, at : at + LANES] = merged.astype(jnp.bfloat16)
        span = pl.ds(low, rows)
        copies.append(pltpu.make_async_copy(held_ref.at[span], out_ref.at[span], sems.at[group]))
        copies[-1].start()
    for copy in copies:
        copy.wait()


def gather_library(keys, values, queries, masks):
    steps = [("qry", 1)]
    mask = lax.axis_size("lib") // 2
    while mask > 1:
        steps.append(("lib", mask))
        mask //= 2
    partner_values = swap(values, "lib", 1)
    leaving, _ = tie(queries, partner_values)
    visitors = [swap(leaving, "qry", mask) for mask in masks]
    early, late = [], []
    for axis, mask in steps:
        place = (0, mask) if axis == "qry" else (mask, 0)
        near = (place, swap(keys, axis, mask), swap(values, axis, mask))
        relayed = []
        for (lib_mask, qry_mask), far_keys, far_values in early + late:
            far_keys, *_ = tie(far_keys, near[1], values)
            far_values, _ = tie(far_values, near[2])
            place = (lib_mask | mask, qry_mask)
            relayed.append((place, swap(far_keys, axis, mask), swap(far_values, axis, mask)))
        early, late = early + late + [near], relayed
    return early, late, partner_values, list(zip(masks, visitors))


def cross_cores(pieces, arrivals=()):
    crossed = []
    for (lib_mask, qry_mask), *pair in pieces:
        pair = tie(*pair, *arrivals)[:2]
        crossed.append(((lib_mask | 1, qry_mask), *(swap(array, "lib", 1) for array in pair)))
    return crossed


def places_of(pieces):
    return [piece[0] for piece in pieces]


def arrays_of(pieces):
    return [array for piece in pieces for array in piece[1:]]


def body(queries, library_keys, library_values, key_scale, block_list, block_count):
    qry_count = lax.axis_size("qry")
    width = library_keys.shape[1]
    value_width = library_values.shape[1]

    partner_keys = swap(library_keys, "lib", 1)
    own_values, _ = tie(library_values, partner_keys)
    values = pl.pallas_call(
        pack_kernel,
        out_shape=jax.ShapeDtypeStruct((TILE + EXTRA, value_width), jnp.bfloat16),
        in_specs=[pl.BlockSpec(memory_space=pl.ANY)] * 2,
        out_specs=VMEM,
        scratch_shapes=[pltpu.VMEM((1, TILE), jnp.bfloat16), pltpu.SemaphoreType.DMA((2,))],
        compiler_params=params(),
    )(own_values, key_scale.reshape(1, TILE))

    window_lists = block_list.T
    window_counts = block_count.reshape(1, -1)
    masks = [2 * at + 1 for at in range(1, qry_count // 2)]
    early, relayed, partner_values, visitors = gather_library(library_keys, values, queries, masks)
    piece_rows = (width // value_width + 1) * TILE + EXTRA
    cost = pl.CostEstimate(flops=2 * TILE * 4 * TILE * width * 2, bytes_accessed=4 * 1024 * 1024, transcendentals=0)
    total_shape = jax.ShapeDtypeStruct((TILE, value_width), jnp.float32)
    line_shape = jax.ShapeDtypeStruct((TILE, LANES), jnp.float32)
    pieces_total = 2 * (1 + len(early) + len(relayed))
    attend_params = params(pieces_total * piece_rows * value_width * 2)
    own_specs = [pl.BlockSpec(memory_space=pl.ANY), VMEM]
    own_scratch = [pltpu.VMEM(library_keys.shape, library_keys.dtype), pltpu.SemaphoreType.DMA]
    early_arrays = arrays_of(early)
    states = []
    for mask, visiting in visitors:
        state = pl.pallas_call(
            functools.partial(early_kernel, places_of(early), mask),
            out_shape=(jax.ShapeDtypeStruct(queries.shape[::-1], queries.dtype), total_shape, line_shape, line_shape),
            in_specs=[VMEM, VMEM] + [VMEM] * (1 + len(early_arrays)) + own_specs,
            out_specs=(VMEM,) * 4,
            scratch_shapes=[pltpu.VMEM((len(early) + 1, TILE, TILE), jnp.float32)] + own_scratch,
            compiler_params=attend_params,
            cost_estimate=cost,
        )(window_lists, window_counts, visiting, *early_arrays, library_keys, values)
        states.append(state)

    bundled = [(lib_mask | 1, qry_mask) for lib_mask, qry_mask in places_of(early)]
    early_values = [piece[2] for piece in early]
    bundle = pl.pallas_call(
        bundle_kernel,
        out_shape=jax.ShapeDtypeStruct((len(early) * (TILE + EXTRA), value_width), jnp.bfloat16),
        in_specs=[VMEM] * len(early),
        out_specs=VMEM,
        compiler_params=params(),
    )(*early_values)
    bundled_arrays = [swap(piece[1], "lib", 1) for piece in early] + [swap(bundle, "lib", 1)]
    late = [((1, 0), partner_keys, partner_values)] + relayed
    late += cross_cores(relayed, [state[3] for state in states])
    late_arrays = arrays_of(late) + bundled_arrays
    returned = []
    for (mask, _), state in zip(visitors, states):
        packed = pl.pallas_call(
            functools.partial(late_kernel, places_of(late), bundled, mask),
            out_shape=jax.ShapeDtypeStruct((TILE + EXTRA, value_width), jnp.bfloat16),
            in_specs=[VMEM, VMEM] + [VMEM] * (4 + len(late_arrays)),
            out_specs=VMEM,
            scratch_shapes=[
                pltpu.VMEM((len(late) + len(bundled), TILE, TILE), jnp.float32),
                pltpu.VMEM((TILE, value_width), jnp.float32),
                pltpu.VMEM((TILE, TILE), jnp.float32),
            ],
            compiler_params=attend_params,
            cost_estimate=cost,
        )(window_lists, window_counts, *state, *late_arrays)
        returned.append(swap(packed, "qry", mask))

    total, stats = pl.pallas_call(
        functools.partial(home_kernel, places_of(early + late), bundled),
        out_shape=(total_shape, jax.ShapeDtypeStruct((2, TILE, LANES), jnp.float32)),
        in_specs=[VMEM, VMEM] + [VMEM] * (1 + len(early_arrays) + len(late_arrays)) + own_specs,
        out_specs=(VMEM, VMEM),
        scratch_shapes=[
            pltpu.VMEM((pieces_total, TILE, TILE), jnp.float32),
            pltpu.VMEM((TILE, TILE), jnp.float32),
        ]
        + own_scratch,
        compiler_params=attend_params,
        cost_estimate=cost,
    )(window_lists, window_counts, queries, *early_arrays, *late_arrays, library_keys, values)

    return pl.pallas_call(
        merge_kernel,
        out_shape=jax.ShapeDtypeStruct((TILE, value_width), jnp.bfloat16),
        in_specs=[VMEM] * (2 + len(returned)),
        out_specs=pl.BlockSpec(memory_space=pl.ANY),
        scratch_shapes=[pltpu.VMEM((TILE, value_width), jnp.bfloat16), pltpu.SemaphoreType.DMA((4,))],
        compiler_params=params(),
    )(total, stats, *returned)


def solution(mesh):
    in_specs = (
        P(("groups", "lib", "qry"), None),
        P(("groups", "lib", "qry"), None),
        P(("groups", "lib", "qry"), None),
        P(("groups", "lib", "qry")),
        P("groups", None),
        P("groups"),
    )
    out_specs = P(("groups", "lib", "qry"), None)
    return jax.shard_map(body, mesh=mesh, in_specs=in_specs, out_specs=out_specs, check_vma=False)
```

```python
import functools
import math

import jax
import jax.numpy as jnp
from jax import lax
from jax.experimental import pallas as pl
from jax.experimental.pallas import tpu as pltpu
from jax.sharding import PartitionSpec as P

TILE = 128
LANES = 128
EXTRA = 16
MASKED_SCORE = -1e30
VMEM = pl.BlockSpec(memory_space=pltpu.VMEM)


def params(operand_bytes=0):
    return pltpu.CompilerParams(vmem_limit_bytes=operand_bytes * 3 // 2 + 6 * 1024 * 1024)


def swap(value, axis, mask):
    length = lax.axis_size(axis)
    return lax.ppermute(value, axis, [(i, i ^ mask) for i in range(length)])


def tie(*values):
    return lax.optimization_barrier(values)


def split_three(value):
    high = value.astype(jnp.bfloat16)
    rest = value - high.astype(jnp.float32)
    middle = rest.astype(jnp.bfloat16)
    low = (rest - middle.astype(jnp.float32)).astype(jnp.bfloat16)
    return high, middle, low


def pack_kernel(values_ref, scale_ref, packed_ref, row_ref, sems):
    value_width = values_ref.shape[1]
    copies = (
        pltpu.make_async_copy(values_ref, packed_ref.at[pl.ds(0, TILE)], sems.at[0]),
        pltpu.make_async_copy(scale_ref, row_ref, sems.at[1]),
    )
    for copy in copies:
        copy.start()
    packed_ref[TILE:, TILE:] = jnp.zeros((EXTRA, value_width - TILE), jnp.bfloat16)
    for copy in reversed(copies):
        copy.wait()
    row = row_ref[...].astype(jnp.float32)
    packed_ref[TILE:, 0:TILE] = jnp.broadcast_to(row, (EXTRA, TILE)).astype(jnp.bfloat16)


class Piece:
    def __init__(self, place, keys_ref, values_ref, row=0, copy=None):
        self.place = place
        self.keys_ref = keys_ref
        self.values_ref = values_ref
        self.row = row
        self.copy = copy

    def scores(self, query_ref, inverse_root):
        product = lax.dot_general(
            query_ref[...], self.keys_ref[...], (((1,), (1,)), ((), ())), preferred_element_type=jnp.float32
        )
        scale = self.values_ref[self.row + TILE : self.row + TILE + EXTRA, 0:TILE]
        return product * (scale.astype(jnp.float32)[0:1] * inverse_root)

    def turned_scores(self, turned_ref, inverse_root):
        product = jnp.transpose(jnp.dot(self.keys_ref[...], turned_ref[...], preferred_element_type=jnp.float32))
        scale = self.values_ref[self.row + TILE : self.row + TILE + EXTRA, 0:TILE]
        return product * (scale.astype(jnp.float32)[0:1] * inverse_root)

    def values(self):
        return self.values_ref[self.row : self.row + TILE, :]


def read_pieces(places, refs, bundled=(), own=None):
    pieces = [Piece(place, refs[2 * at], refs[2 * at + 1]) for at, place in enumerate(places)]
    refs = refs[2 * len(places) :]
    if bundled:
        values_ref = refs[len(bundled)]
        pieces += [
            Piece(place, refs[at], values_ref, at * (TILE + EXTRA)) for at, place in enumerate(bundled)
        ]
        refs = refs[len(bundled) + 1 :]
    if own is not None:
        keys_ref, values_ref, *refs, held_ref, sem = refs
        copy = pltpu.make_async_copy(keys_ref, held_ref, sem)
        copy.start()
        pieces.append(Piece((0, 0), held_ref, values_ref, copy=copy))
    return pieces, refs


def bundle_kernel(*refs):
    *refs, bundle_ref = refs
    row = 0
    for ref in refs:
        bundle_ref[row : row + ref.shape[0], :] = ref[...]
        row += ref.shape[0]


def window_kernel(lists_ref, counts_ref, windows_ref):
    windows_ref[0:1, :] = lists_ref[0:1, :]
    windows_ref[1:2, :] = counts_ref[...]


def pick(ref, row, column):
    rows = lax.broadcasted_iota(jnp.int32, ref.shape, 0)
    columns = lax.broadcasted_iota(jnp.int32, ref.shape, 1)
    chosen = jnp.where((rows == row) & (columns == column), ref[...], 0)
    return jnp.sum(chosen.astype(jnp.float32)).astype(jnp.int32)


def attend(pieces, panel_mask, windows_ref, query_ref, score_ref, total_ref, mass_ref, before=None):
    lib_index = lax.axis_index("lib")
    qry_index = lax.axis_index("qry")
    qry_count = lax.axis_size("qry")
    block_total = lax.axis_size("lib") * qry_count
    panel = lib_index * qry_count + lax.bitwise_xor(qry_index, panel_mask)
    first = pick(windows_ref, 0, panel)
    count = pick(windows_ref, 1, panel)
    inverse_root = 1.0 / math.sqrt(pieces[0].keys_ref.shape[1])

    def active(lib_mask, qry_mask):
        block = lax.bitwise_xor(lib_index, lib_mask) * qry_count + lax.bitwise_xor(qry_index, qry_mask)
        return lax.rem(block - first + block_total, block_total) < count

    flags = [active(*piece.place) for piece in pieces]
    score_ref[...] = jnp.full(score_ref.shape, MASKED_SCORE, jnp.float32)
    for at, (piece, flag) in enumerate(zip(pieces, flags)):
        if piece.copy is not None:
            piece.copy.wait()

        @pl.when(flag)
        def _(at=at, piece=piece):
            scores = piece.scores if before is None else piece.turned_scores
            score_ref[at] = scores(query_ref, inverse_root)

    largest = score_ref[0]
    for at in range(1, len(flags)):
        largest = jnp.maximum(largest, score_ref[at])
    row_max = jnp.max(largest, axis=1, keepdims=True)
    if before is None:
        total_ref[...] = jnp.zeros(total_ref.shape, jnp.float32)
        mass_ref[...] = jnp.zeros(mass_ref.shape, jnp.float32)
    else:
        old_total_ref, old_mass_ref, old_max_ref = before
        old_max = old_max_ref[...]
        new_max = jnp.maximum(old_max, row_max)
        shrink = jnp.exp(old_max - new_max)
        row_max = new_max[:, 0:1]
        mass_ref[...] = old_mass_ref[...] * shrink
        for at in range(0, total_ref.shape[1], LANES):
            total_ref[:, at : at + LANES] = old_total_ref[:, at : at + LANES] * shrink
    for at, (piece, flag) in enumerate(zip(pieces, flags)):

        @pl.when(flag)
        def _(at=at, piece=piece):
            weights = jnp.exp(score_ref[at] - row_max)
            mass_ref[...] += weights
            weight_high = weights.astype(jnp.bfloat16)
            weight_low = (weights - weight_high.astype(jnp.float32)).astype(jnp.bfloat16)
            values = piece.values()
            added = jnp.dot(weight_high, values, preferred_element_type=jnp.float32)
            added = added + jnp.dot(weight_low, values, preferred_element_type=jnp.float32)
            total_ref[...] += added

    return row_max


def early_kernel(places, panel_mask, windows_ref, query_ref, *refs):
    pieces, refs = read_pieces(places, refs, own=True)
    turned_ref, total_ref, mass_ref, max_ref, score_ref = refs
    row_max = attend(pieces, panel_mask, windows_ref, query_ref, score_ref, total_ref, mass_ref)
    max_ref[...] = jnp.broadcast_to(row_max, max_ref.shape)
    turned_ref[...] = jnp.transpose(query_ref[...])


def late_kernel(places, bundled, panel_mask, windows_ref, turned_ref, *refs):
    before, refs = refs[:3], refs[3:]
    pieces, refs = read_pieces(places, refs, bundled)
    packed_ref, score_ref, total_ref, mass_ref = refs
    row_max = attend(pieces, panel_mask, windows_ref, turned_ref, score_ref, total_ref, mass_ref, before)
    row_sum = jnp.sum(mass_ref[...], axis=1, keepdims=True)
    value_width = total_ref.shape[1]
    inverse = 1.0 / jnp.where(row_sum > 0.0, row_sum, 1.0)
    packed_ref[0:TILE, :] = (total_ref[...] * inverse).astype(jnp.bfloat16)
    row = lax.broadcasted_iota(jnp.int32, (EXTRA, LANES), 0)
    packed = jnp.zeros((EXTRA, LANES), jnp.float32)
    for first, column in ((0, row_max), (3, row_sum)):
        turned = jnp.transpose(jnp.broadcast_to(column, (TILE, LANES)))[0:EXTRA]
        for at, part in enumerate(split_three(turned)):
            packed = jnp.where(row == first + at, part.astype(jnp.float32), packed)
    packed_ref[TILE:, 0:LANES] = packed.astype(jnp.bfloat16)
    packed_ref[TILE:, LANES:] = jnp.zeros((EXTRA, value_width - LANES), jnp.bfloat16)


def home_kernel(places, bundled, windows_ref, query_ref, *refs):
    pieces, refs = read_pieces(places, refs, bundled, own=True)
    total_ref, stats_ref, score_ref, mass_ref = refs
    row_max = attend(pieces, 0, windows_ref, query_ref, score_ref, total_ref, mass_ref)
    row_sum = jnp.sum(mass_ref[...], axis=1, keepdims=True)
    stats_ref[0] = jnp.broadcast_to(row_max, (TILE, LANES))
    stats_ref[1] = jnp.broadcast_to(row_sum, (TILE, LANES))


def merge_kernel(total_ref, stats_ref, *refs):
    packed_refs, out_ref = refs[:-1], refs[-1]
    maxima = [stats_ref[0]]
    sums = [stats_ref[1]]
    for packed_ref in packed_refs:
        packed = packed_ref[TILE:, 0:LANES].astype(jnp.float32)
        for first, kept in ((0, maxima), (3, sums)):
            line = packed[first : first + 1] + packed[first + 1 : first + 2] + packed[first + 2 : first + 3]
            kept.append(jnp.transpose(jnp.broadcast_to(line, (TILE, LANES))))
    top = functools.reduce(jnp.maximum, maxima)
    factors = [jnp.exp(row_max - top) for row_max in maxima]
    masses = [factor * row_sum for factor, row_sum in zip(factors, sums)]
    inverse = 1.0 / functools.reduce(jnp.add, masses)
    scales = [factors[0] * inverse] + [mass * inverse for mass in masses[1:]]
    for at in range(0, total_ref.shape[1], LANES):
        merged = total_ref[:, at : at + LANES] * scales[0]
        for packed_ref, scale in zip(packed_refs, scales[1:]):
            merged = merged + packed_ref[0:TILE, at : at + LANES].astype(jnp.float32) * scale
        out_ref[:, at : at + LANES] = merged.astype(jnp.bfloat16)


def gather_library(keys, values, queries, windows, masks):
    steps = [("qry", 1)]
    mask = lax.axis_size("lib") // 2
    while mask > 1:
        steps.append(("lib", mask))
        mask //= 2
    partner_values = swap(values, "lib", 1)
    leaving, *_ = tie(queries, partner_values, windows)
    visitors = [swap(leaving, "qry", mask) for mask in masks]
    early, late = [], []
    for axis, mask in steps:
        place = (0, mask) if axis == "qry" else (mask, 0)
        near = (place, swap(keys, axis, mask), swap(values, axis, mask))
        relayed = []
        for (lib_mask, qry_mask), far_keys, far_values in early + late:
            far_keys, *_ = tie(far_keys, near[1], values)
            far_values, _ = tie(far_values, near[2])
            place = (lib_mask | mask, qry_mask)
            relayed.append((place, swap(far_keys, axis, mask), swap(far_values, axis, mask)))
        early, late = early + late + [near], relayed
    return early, late, partner_values, list(zip(masks, visitors))


def cross_cores(pieces, arrivals=()):
    crossed = []
    for (lib_mask, qry_mask), *pair in pieces:
        pair = tie(*pair, *arrivals)[:2]
        crossed.append(((lib_mask | 1, qry_mask), *(swap(array, "lib", 1) for array in pair)))
    return crossed


def places_of(pieces):
    return [piece[0] for piece in pieces]


def arrays_of(pieces):
    return [array for piece in pieces for array in piece[1:]]


def body(queries, library_keys, library_values, key_scale, block_list, block_count):
    qry_count = lax.axis_size("qry")
    width = library_keys.shape[1]
    value_width = library_values.shape[1]

    partner_keys = swap(library_keys, "lib", 1)
    own_values, _ = tie(library_values, partner_keys)
    values = pl.pallas_call(
        pack_kernel,
        out_shape=jax.ShapeDtypeStruct((TILE + EXTRA, value_width), jnp.bfloat16),
        in_specs=[pl.BlockSpec(memory_space=pl.ANY)] * 2,
        out_specs=VMEM,
        scratch_shapes=[pltpu.VMEM((1, TILE), jnp.bfloat16), pltpu.SemaphoreType.DMA((2,))],
        compiler_params=params(),
    )(own_values, key_scale.reshape(1, TILE))

    windows = pl.pallas_call(
        window_kernel,
        out_shape=jax.ShapeDtypeStruct((2, block_list.shape[0]), jnp.int32),
        in_specs=[VMEM, VMEM],
        out_specs=VMEM,
        compiler_params=params(),
    )(block_list.T, block_count.reshape(1, -1))
    masks = [2 * at + 1 for at in range(1, qry_count // 2)]
    early, relayed, partner_values, visitors = gather_library(library_keys, values, queries, windows, masks)
    piece_rows = (width // value_width + 1) * TILE + EXTRA
    cost = pl.CostEstimate(flops=2 * TILE * 4 * TILE * width * 2, bytes_accessed=4 * 1024 * 1024, transcendentals=0)
    total_shape = jax.ShapeDtypeStruct((TILE, value_width), jnp.float32)
    line_shape = jax.ShapeDtypeStruct((TILE, LANES), jnp.float32)
    pieces_total = 2 * (1 + len(early) + len(relayed))
    attend_params = params(pieces_total * piece_rows * value_width * 2)
    own_specs = [pl.BlockSpec(memory_space=pl.ANY), VMEM]
    own_scratch = [pltpu.VMEM(library_keys.shape, library_keys.dtype), pltpu.SemaphoreType.DMA]
    early_arrays = arrays_of(early)
    states = []
    for mask, visiting in visitors:
        state = pl.pallas_call(
            functools.partial(early_kernel, places_of(early), mask),
            out_shape=(jax.ShapeDtypeStruct(queries.shape[::-1], queries.dtype), total_shape, line_shape, line_shape),
            in_specs=[VMEM] * (2 + len(early_arrays)) + own_specs,
            out_specs=(VMEM,) * 4,
            scratch_shapes=[pltpu.VMEM((len(early) + 1, TILE, TILE), jnp.float32)] + own_scratch,
            compiler_params=attend_params,
            cost_estimate=cost,
        )(windows, visiting, *early_arrays, library_keys, values)
        states.append(state)

    bundled = [(lib_mask | 1, qry_mask) for lib_mask, qry_mask in places_of(early)]
    early_values = [piece[2] for piece in early]
    bundle = pl.pallas_call(
        bundle_kernel,
        out_shape=jax.ShapeDtypeStruct((len(early) * (TILE + EXTRA), value_width), jnp.bfloat16),
        in_specs=[VMEM] * len(early),
        out_specs=VMEM,
        compiler_params=params(),
    )(*early_values)
    bundled_arrays = [swap(piece[1], "lib", 1) for piece in early] + [swap(bundle, "lib", 1)]
    late = [((1, 0), partner_keys, partner_values)] + relayed
    late += cross_cores(relayed, [state[3] for state in states])
    late_arrays = arrays_of(late) + bundled_arrays
    returned = []
    for (mask, _), state in zip(visitors, states):
        packed = pl.pallas_call(
            functools.partial(late_kernel, places_of(late), bundled, mask),
            out_shape=jax.ShapeDtypeStruct((TILE + EXTRA, value_width), jnp.bfloat16),
            in_specs=[VMEM] * (5 + len(late_arrays)),
            out_specs=VMEM,
            scratch_shapes=[
                pltpu.VMEM((len(late) + len(bundled), TILE, TILE), jnp.float32),
                pltpu.VMEM((TILE, value_width), jnp.float32),
                pltpu.VMEM((TILE, TILE), jnp.float32),
            ],
            compiler_params=attend_params,
            cost_estimate=cost,
        )(windows, *state, *late_arrays)
        returned.append(swap(packed, "qry", mask))

    total, stats = pl.pallas_call(
        functools.partial(home_kernel, places_of(early + late), bundled),
        out_shape=(total_shape, jax.ShapeDtypeStruct((2, TILE, LANES), jnp.float32)),
        in_specs=[VMEM] * (2 + len(early_arrays) + len(late_arrays)) + own_specs,
        out_specs=(VMEM, VMEM),
        scratch_shapes=[
            pltpu.VMEM((pieces_total, TILE, TILE), jnp.float32),
            pltpu.VMEM((TILE, TILE), jnp.float32),
        ]
        + own_scratch,
        compiler_params=attend_params,
        cost_estimate=cost,
    )(windows, queries, *early_arrays, *late_arrays, library_keys, values)

    return pl.pallas_call(
        merge_kernel,
        out_shape=jax.ShapeDtypeStruct((TILE, value_width), jnp.bfloat16),
        in_specs=[VMEM] * (2 + len(returned)),
        out_specs=VMEM,
        compiler_params=params(),
    )(total, stats, *returned)


def solution(mesh):
    in_specs = (
        P(("groups", "lib", "qry"), None),
        P(("groups", "lib", "qry"), None),
        P(("groups", "lib", "qry"), None),
        P(("groups", "lib", "qry")),
        P("groups", None),
        P("groups"),
    )
    out_specs = P(("groups", "lib", "qry"), None)
    return jax.shard_map(body, mesh=mesh, in_specs=in_specs, out_specs=out_specs, check_vma=False)
```

```python
import functools
import math

import jax
import jax.numpy as jnp
from jax import lax
from jax.experimental import pallas as pl
from jax.experimental.pallas import tpu as pltpu
from jax.sharding import PartitionSpec as P

TILE = 128
LANES = 128
EXTRA = 16
MASKED_SCORE = -1e30
VMEM = pl.BlockSpec(memory_space=pltpu.VMEM)


def params(operand_bytes=0):
    return pltpu.CompilerParams(vmem_limit_bytes=operand_bytes * 3 // 2 + 6 * 1024 * 1024)


def swap(value, axis, mask):
    length = lax.axis_size(axis)
    return lax.ppermute(value, axis, [(i, i ^ mask) for i in range(length)])


def tie(*values):
    return lax.optimization_barrier(values)


def split_three(value):
    high = value.astype(jnp.bfloat16)
    rest = value - high.astype(jnp.float32)
    middle = rest.astype(jnp.bfloat16)
    low = (rest - middle.astype(jnp.float32)).astype(jnp.bfloat16)
    return high, middle, low


def pack_kernel(values_ref, scale_ref, packed_ref, row_ref, sems):
    value_width = values_ref.shape[1]
    copies = (
        pltpu.make_async_copy(values_ref, packed_ref.at[pl.ds(0, TILE)], sems.at[0]),
        pltpu.make_async_copy(scale_ref, row_ref, sems.at[1]),
    )
    for copy in copies:
        copy.start()
    packed_ref[TILE:, TILE:] = jnp.zeros((EXTRA, value_width - TILE), jnp.bfloat16)
    for copy in reversed(copies):
        copy.wait()
    row = row_ref[...].astype(jnp.float32)
    packed_ref[TILE:, 0:TILE] = jnp.broadcast_to(row, (EXTRA, TILE)).astype(jnp.bfloat16)


class Piece:
    def __init__(self, place, keys_ref, values_ref, row=0, copy=None):
        self.place = place
        self.keys_ref = keys_ref
        self.values_ref = values_ref
        self.row = row
        self.copy = copy

    def scores(self, query_ref, inverse_root):
        product = lax.dot_general(
            query_ref[...], self.keys_ref[...], (((1,), (1,)), ((), ())), preferred_element_type=jnp.float32
        )
        scale = self.values_ref[self.row + TILE : self.row + TILE + EXTRA, 0:TILE]
        return product * (scale.astype(jnp.float32)[0:1] * inverse_root)

    def turned_scores(self, turned_ref, inverse_root):
        product = jnp.transpose(jnp.dot(self.keys_ref[...], turned_ref[...], preferred_element_type=jnp.float32))
        scale = self.values_ref[self.row + TILE : self.row + TILE + EXTRA, 0:TILE]
        return product * (scale.astype(jnp.float32)[0:1] * inverse_root)

    def values(self):
        return self.values_ref[self.row : self.row + TILE, :]


def read_pieces(places, refs, bundled=(), own=None):
    pieces = [Piece(place, refs[2 * at], refs[2 * at + 1]) for at, place in enumerate(places)]
    refs = refs[2 * len(places) :]
    if bundled:
        values_ref = refs[len(bundled)]
        pieces += [
            Piece(place, refs[at], values_ref, at * (TILE + EXTRA)) for at, place in enumerate(bundled)
        ]
        refs = refs[len(bundled) + 1 :]
    if own is not None:
        keys_ref, values_ref, *refs, held_ref, sem = refs
        copy = pltpu.make_async_copy(keys_ref, held_ref, sem)
        copy.start()
        pieces.append(Piece((0, 0), held_ref, values_ref, copy=copy))
    return pieces, refs


def bundle_kernel(*refs):
    *refs, bundle_ref = refs
    row = 0
    for ref in refs:
        bundle_ref[row : row + ref.shape[0], :] = ref[...]
        row += ref.shape[0]


def window_kernel(lists_ref, counts_ref, windows_ref):
    windows_ref[0:1, :] = lists_ref[0:1, :]
    windows_ref[1:2, :] = counts_ref[...]


def pick(ref, row, column):
    rows = lax.broadcasted_iota(jnp.int32, ref.shape, 0)
    columns = lax.broadcasted_iota(jnp.int32, ref.shape, 1)
    chosen = jnp.where((rows == row) & (columns == column), ref[...], 0)
    return jnp.sum(chosen.astype(jnp.float32)).astype(jnp.int32)


def attend(pieces, panel_mask, windows_ref, query_ref, score_ref, total_ref, mass_ref, before=None):
    lib_index = lax.axis_index("lib")
    qry_index = lax.axis_index("qry")
    qry_count = lax.axis_size("qry")
    block_total = lax.axis_size("lib") * qry_count
    panel = lib_index * qry_count + lax.bitwise_xor(qry_index, panel_mask)
    first = pick(windows_ref, 0, panel)
    count = pick(windows_ref, 1, panel)
    inverse_root = 1.0 / math.sqrt(pieces[0].keys_ref.shape[1])

    def active(lib_mask, qry_mask):
        block = lax.bitwise_xor(lib_index, lib_mask) * qry_count + lax.bitwise_xor(qry_index, qry_mask)
        return lax.rem(block - first + block_total, block_total) < count

    flags = [active(*piece.place) for piece in pieces]
    score_ref[...] = jnp.full(score_ref.shape, MASKED_SCORE, jnp.float32)
    for at, (piece, flag) in enumerate(zip(pieces, flags)):
        if piece.copy is not None:
            piece.copy.wait()

        @pl.when(flag)
        def _(at=at, piece=piece):
            scores = piece.scores if before is None else piece.turned_scores
            score_ref[at] = scores(query_ref, inverse_root)

    largest = score_ref[0]
    for at in range(1, len(flags)):
        largest = jnp.maximum(largest, score_ref[at])
    row_max = jnp.max(largest, axis=1, keepdims=True)
    if before is None:
        total_ref[...] = jnp.zeros(total_ref.shape, jnp.float32)
        mass_ref[...] = jnp.zeros(mass_ref.shape, jnp.float32)
    else:
        old_total_ref, old_mass_ref, old_max_ref = before
        old_max = old_max_ref[...]
        new_max = jnp.maximum(old_max, row_max)
        shrink = jnp.exp(old_max - new_max)
        row_max = new_max[:, 0:1]
        mass_ref[...] = old_mass_ref[...] * shrink
        for at in range(0, total_ref.shape[1], LANES):
            total_ref[:, at : at + LANES] = old_total_ref[:, at : at + LANES] * shrink
    for at, (piece, flag) in enumerate(zip(pieces, flags)):

        @pl.when(flag)
        def _(at=at, piece=piece):
            weights = jnp.exp(score_ref[at] - row_max)
            mass_ref[...] += weights
            weight_high = weights.astype(jnp.bfloat16)
            weight_low = (weights - weight_high.astype(jnp.float32)).astype(jnp.bfloat16)
            values = piece.values()
            added = jnp.dot(weight_high, values, preferred_element_type=jnp.float32)
            added = added + jnp.dot(weight_low, values, preferred_element_type=jnp.float32)
            total_ref[...] += added

    return row_max


def early_kernel(places, panel_mask, windows_ref, query_ref, *refs):
    pieces, refs = read_pieces(places, refs, own=True)
    turned_ref, total_ref, mass_ref, max_ref, score_ref = refs
    row_max = attend(pieces, panel_mask, windows_ref, query_ref, score_ref, total_ref, mass_ref)
    max_ref[...] = jnp.broadcast_to(row_max, max_ref.shape)
    turned_ref[...] = jnp.transpose(query_ref[...])


def late_kernel(places, bundled, panel_mask, windows_ref, turned_ref, *refs):
    before, refs = refs[:3], refs[3:]
    pieces, refs = read_pieces(places, refs, bundled)
    packed_ref, score_ref, total_ref, mass_ref = refs
    row_max = attend(pieces, panel_mask, windows_ref, turned_ref, score_ref, total_ref, mass_ref, before)
    row_sum = jnp.sum(mass_ref[...], axis=1, keepdims=True)
    value_width = total_ref.shape[1]
    inverse = 1.0 / jnp.where(row_sum > 0.0, row_sum, 1.0)
    packed_ref[0:TILE, :] = (total_ref[...] * inverse).astype(jnp.bfloat16)
    row = lax.broadcasted_iota(jnp.int32, (EXTRA, LANES), 0)
    packed = jnp.zeros((EXTRA, LANES), jnp.float32)
    for first, column in ((0, row_max), (3, row_sum)):
        turned = jnp.transpose(jnp.broadcast_to(column, (TILE, LANES)))[0:EXTRA]
        for at, part in enumerate(split_three(turned)):
            packed = jnp.where(row == first + at, part.astype(jnp.float32), packed)
    packed_ref[TILE:, 0:LANES] = packed.astype(jnp.bfloat16)
    packed_ref[TILE:, LANES:] = jnp.zeros((EXTRA, value_width - LANES), jnp.bfloat16)


def home_kernel(places, bundled, windows_ref, query_ref, *refs):
    pieces, refs = read_pieces(places, refs, bundled, own=True)
    total_ref, stats_ref, score_ref, mass_ref = refs
    row_max = attend(pieces, 0, windows_ref, query_ref, score_ref, total_ref, mass_ref)
    row_sum = jnp.sum(mass_ref[...], axis=1, keepdims=True)
    stats_ref[0] = jnp.broadcast_to(row_max, (TILE, LANES))
    stats_ref[1] = jnp.broadcast_to(row_sum, (TILE, LANES))


def merge_kernel(total_ref, stats_ref, *refs):
    packed_refs, out_ref = refs[:-1], refs[-1]
    maxima = [stats_ref[0]]
    sums = [stats_ref[1]]
    for packed_ref in packed_refs:
        packed = packed_ref[TILE:, 0:LANES].astype(jnp.float32)
        for first, kept in ((0, maxima), (3, sums)):
            line = packed[first : first + 1] + packed[first + 1 : first + 2] + packed[first + 2 : first + 3]
            kept.append(jnp.transpose(jnp.broadcast_to(line, (TILE, LANES))))
    top = functools.reduce(jnp.maximum, maxima)
    factors = [jnp.exp(row_max - top) for row_max in maxima]
    masses = [factor * row_sum for factor, row_sum in zip(factors, sums)]
    inverse = 1.0 / functools.reduce(jnp.add, masses)
    scales = [factors[0] * inverse] + [mass * inverse for mass in masses[1:]]
    for at in range(0, total_ref.shape[1], LANES):
        merged = total_ref[:, at : at + LANES] * scales[0]
        for packed_ref, scale in zip(packed_refs, scales[1:]):
            merged = merged + packed_ref[0:TILE, at : at + LANES].astype(jnp.float32) * scale
        out_ref[:, at : at + LANES] = merged.astype(jnp.bfloat16)


def gather_library(keys, values, queries, windows, masks):
    steps = [("qry", 1)]
    mask = lax.axis_size("lib") // 2
    while mask > 1:
        steps.append(("lib", mask))
        mask //= 2
    partner_values = swap(values, "lib", 1)
    leaving, *_ = tie(queries, partner_values, windows)
    visitors = [swap(leaving, "qry", mask) for mask in masks]
    early, late = [], []
    for axis, mask in steps:
        place = (0, mask) if axis == "qry" else (mask, 0)
        near = (place, swap(keys, axis, mask), swap(values, axis, mask))
        relayed = []
        for (lib_mask, qry_mask), far_keys, far_values in early + late:
            far_keys, *_ = tie(far_keys, near[1], values)
            far_values, _ = tie(far_values, near[2])
            place = (lib_mask | mask, qry_mask)
            relayed.append((place, swap(far_keys, axis, mask), swap(far_values, axis, mask)))
        early, late = early + late + [near], relayed
    return early, late, partner_values, list(zip(masks, visitors))


def cross_cores(pieces, arrivals=()):
    crossed = []
    for (lib_mask, qry_mask), *pair in pieces:
        pair = tie(*pair, *arrivals)[:2]
        crossed.append(((lib_mask | 1, qry_mask), *(swap(array, "lib", 1) for array in pair)))
    return crossed


def places_of(pieces):
    return [piece[0] for piece in pieces]


def arrays_of(pieces):
    return [array for piece in pieces for array in piece[1:]]


def body(queries, library_keys, library_values, key_scale, block_list, block_count):
    qry_count = lax.axis_size("qry")
    width = library_keys.shape[1]
    value_width = library_values.shape[1]

    partner_keys = swap(library_keys, "lib", 1)
    own_values, _ = tie(library_values, partner_keys)
    values = pl.pallas_call(
        pack_kernel,
        out_shape=jax.ShapeDtypeStruct((TILE + EXTRA, value_width), jnp.bfloat16),
        in_specs=[pl.BlockSpec(memory_space=pl.ANY)] * 2,
        out_specs=VMEM,
        scratch_shapes=[pltpu.VMEM((1, TILE), jnp.bfloat16), pltpu.SemaphoreType.DMA((2,))],
        compiler_params=params(),
    )(own_values, key_scale.reshape(1, TILE))

    windows = pl.pallas_call(
        window_kernel,
        out_shape=jax.ShapeDtypeStruct((2, block_list.shape[0]), jnp.int32),
        in_specs=[VMEM, VMEM],
        out_specs=VMEM,
        compiler_params=params(),
    )(block_list.T, block_count.reshape(1, -1))
    masks = [2 * at + 1 for at in range(1, qry_count // 2)]
    early, relayed, partner_values, visitors = gather_library(library_keys, values, queries, windows, masks)
    piece_rows = (width // value_width + 1) * TILE + EXTRA
    cost = pl.CostEstimate(flops=2 * TILE * 4 * TILE * width * 2, bytes_accessed=4 * 1024 * 1024, transcendentals=0)
    total_shape = jax.ShapeDtypeStruct((TILE, value_width), jnp.float32)
    line_shape = jax.ShapeDtypeStruct((TILE, LANES), jnp.float32)
    pieces_total = 2 * (1 + len(early) + len(relayed))
    attend_params = params(pieces_total * piece_rows * value_width * 2)
    own_specs = [pl.BlockSpec(memory_space=pl.ANY), VMEM]
    own_scratch = [pltpu.VMEM(library_keys.shape, library_keys.dtype), pltpu.SemaphoreType.DMA]
    early_arrays = arrays_of(early)
    states = []
    for mask, visiting in visitors:
        state = pl.pallas_call(
            functools.partial(early_kernel, places_of(early), mask),
            out_shape=(jax.ShapeDtypeStruct(queries.shape[::-1], queries.dtype), total_shape, line_shape, line_shape),
            in_specs=[VMEM] * (2 + len(early_arrays)) + own_specs,
            out_specs=(VMEM,) * 4,
            scratch_shapes=[pltpu.VMEM((len(early) + 1, TILE, TILE), jnp.float32)] + own_scratch,
            compiler_params=attend_params,
            cost_estimate=cost,
        )(windows, visiting, *early_arrays, library_keys, values)
        states.append(state)

    bundled = [(lib_mask | 1, qry_mask) for lib_mask, qry_mask in places_of(early)]
    early_values = [piece[2] for piece in early]
    bundle = pl.pallas_call(
        bundle_kernel,
        out_shape=jax.ShapeDtypeStruct((len(early) * (TILE + EXTRA), value_width), jnp.bfloat16),
        in_specs=[VMEM] * len(early),
        out_specs=VMEM,
        compiler_params=params(),
    )(*early_values)
    bundled_arrays = [swap(piece[1], "lib", 1) for piece in early] + [swap(bundle, "lib", 1)]
    late = [((1, 0), partner_keys, partner_values)] + relayed
    late += cross_cores(relayed)
    late_arrays = arrays_of(late) + bundled_arrays
    returned = []
    for (mask, _), state in zip(visitors, states):
        packed = pl.pallas_call(
            functools.partial(late_kernel, places_of(late), bundled, mask),
            out_shape=jax.ShapeDtypeStruct((TILE + EXTRA, value_width), jnp.bfloat16),
            in_specs=[VMEM] * (5 + len(late_arrays)),
            out_specs=VMEM,
            scratch_shapes=[
                pltpu.VMEM((len(late) + len(bundled), TILE, TILE), jnp.float32),
                pltpu.VMEM((TILE, value_width), jnp.float32),
                pltpu.VMEM((TILE, TILE), jnp.float32),
            ],
            compiler_params=attend_params,
            cost_estimate=cost,
        )(windows, *state, *late_arrays)
        returned.append(swap(packed, "qry", mask))

    total, stats = pl.pallas_call(
        functools.partial(home_kernel, places_of(early + late), bundled),
        out_shape=(total_shape, jax.ShapeDtypeStruct((2, TILE, LANES), jnp.float32)),
        in_specs=[VMEM] * (2 + len(early_arrays) + len(late_arrays)) + own_specs,
        out_specs=(VMEM, VMEM),
        scratch_shapes=[
            pltpu.VMEM((pieces_total, TILE, TILE), jnp.float32),
            pltpu.VMEM((TILE, TILE), jnp.float32),
        ]
        + own_scratch,
        compiler_params=attend_params,
        cost_estimate=cost,
    )(windows, queries, *early_arrays, *late_arrays, library_keys, values)

    return pl.pallas_call(
        merge_kernel,
        out_shape=jax.ShapeDtypeStruct((TILE, value_width), jnp.bfloat16),
        in_specs=[VMEM] * (2 + len(returned)),
        out_specs=VMEM,
        compiler_params=params(),
    )(total, stats, *returned)


def solution(mesh):
    in_specs = (
        P(("groups", "lib", "qry"), None),
        P(("groups", "lib", "qry"), None),
        P(("groups", "lib", "qry"), None),
        P(("groups", "lib", "qry")),
        P("groups", None),
        P("groups"),
    )
    out_specs = P(("groups", "lib", "qry"), None)
    return jax.shard_map(body, mesh=mesh, in_specs=in_specs, out_specs=out_specs, check_vma=False)
```

```python
import functools
import math

import jax
import jax.numpy as jnp
from jax import lax
from jax.experimental import pallas as pl
from jax.experimental.pallas import tpu as pltpu
from jax.sharding import PartitionSpec as P

TILE = 128
LANES = 128
EXTRA = 16
MASKED_SCORE = -1e30
VMEM = pl.BlockSpec(memory_space=pltpu.VMEM)


def params(operand_bytes=0):
    return pltpu.CompilerParams(vmem_limit_bytes=operand_bytes * 3 // 2 + 6 * 1024 * 1024)


def swap(value, axis, mask):
    length = lax.axis_size(axis)
    return lax.ppermute(value, axis, [(i, i ^ mask) for i in range(length)])


def tie(*values):
    return lax.optimization_barrier(values)


def split_three(value):
    high = value.astype(jnp.bfloat16)
    rest = value - high.astype(jnp.float32)
    middle = rest.astype(jnp.bfloat16)
    low = (rest - middle.astype(jnp.float32)).astype(jnp.bfloat16)
    return high, middle, low


def pack_kernel(values_ref, scale_ref, packed_ref, row_ref, sems):
    value_width = values_ref.shape[1]
    copies = (
        pltpu.make_async_copy(values_ref, packed_ref.at[pl.ds(0, TILE)], sems.at[0]),
        pltpu.make_async_copy(scale_ref, row_ref, sems.at[1]),
    )
    for copy in copies:
        copy.start()
    packed_ref[TILE:, TILE:] = jnp.zeros((EXTRA, value_width - TILE), jnp.bfloat16)
    for copy in reversed(copies):
        copy.wait()
    row = row_ref[...].astype(jnp.float32)
    packed_ref[TILE:, 0:TILE] = jnp.broadcast_to(row, (EXTRA, TILE)).astype(jnp.bfloat16)


class Piece:
    def __init__(self, place, keys_ref, values_ref, row=0, copy=None):
        self.place = place
        self.keys_ref = keys_ref
        self.values_ref = values_ref
        self.row = row
        self.copy = copy

    def scores(self, query_ref, inverse_root):
        product = lax.dot_general(
            query_ref[...], self.keys_ref[...], (((1,), (1,)), ((), ())), preferred_element_type=jnp.float32
        )
        scale = self.values_ref[self.row + TILE : self.row + TILE + EXTRA, 0:TILE]
        return product * (scale.astype(jnp.float32)[0:1] * inverse_root)

    def turned_scores(self, turned_ref, inverse_root):
        product = jnp.transpose(jnp.dot(self.keys_ref[...], turned_ref[...], preferred_element_type=jnp.float32))
        scale = self.values_ref[self.row + TILE : self.row + TILE + EXTRA, 0:TILE]
        return product * (scale.astype(jnp.float32)[0:1] * inverse_root)

    def values(self):
        return self.values_ref[self.row : self.row + TILE, :]


def read_pieces(places, refs, bundled=(), own=None):
    pieces = [Piece(place, refs[2 * at], refs[2 * at + 1]) for at, place in enumerate(places)]
    refs = refs[2 * len(places) :]
    if bundled:
        values_ref = refs[len(bundled)]
        pieces += [
            Piece(place, refs[at], values_ref, at * (TILE + EXTRA)) for at, place in enumerate(bundled)
        ]
        refs = refs[len(bundled) + 1 :]
    if own is not None:
        keys_ref, values_ref, *refs, held_ref, sem = refs
        copy = pltpu.make_async_copy(keys_ref, held_ref, sem)
        copy.start()
        pieces.append(Piece((0, 0), held_ref, values_ref, copy=copy))
    return pieces, refs


def bundle_kernel(*refs):
    *refs, bundle_ref = refs
    row = 0
    for ref in refs:
        bundle_ref[row : row + ref.shape[0], :] = ref[...]
        row += ref.shape[0]


def window_kernel(lists_ref, counts_ref, windows_ref):
    windows_ref[0:1, :] = lists_ref[0:1, :]
    windows_ref[1:2, :] = counts_ref[...]


def pick(ref, row, column):
    rows = lax.broadcasted_iota(jnp.int32, ref.shape, 0)
    columns = lax.broadcasted_iota(jnp.int32, ref.shape, 1)
    chosen = jnp.where((rows == row) & (columns == column), ref[...], 0)
    return jnp.sum(chosen.astype(jnp.float32)).astype(jnp.int32)


def attend(pieces, panel_mask, windows_ref, query_ref, score_ref, total_ref, mass_ref, before=None):
    lib_index = lax.axis_index("lib")
    qry_index = lax.axis_index("qry")
    qry_count = lax.axis_size("qry")
    block_total = lax.axis_size("lib") * qry_count
    panel = lib_index * qry_count + lax.bitwise_xor(qry_index, panel_mask)
    first = pick(windows_ref, 0, panel)
    count = pick(windows_ref, 1, panel)
    inverse_root = 1.0 / math.sqrt(pieces[0].keys_ref.shape[1])

    def active(lib_mask, qry_mask):
        block = lax.bitwise_xor(lib_index, lib_mask) * qry_count + lax.bitwise_xor(qry_index, qry_mask)
        return lax.rem(block - first + block_total, block_total) < count

    flags = [active(*piece.place) for piece in pieces]
    score_ref[...] = jnp.full(score_ref.shape, MASKED_SCORE, jnp.float32)
    for at, (piece, flag) in enumerate(zip(pieces, flags)):
        if piece.copy is not None:
            piece.copy.wait()

        @pl.when(flag)
        def _(at=at, piece=piece):
            scores = piece.scores if before is None else piece.turned_scores
            score_ref[at] = scores(query_ref, inverse_root)

    largest = score_ref[0]
    for at in range(1, len(flags)):
        largest = jnp.maximum(largest, score_ref[at])
    row_max = jnp.max(largest, axis=1, keepdims=True)
    if before is None:
        total_ref[...] = jnp.zeros(total_ref.shape, jnp.float32)
        mass_ref[...] = jnp.zeros(mass_ref.shape, jnp.float32)
    else:
        old_total_ref, old_mass_ref, old_max_ref = before
        old_max = old_max_ref[...]
        new_max = jnp.maximum(old_max, row_max)
        shrink = jnp.exp(old_max - new_max)
        row_max = new_max[:, 0:1]
        mass_ref[...] = old_mass_ref[...] * shrink
        for at in range(0, total_ref.shape[1], LANES):
            total_ref[:, at : at + LANES] = old_total_ref[:, at : at + LANES] * shrink
    for at, (piece, flag) in enumerate(zip(pieces, flags)):

        @pl.when(flag)
        def _(at=at, piece=piece):
            weights = jnp.exp(score_ref[at] - row_max)
            mass_ref[...] += weights
            weight_high = weights.astype(jnp.bfloat16)
            weight_low = (weights - weight_high.astype(jnp.float32)).astype(jnp.bfloat16)
            values = piece.values()
            added = jnp.dot(weight_high, values, preferred_element_type=jnp.float32)
            added = added + jnp.dot(weight_low, values, preferred_element_type=jnp.float32)
            total_ref[...] += added

    return row_max


def early_kernel(places, panel_mask, windows_ref, query_ref, *refs):
    pieces, refs = read_pieces(places, refs, own=True)
    turned_ref, total_ref, mass_ref, max_ref, score_ref = refs
    row_max = attend(pieces, panel_mask, windows_ref, query_ref, score_ref, total_ref, mass_ref)
    max_ref[...] = jnp.broadcast_to(row_max, max_ref.shape)
    turned_ref[...] = jnp.transpose(query_ref[...])


def late_kernel(places, bundled, panel_mask, windows_ref, turned_ref, *refs):
    before, refs = refs[:3], refs[3:]
    pieces, refs = read_pieces(places, refs, bundled)
    packed_ref, score_ref, total_ref, mass_ref = refs
    row_max = attend(pieces, panel_mask, windows_ref, turned_ref, score_ref, total_ref, mass_ref, before)
    row_sum = jnp.sum(mass_ref[...], axis=1, keepdims=True)
    value_width = total_ref.shape[1]
    inverse = 1.0 / jnp.where(row_sum > 0.0, row_sum, 1.0)
    packed_ref[0:TILE, :] = (total_ref[...] * inverse).astype(jnp.bfloat16)
    row = lax.broadcasted_iota(jnp.int32, (EXTRA, LANES), 0)
    packed = jnp.zeros((EXTRA, LANES), jnp.float32)
    for first, column in ((0, row_max), (3, row_sum)):
        turned = jnp.transpose(jnp.broadcast_to(column, (TILE, LANES)))[0:EXTRA]
        for at, part in enumerate(split_three(turned)):
            packed = jnp.where(row == first + at, part.astype(jnp.float32), packed)
    packed_ref[TILE:, 0:LANES] = packed.astype(jnp.bfloat16)
    packed_ref[TILE:, LANES:] = jnp.zeros((EXTRA, value_width - LANES), jnp.bfloat16)


def home_kernel(places, bundled, windows_ref, query_ref, *refs):
    pieces, refs = read_pieces(places, refs, bundled, own=True)
    total_ref, stats_ref, score_ref, mass_ref = refs
    row_max = attend(pieces, 0, windows_ref, query_ref, score_ref, total_ref, mass_ref)
    row_sum = jnp.sum(mass_ref[...], axis=1, keepdims=True)
    stats_ref[0] = jnp.broadcast_to(row_max, (TILE, LANES))
    stats_ref[1] = jnp.broadcast_to(row_sum, (TILE, LANES))


def merge_kernel(total_ref, stats_ref, *refs):
    packed_refs, out_ref = refs[:-1], refs[-1]
    maxima = [stats_ref[0]]
    sums = [stats_ref[1]]
    for packed_ref in packed_refs:
        packed = packed_ref[TILE:, 0:LANES].astype(jnp.float32)
        for first, kept in ((0, maxima), (3, sums)):
            line = packed[first : first + 1] + packed[first + 1 : first + 2] + packed[first + 2 : first + 3]
            kept.append(jnp.transpose(jnp.broadcast_to(line, (TILE, LANES))))
    top = functools.reduce(jnp.maximum, maxima)
    factors = [jnp.exp(row_max - top) for row_max in maxima]
    masses = [factor * row_sum for factor, row_sum in zip(factors, sums)]
    inverse = 1.0 / functools.reduce(jnp.add, masses)
    scales = [factors[0] * inverse] + [mass * inverse for mass in masses[1:]]
    for at in range(0, total_ref.shape[1], LANES):
        merged = total_ref[:, at : at + LANES] * scales[0]
        for packed_ref, scale in zip(packed_refs, scales[1:]):
            merged = merged + packed_ref[0:TILE, at : at + LANES].astype(jnp.float32) * scale
        out_ref[:, at : at + LANES] = merged.astype(jnp.bfloat16)


def gather_library(keys, values, queries, windows, masks):
    steps = [("qry", 1)]
    mask = lax.axis_size("lib") // 2
    while mask > 1:
        steps.append(("lib", mask))
        mask //= 2
    partner_values = swap(values, "lib", 1)
    early, late = [], []
    for axis, mask in steps:
        place = (0, mask) if axis == "qry" else (mask, 0)
        near = (place, swap(keys, axis, mask), swap(values, axis, mask))
        relayed = []
        for (lib_mask, qry_mask), far_keys, far_values in early + late:
            far_keys, *_ = tie(far_keys, near[1], values)
            far_values, _ = tie(far_values, near[2])
            place = (lib_mask | mask, qry_mask)
            relayed.append((place, swap(far_keys, axis, mask), swap(far_values, axis, mask)))
        early, late = early + late + [near], relayed
    leaving, *_ = tie(queries, partner_values, windows, early[-1][1])
    visitors = [swap(leaving, "qry", mask) for mask in masks]
    return early, late, partner_values, list(zip(masks, visitors))


def cross_cores(pieces, arrivals=()):
    crossed = []
    for (lib_mask, qry_mask), *pair in pieces:
        pair = tie(*pair, *arrivals)[:2]
        crossed.append(((lib_mask | 1, qry_mask), *(swap(array, "lib", 1) for array in pair)))
    return crossed


def places_of(pieces):
    return [piece[0] for piece in pieces]


def arrays_of(pieces):
    return [array for piece in pieces for array in piece[1:]]


def body(queries, library_keys, library_values, key_scale, block_list, block_count):
    qry_count = lax.axis_size("qry")
    width = library_keys.shape[1]
    value_width = library_values.shape[1]

    partner_keys = swap(library_keys, "lib", 1)
    own_values, _ = tie(library_values, partner_keys)
    values = pl.pallas_call(
        pack_kernel,
        out_shape=jax.ShapeDtypeStruct((TILE + EXTRA, value_width), jnp.bfloat16),
        in_specs=[pl.BlockSpec(memory_space=pl.ANY)] * 2,
        out_specs=VMEM,
        scratch_shapes=[pltpu.VMEM((1, TILE), jnp.bfloat16), pltpu.SemaphoreType.DMA((2,))],
        compiler_params=params(),
    )(own_values, key_scale.reshape(1, TILE))

    windows = pl.pallas_call(
        window_kernel,
        out_shape=jax.ShapeDtypeStruct((2, block_list.shape[0]), jnp.int32),
        in_specs=[VMEM, VMEM],
        out_specs=VMEM,
        compiler_params=params(),
    )(block_list.T, block_count.reshape(1, -1))
    masks = [2 * at + 1 for at in range(1, qry_count // 2)]
    early, relayed, partner_values, visitors = gather_library(library_keys, values, queries, windows, masks)
    piece_rows = (width // value_width + 1) * TILE + EXTRA
    cost = pl.CostEstimate(flops=2 * TILE * 4 * TILE * width * 2, bytes_accessed=4 * 1024 * 1024, transcendentals=0)
    total_shape = jax.ShapeDtypeStruct((TILE, value_width), jnp.float32)
    line_shape = jax.ShapeDtypeStruct((TILE, LANES), jnp.float32)
    pieces_total = 2 * (1 + len(early) + len(relayed))
    attend_params = params(pieces_total * piece_rows * value_width * 2)
    own_specs = [pl.BlockSpec(memory_space=pl.ANY), VMEM]
    own_scratch = [pltpu.VMEM(library_keys.shape, library_keys.dtype), pltpu.SemaphoreType.DMA]
    early_arrays = arrays_of(early)
    states = []
    for mask, visiting in visitors:
        state = pl.pallas_call(
            functools.partial(early_kernel, places_of(early), mask),
            out_shape=(jax.ShapeDtypeStruct(queries.shape[::-1], queries.dtype), total_shape, line_shape, line_shape),
            in_specs=[VMEM] * (2 + len(early_arrays)) + own_specs,
            out_specs=(VMEM,) * 4,
            scratch_shapes=[pltpu.VMEM((len(early) + 1, TILE, TILE), jnp.float32)] + own_scratch,
            compiler_params=attend_params,
            cost_estimate=cost,
        )(windows, visiting, *early_arrays, library_keys, values)
        states.append(state)

    bundled = [(lib_mask | 1, qry_mask) for lib_mask, qry_mask in places_of(early)]
    early_values = [piece[2] for piece in early]
    bundle = pl.pallas_call(
        bundle_kernel,
        out_shape=jax.ShapeDtypeStruct((len(early) * (TILE + EXTRA), value_width), jnp.bfloat16),
        in_specs=[VMEM] * len(early),
        out_specs=VMEM,
        compiler_params=params(),
    )(*early_values)
    bundled_arrays = [swap(piece[1], "lib", 1) for piece in early] + [swap(bundle, "lib", 1)]
    late = [((1, 0), partner_keys, partner_values)] + relayed
    late += cross_cores(relayed, [state[3] for state in states])
    late_arrays = arrays_of(late) + bundled_arrays
    returned = []
    for (mask, _), state in zip(visitors, states):
        packed = pl.pallas_call(
            functools.partial(late_kernel, places_of(late), bundled, mask),
            out_shape=jax.ShapeDtypeStruct((TILE + EXTRA, value_width), jnp.bfloat16),
            in_specs=[VMEM] * (5 + len(late_arrays)),
            out_specs=VMEM,
            scratch_shapes=[
                pltpu.VMEM((len(late) + len(bundled), TILE, TILE), jnp.float32),
                pltpu.VMEM((TILE, value_width), jnp.float32),
                pltpu.VMEM((TILE, TILE), jnp.float32),
            ],
            compiler_params=attend_params,
            cost_estimate=cost,
        )(windows, *state, *late_arrays)
        returned.append(swap(packed, "qry", mask))

    total, stats = pl.pallas_call(
        functools.partial(home_kernel, places_of(early + late), bundled),
        out_shape=(total_shape, jax.ShapeDtypeStruct((2, TILE, LANES), jnp.float32)),
        in_specs=[VMEM] * (2 + len(early_arrays) + len(late_arrays)) + own_specs,
        out_specs=(VMEM, VMEM),
        scratch_shapes=[
            pltpu.VMEM((pieces_total, TILE, TILE), jnp.float32),
            pltpu.VMEM((TILE, TILE), jnp.float32),
        ]
        + own_scratch,
        compiler_params=attend_params,
        cost_estimate=cost,
    )(windows, queries, *early_arrays, *late_arrays, library_keys, values)

    return pl.pallas_call(
        merge_kernel,
        out_shape=jax.ShapeDtypeStruct((TILE, value_width), jnp.bfloat16),
        in_specs=[VMEM] * (2 + len(returned)),
        out_specs=VMEM,
        compiler_params=params(),
    )(total, stats, *returned)


def solution(mesh):
    in_specs = (
        P(("groups", "lib", "qry"), None),
        P(("groups", "lib", "qry"), None),
        P(("groups", "lib", "qry"), None),
        P(("groups", "lib", "qry")),
        P("groups", None),
        P("groups"),
    )
    out_specs = P(("groups", "lib", "qry"), None)
    return jax.shard_map(body, mesh=mesh, in_specs=in_specs, out_specs=out_specs, check_vma=False)
```

```python
import functools
import math

import jax
import jax.numpy as jnp
from jax import lax
from jax.experimental import pallas as pl
from jax.experimental.pallas import tpu as pltpu
from jax.sharding import PartitionSpec as P

TILE = 128
LANES = 128
EXTRA = 16
LINES = 8
MASKED_SCORE = -1e30
VMEM = pl.BlockSpec(memory_space=pltpu.VMEM)


def params(operand_bytes=0):
    return pltpu.CompilerParams(vmem_limit_bytes=operand_bytes * 3 // 2 + 6 * 1024 * 1024)


def swap(value, axis, mask):
    length = lax.axis_size(axis)
    return lax.ppermute(value, axis, [(i, i ^ mask) for i in range(length)])


def tie(*values):
    return lax.optimization_barrier(values)


def split_three(value):
    high = value.astype(jnp.bfloat16)
    rest = value - high.astype(jnp.float32)
    middle = rest.astype(jnp.bfloat16)
    low = (rest - middle.astype(jnp.float32)).astype(jnp.bfloat16)
    return high, middle, low


def pack_kernel(values_ref, scale_ref, packed_ref, row_ref, sems):
    value_width = values_ref.shape[1]
    copies = (
        pltpu.make_async_copy(values_ref, packed_ref.at[pl.ds(0, TILE)], sems.at[0]),
        pltpu.make_async_copy(scale_ref, row_ref, sems.at[1]),
    )
    for copy in copies:
        copy.start()
    packed_ref[TILE:, TILE:] = jnp.zeros((EXTRA, value_width - TILE), jnp.bfloat16)
    for copy in reversed(copies):
        copy.wait()
    row = row_ref[...].astype(jnp.float32)
    packed_ref[TILE:, 0:TILE] = jnp.broadcast_to(row, (EXTRA, TILE)).astype(jnp.bfloat16)


class Piece:
    def __init__(self, place, keys_ref, values_ref, row=0, copy=None):
        self.place = place
        self.keys_ref = keys_ref
        self.values_ref = values_ref
        self.row = row
        self.copy = copy

    def scores(self, query_ref, inverse_root):
        product = lax.dot_general(
            query_ref[...], self.keys_ref[...], (((1,), (1,)), ((), ())), preferred_element_type=jnp.float32
        )
        scale = self.values_ref[self.row + TILE : self.row + TILE + EXTRA, 0:TILE]
        return product * (scale.astype(jnp.float32)[0:1] * inverse_root)

    def turned_scores(self, turned_ref, inverse_root):
        product = jnp.transpose(jnp.dot(self.keys_ref[...], turned_ref[...], preferred_element_type=jnp.float32))
        scale = self.values_ref[self.row + TILE : self.row + TILE + EXTRA, 0:TILE]
        return product * (scale.astype(jnp.float32)[0:1] * inverse_root)

    def values(self):
        return self.values_ref[self.row : self.row + TILE, :]


def read_pieces(places, refs, bundled=(), own=None):
    pieces = [Piece(place, refs[2 * at], refs[2 * at + 1]) for at, place in enumerate(places)]
    refs = refs[2 * len(places) :]
    if bundled:
        values_ref = refs[len(bundled)]
        pieces += [
            Piece(place, refs[at], values_ref, at * (TILE + EXTRA)) for at, place in enumerate(bundled)
        ]
        refs = refs[len(bundled) + 1 :]
    if own is not None:
        keys_ref, values_ref, *refs, held_ref, sem = refs
        copy = pltpu.make_async_copy(keys_ref, held_ref, sem)
        copy.start()
        pieces.append(Piece((0, 0), held_ref, values_ref, copy=copy))
    return pieces, refs


def bundle_kernel(*refs):
    *refs, bundle_ref = refs
    row = 0
    for ref in refs:
        bundle_ref[row : row + ref.shape[0], :] = ref[...]
        row += ref.shape[0]


def window_kernel(lists_ref, counts_ref, windows_ref):
    windows_ref[0:1, :] = lists_ref[0:1, :]
    windows_ref[1:2, :] = counts_ref[...]


def pick(ref, row, column):
    rows = lax.broadcasted_iota(jnp.int32, ref.shape, 0)
    columns = lax.broadcasted_iota(jnp.int32, ref.shape, 1)
    chosen = jnp.where((rows == row) & (columns == column), ref[...], 0)
    return jnp.sum(chosen.astype(jnp.float32)).astype(jnp.int32)


def attend(pieces, panel_mask, windows_ref, query_ref, score_ref, total_ref, mass_ref, before=None):
    lib_index = lax.axis_index("lib")
    qry_index = lax.axis_index("qry")
    qry_count = lax.axis_size("qry")
    block_total = lax.axis_size("lib") * qry_count
    panel = lib_index * qry_count + lax.bitwise_xor(qry_index, panel_mask)
    first = pick(windows_ref, 0, panel)
    count = pick(windows_ref, 1, panel)
    inverse_root = 1.0 / math.sqrt(pieces[0].keys_ref.shape[1])

    def active(lib_mask, qry_mask):
        block = lax.bitwise_xor(lib_index, lib_mask) * qry_count + lax.bitwise_xor(qry_index, qry_mask)
        return lax.rem(block - first + block_total, block_total) < count

    flags = [active(*piece.place) for piece in pieces]
    score_ref[...] = jnp.full(score_ref.shape, MASKED_SCORE, jnp.float32)
    for at, (piece, flag) in enumerate(zip(pieces, flags)):
        if piece.copy is not None:
            piece.copy.wait()

        @pl.when(flag)
        def _(at=at, piece=piece):
            scores = piece.scores if before is None else piece.turned_scores
            score_ref[at] = scores(query_ref, inverse_root)

    largest = score_ref[0]
    for at in range(1, len(flags)):
        largest = jnp.maximum(largest, score_ref[at])
    row_max = jnp.max(largest, axis=1, keepdims=True)
    if before is None:
        total_ref[...] = jnp.zeros(total_ref.shape, jnp.float32)
        mass_ref[...] = jnp.zeros(mass_ref.shape, jnp.float32)
    else:
        old_total_ref, old_mass_ref, old_max_ref = before
        old_max = old_max_ref[...]
        new_max = jnp.maximum(old_max, row_max)
        shrink = jnp.exp(old_max - new_max)
        row_max = new_max[:, 0:1]
        mass_ref[...] = old_mass_ref[...] * shrink
        for at in range(0, total_ref.shape[1], LANES):
            total_ref[:, at : at + LANES] = old_total_ref[:, at : at + LANES] * shrink
    for at, (piece, flag) in enumerate(zip(pieces, flags)):

        @pl.when(flag)
        def _(at=at, piece=piece):
            weights = jnp.exp(score_ref[at] - row_max)
            mass_ref[...] += weights
            weight_high = weights.astype(jnp.bfloat16)
            weight_low = (weights - weight_high.astype(jnp.float32)).astype(jnp.bfloat16)
            values = piece.values()
            added = jnp.dot(weight_high, values, preferred_element_type=jnp.float32)
            added = added + jnp.dot(weight_low, values, preferred_element_type=jnp.float32)
            total_ref[...] += added

    return row_max


def early_kernel(places, panel_mask, windows_ref, query_ref, *refs):
    pieces, refs = read_pieces(places, refs, own=True)
    turned_ref, total_ref, mass_ref, max_ref, score_ref = refs
    row_max = attend(pieces, panel_mask, windows_ref, query_ref, score_ref, total_ref, mass_ref)
    max_ref[...] = jnp.broadcast_to(row_max, max_ref.shape)
    turned_ref[...] = jnp.transpose(query_ref[...])


def late_kernel(places, bundled, panel_mask, windows_ref, turned_ref, *refs):
    before, refs = refs[:3], refs[3:]
    pieces, refs = read_pieces(places, refs, bundled)
    packed_ref, score_ref, total_ref, mass_ref = refs
    row_max = attend(pieces, panel_mask, windows_ref, turned_ref, score_ref, total_ref, mass_ref, before)
    row_sum = jnp.sum(mass_ref[...], axis=1, keepdims=True)
    value_width = total_ref.shape[1]
    inverse = 1.0 / jnp.where(row_sum > 0.0, row_sum, 1.0)
    packed_ref[0:TILE, :] = (total_ref[...] * inverse).astype(jnp.bfloat16)
    row = lax.broadcasted_iota(jnp.int32, (LINES, LANES), 0)
    packed = jnp.zeros((LINES, LANES), jnp.float32)
    for first, column in ((0, row_max), (3, row_sum)):
        turned = jnp.transpose(jnp.broadcast_to(column, (TILE, LANES)))[0:LINES]
        for at, part in enumerate(split_three(turned)):
            packed = jnp.where(row == first + at, part.astype(jnp.float32), packed)
    packed_ref[TILE:, 0:LANES] = packed.astype(jnp.bfloat16)
    packed_ref[TILE:, LANES:] = jnp.zeros((LINES, value_width - LANES), jnp.bfloat16)


def home_kernel(places, bundled, windows_ref, query_ref, *refs):
    pieces, refs = read_pieces(places, refs, bundled, own=True)
    total_ref, stats_ref, score_ref, mass_ref = refs
    row_max = attend(pieces, 0, windows_ref, query_ref, score_ref, total_ref, mass_ref)
    row_sum = jnp.sum(mass_ref[...], axis=1, keepdims=True)
    stats_ref[0] = jnp.broadcast_to(row_max, (TILE, LANES))
    stats_ref[1] = jnp.broadcast_to(row_sum, (TILE, LANES))


def merge_kernel(total_ref, stats_ref, *refs):
    packed_refs, out_ref = refs[:-1], refs[-1]
    maxima = [stats_ref[0]]
    sums = [stats_ref[1]]
    for packed_ref in packed_refs:
        packed = packed_ref[TILE:, 0:LANES].astype(jnp.float32)
        for first, kept in ((0, maxima), (3, sums)):
            line = packed[first : first + 1] + packed[first + 1 : first + 2] + packed[first + 2 : first + 3]
            kept.append(jnp.transpose(jnp.broadcast_to(line, (TILE, LANES))))
    top = functools.reduce(jnp.maximum, maxima)
    factors = [jnp.exp(row_max - top) for row_max in maxima]
    masses = [factor * row_sum for factor, row_sum in zip(factors, sums)]
    inverse = 1.0 / functools.reduce(jnp.add, masses)
    scales = [factors[0] * inverse] + [mass * inverse for mass in masses[1:]]
    for at in range(0, total_ref.shape[1], LANES):
        merged = total_ref[:, at : at + LANES] * scales[0]
        for packed_ref, scale in zip(packed_refs, scales[1:]):
            merged = merged + packed_ref[0:TILE, at : at + LANES].astype(jnp.float32) * scale
        out_ref[:, at : at + LANES] = merged.astype(jnp.bfloat16)


def gather_library(keys, values, queries, windows, masks):
    steps = [("qry", 1)]
    mask = lax.axis_size("lib") // 2
    while mask > 1:
        steps.append(("lib", mask))
        mask //= 2
    partner_values = swap(values, "lib", 1)
    leaving, *_ = tie(queries, partner_values, windows)
    visitors = [swap(leaving, "qry", mask) for mask in masks]
    early, late = [], []
    for axis, mask in steps:
        place = (0, mask) if axis == "qry" else (mask, 0)
        near = (place, swap(keys, axis, mask), swap(values, axis, mask))
        relayed = []
        for (lib_mask, qry_mask), far_keys, far_values in early + late:
            far_keys, *_ = tie(far_keys, near[1], values)
            far_values, _ = tie(far_values, near[2])
            place = (lib_mask | mask, qry_mask)
            relayed.append((place, swap(far_keys, axis, mask), swap(far_values, axis, mask)))
        early, late = early + late + [near], relayed
    return early, late, partner_values, list(zip(masks, visitors))


def cross_cores(pieces, arrivals=()):
    crossed = []
    for (lib_mask, qry_mask), *pair in pieces:
        pair = tie(*pair, *arrivals)[:2]
        crossed.append(((lib_mask | 1, qry_mask), *(swap(array, "lib", 1) for array in pair)))
    return crossed


def places_of(pieces):
    return [piece[0] for piece in pieces]


def arrays_of(pieces):
    return [array for piece in pieces for array in piece[1:]]


def body(queries, library_keys, library_values, key_scale, block_list, block_count):
    qry_count = lax.axis_size("qry")
    width = library_keys.shape[1]
    value_width = library_values.shape[1]

    partner_keys = swap(library_keys, "lib", 1)
    own_values, _ = tie(library_values, partner_keys)
    values = pl.pallas_call(
        pack_kernel,
        out_shape=jax.ShapeDtypeStruct((TILE + EXTRA, value_width), jnp.bfloat16),
        in_specs=[pl.BlockSpec(memory_space=pl.ANY)] * 2,
        out_specs=VMEM,
        scratch_shapes=[pltpu.VMEM((1, TILE), jnp.bfloat16), pltpu.SemaphoreType.DMA((2,))],
        compiler_params=params(),
    )(own_values, key_scale.reshape(1, TILE))

    windows = pl.pallas_call(
        window_kernel,
        out_shape=jax.ShapeDtypeStruct((2, block_list.shape[0]), jnp.int32),
        in_specs=[VMEM, VMEM],
        out_specs=VMEM,
        compiler_params=params(),
    )(block_list.T, block_count.reshape(1, -1))
    masks = [2 * at + 1 for at in range(1, qry_count // 2)]
    early, relayed, partner_values, visitors = gather_library(library_keys, values, queries, windows, masks)
    piece_rows = (width // value_width + 1) * TILE + EXTRA
    cost = pl.CostEstimate(flops=2 * TILE * 4 * TILE * width * 2, bytes_accessed=4 * 1024 * 1024, transcendentals=0)
    total_shape = jax.ShapeDtypeStruct((TILE, value_width), jnp.float32)
    line_shape = jax.ShapeDtypeStruct((TILE, LANES), jnp.float32)
    pieces_total = 2 * (1 + len(early) + len(relayed))
    attend_params = params(pieces_total * piece_rows * value_width * 2)
    own_specs = [pl.BlockSpec(memory_space=pl.ANY), VMEM]
    own_scratch = [pltpu.VMEM(library_keys.shape, library_keys.dtype), pltpu.SemaphoreType.DMA]
    early_arrays = arrays_of(early)
    states = []
    for mask, visiting in visitors:
        state = pl.pallas_call(
            functools.partial(early_kernel, places_of(early), mask),
            out_shape=(jax.ShapeDtypeStruct(queries.shape[::-1], queries.dtype), total_shape, line_shape, line_shape),
            in_specs=[VMEM] * (2 + len(early_arrays)) + own_specs,
            out_specs=(VMEM,) * 4,
            scratch_shapes=[pltpu.VMEM((len(early) + 1, TILE, TILE), jnp.float32)] + own_scratch,
            compiler_params=attend_params,
            cost_estimate=cost,
        )(windows, visiting, *early_arrays, library_keys, values)
        states.append(state)

    bundled = [(lib_mask | 1, qry_mask) for lib_mask, qry_mask in places_of(early)]
    early_values = [piece[2] for piece in early]
    bundle = pl.pallas_call(
        bundle_kernel,
        out_shape=jax.ShapeDtypeStruct((len(early) * (TILE + EXTRA), value_width), jnp.bfloat16),
        in_specs=[VMEM] * len(early),
        out_specs=VMEM,
        compiler_params=params(),
    )(*early_values)
    bundled_arrays = [swap(piece[1], "lib", 1) for piece in early] + [swap(bundle, "lib", 1)]
    late = [((1, 0), partner_keys, partner_values)] + relayed
    late += cross_cores(relayed, [state[3] for state in states])
    late_arrays = arrays_of(late) + bundled_arrays
    returned = []
    for (mask, _), state in zip(visitors, states):
        packed = pl.pallas_call(
            functools.partial(late_kernel, places_of(late), bundled, mask),
            out_shape=jax.ShapeDtypeStruct((TILE + LINES, value_width), jnp.bfloat16),
            in_specs=[VMEM] * (5 + len(late_arrays)),
            out_specs=VMEM,
            scratch_shapes=[
                pltpu.VMEM((len(late) + len(bundled), TILE, TILE), jnp.float32),
                pltpu.VMEM((TILE, value_width), jnp.float32),
                pltpu.VMEM((TILE, TILE), jnp.float32),
            ],
            compiler_params=attend_params,
            cost_estimate=cost,
        )(windows, *state, *late_arrays)
        returned.append(swap(packed, "qry", mask))

    total, stats = pl.pallas_call(
        functools.partial(home_kernel, places_of(early + late), bundled),
        out_shape=(total_shape, jax.ShapeDtypeStruct((2, TILE, LANES), jnp.float32)),
        in_specs=[VMEM] * (2 + len(early_arrays) + len(late_arrays)) + own_specs,
        out_specs=(VMEM, VMEM),
        scratch_shapes=[
            pltpu.VMEM((pieces_total, TILE, TILE), jnp.float32),
            pltpu.VMEM((TILE, TILE), jnp.float32),
        ]
        + own_scratch,
        compiler_params=attend_params,
        cost_estimate=cost,
    )(windows, queries, *early_arrays, *late_arrays, library_keys, values)

    return pl.pallas_call(
        merge_kernel,
        out_shape=jax.ShapeDtypeStruct((TILE, value_width), jnp.bfloat16),
        in_specs=[VMEM] * (2 + len(returned)),
        out_specs=VMEM,
        compiler_params=params(),
    )(total, stats, *returned)


def solution(mesh):
    in_specs = (
        P(("groups", "lib", "qry"), None),
        P(("groups", "lib", "qry"), None),
        P(("groups", "lib", "qry"), None),
        P(("groups", "lib", "qry")),
        P("groups", None),
        P("groups"),
    )
    out_specs = P(("groups", "lib", "qry"), None)
    return jax.shard_map(body, mesh=mesh, in_specs=in_specs, out_specs=out_specs, check_vma=False)
```
